128 devices in a mesh: dp: 8 (over y, z_hi), px: 8 (over x, z_lo), py: 2 (over core).
Axes of the slice: x: 4, y: 4, z: 4 (z_hi: 2, z_lo: 2; z = z_hi * 2 + z_lo), core: 2. Of those that a mesh axis runs over, the one named last changes fastest.
Arguments:
- fields: bfloat16 [8, 32, 16, 32, 256], P('dp', 'px', 'py'), may hold values from -6 to 6
- cotangent: bfloat16 [8, 32, 16, 32, 256], P('dp', 'px', 'py'), may hold values from -6 to 6
- first_weight: bfloat16 [6912, 256], replicated, may hold values from -0.078125 to 0.078125
- second_weight: bfloat16 [6912, 256], replicated, may hold values from -0.078125 to 0.078125
Outputs:
- output: bfloat16 [8, 32, 16, 32, 256], P('dp', 'px', 'py')
- field_grad: bfloat16 [8, 32, 16, 32, 256], P('dp', 'px', 'py')
- first_grad: float32 [6912, 256], P('dp', ('px', 'py'))
- second_grad: float32 [6912, 256], P('dp', ('px', 'py'))
The draws below stay inside these ranges and needn't reach their ends.
All inputs are finite; a program needn't handle non-finite values.
Results may differ from the reference program's by a relative error of at most 0.0033.
Values may be sent and summed in bfloat16 or wider, within the bound.
No kernel may reach another device: no remote copies, remote signals or barrier semaphores. Data moves between devices by JAX's collectives and lax.ppermute only.
A program may use at most 128 MiB of HBM per device.

```python
import jax
import jax.numpy as jnp
from jax import lax

C = 256
KC = 6912
ROLL = 8
NX = 32
NY = 16
NZ = 32


def shard_levels(stream_key, shape, shards, low, top_value):
    factor_of, own = 1.0, jax.random.fold_in(stream_key, 6)
    for dim, blocks in shards:
        draws = jnp.exp(jax.random.uniform(jax.random.fold_in(own, dim), (blocks,), jnp.float32, low / len(shards), top_value / len(shards)))
        factor_of = factor_of * jnp.repeat(draws, shape[dim] // blocks).reshape([-1 if axis == dim else 1 for axis in range(len(shape))])
    return factor_of


def centred(rng, dims, scale, most, split=(), dtype=jnp.bfloat16):
    loudness = shard_levels(rng, dims, split, -0.22, 0.18) if split else 1.0
    drawn = jax.random.normal(rng, dims, jnp.float32) * scale * loudness
    return jnp.minimum(jnp.maximum(drawn, -most), most).astype(dtype)


def setup_inputs(seed: int = 0) -> dict:
    key_of = jax.random.split(jax.random.key(seed), 5)
    return {
        "fields": centred(key_of[0], (ROLL, NX, NY, NZ, C), 1.0, 6.0, ((0, 8), (1, 8), (2, 2))),
        "cotangent": centred(key_of[1], (ROLL, NX, NY, NZ, C), 1.0, 6.0, ((0, 8), (1, 8), (2, 2))),
        "first_weight": centred(key_of[2], (KC, C), KC ** -0.5, 0.078125),
        "second_weight": centred(key_of[3], (KC, C), KC ** -0.5, 0.078125),
    }


def gelu_tanh(v):
    return jax.nn.gelu(v, approximate=True)

def padded_grid(field):
    return jnp.pad(field, ((1, 1), (1, 1), (1, 1), (0, 0)))

def window(padded, start_x, start_y, start_z):
    size_x, size_y, size_z, width = padded.shape
    block = padded[start_x:start_x + size_x - 2, start_y:start_y + size_y - 2, start_z:start_z + size_z - 2, :]
    return block.reshape(-1, width)

def conv_forward(padded, weight):
    width = padded.shape[-1]
    total = None
    for offset in range(27):
        first, second, third = (offset // 9, offset // 3 % 3, offset % 3)
        block = weight[offset * width:(offset + 1) * width]
        term = jnp.dot(window(padded, first, second, third), block, preferred_element_type=jnp.float32)
        total = term if total is None else total + term
    return total

def conv_transposed(padded, weight):
    width = padded.shape[-1]
    total = None
    for offset in range(27):
        first, second, third = (offset // 9, offset // 3 % 3, offset % 3)
        block = weight[offset * width:(offset + 1) * width]
        rows = window(padded, 2 - first, 2 - second, 2 - third)
        term = lax.dot_general(rows, block, (((1,), (1,)), ((), ())), preferred_element_type=jnp.float32)
        total = term if total is None else total + term
    return total

def weight_terms(padded, grads):
    blocks = []
    for offset in range(27):
        first, second, third = (offset // 9, offset // 3 % 3, offset % 3)
        rows = window(padded, first, second, third)
        blocks.append(lax.dot_general(rows, grads, (((0,), (0,)), ((), ())), preferred_element_type=jnp.float32))
    return jnp.concatenate(blocks, axis=0)

def reference(fields, cotangent, first_weight, second_weight):

    def one_rollout(carry, pair):
        first_acc, second_acc = carry
        field_one, cot_one = pair
        shape = field_one.shape
        width = shape[-1]
        fields_padded = padded_grid(field_one)
        pre = conv_forward(fields_padded, first_weight)
        hidden = gelu_tanh(pre).astype(jnp.bfloat16)
        hidden_padded = padded_grid(hidden.reshape(shape))
        second_out = conv_forward(hidden_padded, second_weight)
        output = (field_one.reshape(-1, width).astype(jnp.float32) + second_out).astype(jnp.bfloat16).reshape(shape)
        cot_flat = cot_one.reshape(-1, width)
        hidden_grad = conv_transposed(padded_grid(cot_one), second_weight)
        second_acc = second_acc + weight_terms(hidden_padded, cot_flat)
        gelu_back = jax.vjp(gelu_tanh, pre)[1]
        pre_grad = gelu_back(hidden_grad)[0].astype(jnp.bfloat16)
        field_term = conv_transposed(padded_grid(pre_grad.reshape(shape)), first_weight)
        field_grad = (cot_flat.astype(jnp.float32) + field_term).astype(jnp.bfloat16).reshape(shape)
        first_acc = first_acc + weight_terms(fields_padded, pre_grad)
        return ((first_acc, second_acc), (output, field_grad))
    zeros = jnp.zeros((KC, C), jnp.float32)
    sums, outs = lax.scan(one_rollout, (zeros, zeros), (fields, cotangent))
    output, field_grad = outs
    return (output, field_grad, sums[0] / ROLL, sums[1] / ROLL)
```

```python
import functools

import jax
import jax.numpy as jnp
from jax import lax
from jax.experimental import pallas as pl
from jax.experimental.pallas import tpu as pltpu
from jax.sharding import PartitionSpec as P

BF = jnp.bfloat16
F32 = jnp.float32
ALL = ("dp", "px", "py")
X, Y, Z = 0, 1, 2
ORDER = ((X, Y, Z), (Y, Z, X))
LANES = 896


def device(x, y, z, core):
    x, y, z = x % 4, y % 4, z % 4
    return (y * 2 + z // 2) * 16 + (x * 2 + z % 2) * 2 + core


def hop_pairs(stage, distance):
    pairs = []
    for core in range(2):
        step = [0, 0, 0]
        step[ORDER[core][stage]] = distance
        for x in range(4):
            for y in range(4):
                for z in range(4):
                    pairs.append(
                        (
                            device(x, y, z, core),
                            device(x + step[0], y + step[1], z + step[2], core),
                        )
                    )
    return pairs


def shifted(block):
    wide = block.astype(F32)
    place = lax.broadcasted_iota(jnp.int32, wide.shape, 1)
    low = jnp.where(place == 0, 0.0, pltpu.roll(wide, 1, 1)).astype(BF)
    high = jnp.where(place == 31, 0.0, pltpu.roll(wide, 31, 1)).astype(BF)
    return low, high


def put(stack, row, start, block, flip):
    low, high = shifted(block)
    if flip:
        low, high = high, low
    rows = pl.ds(start, block.shape[0])
    stack[row, rows, :, 0:256] = low
    stack[row, rows, :, 256:512] = block
    stack[row, rows, :, 512:768] = high


def put_grid(stack, own, low, high, which, first, flip):
    put(stack, 0, first, low[which], flip)
    put(stack, 5, first, high[which], flip)

    def step(i, _):
        put(stack, i + 1, first, own[i], flip)
        return 0

    lax.fori_loop(0, 4, step, 0)


def put_face(stack, core, other, place_first, place_second, flip):
    place = jnp.where(core == 0, place_first, place_second)
    row = jnp.where(core == 0, 9, 0)
    zeros = jnp.zeros((1, 32, 768), BF)

    def step(i, _):
        put(stack, i, row, other[i, pl.ds(place, 1)], flip)
        stack[i, pl.ds(9 - row, 1)] = zeros
        return 0

    lax.fori_loop(0, 6, step, 0)


def conv_into(total, stack, weight):
    for k in range(9):
        a, b = k // 3, k % 3
        rows = stack[a : a + 4, b : b + 8].reshape(1024, 768)
        term = jnp.dot(rows, weight[k * 768 : (k + 1) * 768], preferred_element_type=F32)
        if k == 0:
            total[...] = term
        else:
            total[...] += term


def conv_back_into(total, stack, weight):
    for k in range(9):
        a, b = k // 3, k % 3
        term = None
        for c in range(3):
            rows = stack[2 - a : 6 - a, 2 - b : 10 - b, :, c * 256 : (c + 1) * 256]
            block = weight[(k * 3 + c) * 256 : (k * 3 + c + 1) * 256]
            part = lax.dot_general(
                rows.reshape(1024, 256),
                block,
                (((1,), (1,)), ((), ())),
                preferred_element_type=F32,
            )
            term = part if term is None else term + part
        if k == 0:
            total[...] = term
        else:
            total[...] += term


def gelu_and_slope(v):
    scale = 0.7978845608028654
    square = v * v
    t = jnp.tanh(scale * (v + 0.044715 * (square * v)))
    half = 0.5 * (1.0 + t)
    slope = half + 0.5 * v * (1.0 - t * t) * (scale * (1.0 + 3.0 * 0.044715 * square))
    return v * half, slope


def first_kernel(
    place, cot, field, low, high, other, first_w, second_w, hidden, pre_grad, stack, back, pre, grad
):
    core = place[0]
    put_grid(stack, field, low, high, 1, 1, False)
    put_face(stack, core, other, 0, 8, False)
    conv_into(pre, stack, first_w)
    put_grid(back, cot, low, high, 0, 1, True)
    put_face(back, core, other, 8, 7, True)
    conv_back_into(grad, back, second_w)

    def step(i, _):
        rows = pl.ds(pl.multiple_of(i * 256, 256), 256)
        value, slope = gelu_and_slope(pre[rows])
        hidden[i] = value.astype(BF).reshape(8, 32, 256)
        pre_grad[i] = (grad[rows] * slope).astype(BF).reshape(8, 32, 256)
        return 0

    lax.fori_loop(0, 4, step, 0)


def last_kernel(
    place, hid, pre_grad, low, high, other, field, cot, first_w, second_w, out, field_grad,
    stack, back, total, grad,
):
    core = place[0]
    put_grid(stack, hid, low, high, 0, 1, False)
    put_face(stack, core, other, 8, 7, False)
    conv_into(total, stack, second_w)
    put_grid(back, pre_grad, low, high, 1, 1, True)
    put_face(back, core, other, 0, 8, True)
    conv_back_into(grad, back, first_w)

    def step(i, _):
        rows = pl.ds(pl.multiple_of(i * 256, 256), 256)
        one = field[i].astype(F32).reshape(256, 256) + total[rows]
        out[i] = one.astype(BF).reshape(8, 32, 256)
        two = cot[i].astype(F32).reshape(256, 256) + grad[rows]
        field_grad[i] = two.astype(BF).reshape(8, 32, 256)
        return 0

    lax.fori_loop(0, 4, step, 0)


def weight_kernel(
    place, cot, field, low1, high1, other1, hid, pre_grad, low2, high2, other2,
    own, send1, send2, send3, stack, turned, flat, tiles,
):
    core = place[0]

    def fill(value, low, high, which, far, near_grad, far_grad, half):
        put_grid(stack, value, low, high, which, 1 + 8 * half, False)

        def step(i, _):
            put(stack, i, 1 + 8 * (1 - half), far[i, 0:8], False)
            edge = jnp.zeros((1, 32, 768), BF)
            stack[i, 0:1] = edge
            stack[i, 17:18] = edge
            return 0

        lax.fori_loop(0, 6, step, 0)
        for i in range(4):
            at = i * 512 + 256 * half
            turned[:, at : at + 256] = near_grad[i].reshape(256, 256).T
            at = i * 512 + 256 * (1 - half)
            turned[:, at : at + 256] = far_grad[i + 1, 0:8].reshape(256, 256).T

    @pl.when(core == 0)
    def _():
        fill(field, low1, high1, 1, other1, pre_grad, other2, 0)

    @pl.when(core == 1)
    def _():
        fill(hid, low2, high2, 0, other2, cot, other1, 1)

    flat[:, 6912:7040] = jnp.zeros((256, 128), BF)

    def block(k, _):
        a, b = k // 3, k % 3
        rows = stack[pl.ds(a, 4), pl.ds(b, 16)].reshape(2048, 768)
        term = jnp.dot(turned[...], rows, preferred_element_type=F32)
        flat[:, pl.ds(pl.multiple_of(k * 768, 768), 768)] = (term * 0.125).astype(BF)
        return 0

    lax.fori_loop(0, 9, block, 0)
    for k in range(8):
        tiles[k] = flat[:, k * 864 : k * 864 + LANES]
    x, y, z = place[1], place[2], place[3]
    zero = core == 0
    for first, ref in enumerate((own, send1, send2, send3)):

        def pick(i, _):
            second, third = i // 4, i % 4
            to_x = lax.rem(x + jnp.where(zero, first, third), 4)
            to_y = lax.rem(y + jnp.where(zero, second, first), 4)
            to_z = lax.rem(z + jnp.where(zero, third, second), 4)
            to_dp = to_y * 2 + to_z // 2
            to_px = to_x * 2 + lax.rem(to_z, 2)
            ref[i] = tiles[to_dp, pl.ds(pl.multiple_of(to_px * 32, 32), 32), :]
            return 0

        lax.fori_loop(0, 16, pick, 0)


def call(kernel, name, flops, args, outs, scratch):
    whole = pl.BlockSpec(memory_space=pltpu.VMEM)
    return pl.pallas_call(
        kernel,
        name=name,
        out_shape=outs,
        in_specs=[pl.BlockSpec(memory_space=pltpu.SMEM)] + [whole] * (len(args) - 1),
        out_specs=[whole] * len(outs),
        scratch_shapes=scratch,
        compiler_params=pltpu.CompilerParams(vmem_limit_bytes=56 * 2**20),
        cost_estimate=pl.CostEstimate(
            flops=flops, bytes_accessed=8 * 2**20, transcendentals=0
        ),
    )(*args)


def exchange(first, second, core):
    count = lax.axis_size("px")
    forward = [(i, i + 1) for i in range(count - 1)]
    backward = [(i + 1, i) for i in range(count - 1)]
    low = lax.ppermute(jnp.stack([first[3], second[3]]), "px", forward)
    high = lax.ppermute(jnp.stack([first[0], second[0]]), "px", backward)
    first = jnp.concatenate([low[0:1], first, high[0:1]], axis=0)
    second = jnp.concatenate([low[1:2], second, high[1:2]], axis=0)
    full = jnp.where(core == 0, first, second)
    face = jnp.where(core == 0, second[:, 7:8], first[:, 0:1])
    other = lax.ppermute(
        jnp.concatenate([full, face], axis=1), "py", [(0, 1), (1, 0)]
    )
    return low, high, other


def hop(parts, stage):
    return [
        lax.ppermute(part, ALL, hop_pairs(stage, distance))
        for part, distance in zip(parts, (1, 3, 2))
    ]


def reduce_tiles(own, plus, two, minus, core):
    got = hop((plus, minus, two), 0)
    total = own.astype(F32)
    for part in got:
        total = total + part.astype(F32)
    got = hop([total[4 * d : 4 * d + 4].astype(BF) for d in (1, 3, 2)], 1)
    total = total[0:4]
    for part in got:
        total = total + part.astype(F32)
    got = hop([total[d] for d in (1, 3, 2)], 2)
    total = total[0] + got[0] + got[1] + got[2]
    keep = jnp.where(core == 0, total[:16], total[16:])
    give = jnp.where(core == 0, total[16:], total[:16])
    other = lax.ppermute(give, "py", [(0, 1), (1, 0)])
    first = jnp.where(core == 0, keep, other)[:, :864]
    second = jnp.where(core == 0, other, keep)[:, :864]
    return first.T, second.T


def body(fields, cotangent, first_weight, second_weight):
    shape = jax.ShapeDtypeStruct
    core = lax.axis_index("py")
    dp, px = lax.axis_index("dp"), lax.axis_index("px")
    place = jnp.stack([core, px // 2, dp // 2, (dp % 2) * 2 + px % 2]).astype(jnp.int32)
    field, cot = fields[0], cotangent[0]
    grid = shape((4, 8, 32, 256), BF)
    conv_scratch = [
        pltpu.VMEM((6, 10, 32, 768), BF),
        pltpu.VMEM((6, 10, 32, 768), BF),
        pltpu.VMEM((1024, 256), F32),
        pltpu.VMEM((1024, 256), F32),
    ]
    low1, high1, other1 = exchange(cot, field, core)
    hidden, pre_grad = call(
        first_kernel,
        "hidden",
        2 * 2 * 1024 * 6912 * 256,
        (place, cot, field, low1, high1, other1, first_weight, second_weight),
        [grid, grid],
        conv_scratch,
    )
    low2, high2, other2 = exchange(hidden, pre_grad, core)
    own, send1, send2, send3 = call(
        weight_kernel,
        "weight_terms",
        2 * 2 * 1024 * 6912 * 256,
        (place, cot, field, low1, high1, other1, hidden, pre_grad, low2, high2, other2),
        [shape((16, 32, LANES), BF)] * 4,
        [
            pltpu.VMEM((6, 18, 32, 768), BF),
            pltpu.VMEM((256, 2048), BF),
            pltpu.VMEM((256, 7040), BF),
            pltpu.VMEM((8, 256, LANES), BF),
        ],
    )
    output, field_grad = call(
        last_kernel,
        "outputs",
        2 * 2 * 1024 * 6912 * 256,
        (place, hidden, pre_grad, low2, high2, other2, field, cot, first_weight, second_weight),
        [grid, grid],
        conv_scratch,
    )
    first_grad, second_grad = reduce_tiles(own, send1, send2, send3, core)
    return output[None], field_grad[None], first_grad, second_grad


def solution(mesh):
    placed = P("dp", "px", "py", None, None)
    return jax.shard_map(
        body,
        mesh=mesh,
        in_specs=(placed, placed, P(), P()),
        out_specs=(placed, placed, P("dp", ("px", "py")), P("dp", ("px", "py"))),
        check_vma=False,
    )
```

```python
import jax
import jax.numpy as jnp
from jax import lax
from jax.experimental import pallas as pl
from jax.experimental.pallas import tpu as pltpu
from jax.sharding import PartitionSpec as P

BF = jnp.bfloat16
F32 = jnp.float32
ALL = ("dp", "px", "py")
X, Y, Z = 0, 1, 2
ORDER = ((X, Y, Z), (Y, Z, X))
LANES = 896


def device(x, y, z, core):
    x, y, z = x % 4, y % 4, z % 4
    return (y * 2 + z // 2) * 16 + (x * 2 + z % 2) * 2 + core


def hop_pairs(stage, distance):
    pairs = []
    for core in range(2):
        step = [0, 0, 0]
        step[ORDER[core][stage]] = distance
        for x in range(4):
            for y in range(4):
                for z in range(4):
                    pairs.append(
                        (
                            device(x, y, z, core),
                            device(x + step[0], y + step[1], z + step[2], core),
                        )
                    )
    return pairs


def shifted(block):
    wide = block.astype(F32)
    place = lax.broadcasted_iota(jnp.int32, wide.shape, 1)
    low = jnp.where(place == 0, 0.0, pltpu.roll(wide, 1, 1)).astype(BF)
    high = jnp.where(place == 31, 0.0, pltpu.roll(wide, 31, 1)).astype(BF)
    return low, high


def put(stack, row, start, block, flip):
    low, high = shifted(block)
    if flip:
        low, high = high, low
    rows = pl.ds(start, block.shape[0])
    stack[row, rows, :, 0:256] = low
    stack[row, rows, :, 256:512] = block
    stack[row, rows, :, 512:768] = high


def put_own(stack, slab, start, own, flip):
    def step(i, _):
        put(stack, i + slab, start, own[i], flip)
        return 0

    lax.fori_loop(0, own.shape[0], step, 0)


def put_faces(stack, core, slab, count, other, at_first, at_second, flip):
    at = jnp.where(core == 0, at_first, at_second)
    row = jnp.where(core == 0, 9, 0)

    def step(i, _):
        put(stack, i + slab, row, other[i, pl.ds(at, 1)], flip)
        stack[i + slab, pl.ds(9 - row, 1)] = jnp.zeros((1, 32, 768), BF)
        return 0

    lax.fori_loop(0, count, step, 0)


def put_halo(stack, core, slab, halo, which, flip):
    row = jnp.where(core == 0, 9, 0)
    put(stack, slab, 1, halo[which, 0:8], flip)
    put(stack, slab, row, halo[which, 8:9], flip)
    stack[slab, pl.ds(9 - row, 1)] = jnp.zeros((1, 32, 768), BF)


def conv_into(total, slabs, stack, weight):
    for k in range(9):
        a, b = k // 3, k % 3
        rows = [
            stack[x : x + n, b : b + 8].reshape(n * 256, 768) for x, n in slabs(a)
        ]
        rows = rows[0] if len(rows) == 1 else jnp.concatenate(rows, axis=0)
        term = jnp.dot(rows, weight[k * 768 : (k + 1) * 768], preferred_element_type=F32)
        if k == 0:
            total[...] = term
        else:
            total[...] += term


def conv_back_into(total, slabs, stack, weight):
    for k in range(9):
        a, b = k // 3, k % 3
        term = None
        for c in range(3):
            lanes = slice(c * 256, (c + 1) * 256)
            rows = [
                stack[x : x + n, 2 - b : 10 - b, :, lanes].reshape(n * 256, 256)
                for x, n in slabs(2 - a)
            ]
            rows = rows[0] if len(rows) == 1 else jnp.concatenate(rows, axis=0)
            block = weight[(k * 3 + c) * 256 : (k * 3 + c + 1) * 256]
            part = lax.dot_general(
                rows, block, (((1,), (1,)), ((), ())), preferred_element_type=F32
            )
            term = part if term is None else term + part
        if k == 0:
            total[...] = term
        else:
            total[...] += term


def gelu_and_slope(v):
    scale = 0.7978845608028654
    square = v * v
    t = jnp.tanh(scale * (v + 0.044715 * (square * v)))
    half = 0.5 * (1.0 + t)
    slope = half + 0.5 * v * (1.0 - t * t) * (scale * (1.0 + 3.0 * 0.044715 * square))
    return v * half, slope


def inner_kernel(
    place, cot, field, other, first_w, second_w, hidden, pre_grad, stack, back, pre, grad
):
    core = place[0]
    put_own(stack, 0, 1, field, False)
    put_faces(stack, core, 0, 4, other, 0, 8, False)
    put_own(back, 0, 1, cot, True)
    put_faces(back, core, 0, 4, other, 8, 7, True)
    conv_into(pre, lambda a: [(a, 2)], stack, first_w)
    conv_back_into(grad, lambda a: [(a, 2)], back, second_w)
    for i in range(2):
        rows = slice(i * 256, (i + 1) * 256)
        value, slope = gelu_and_slope(pre[rows])
        hidden[i] = value.astype(BF).reshape(8, 32, 256)
        pre_grad[i] = (grad[rows] * slope).astype(BF).reshape(8, 32, 256)


def outer_kernel(
    place, cot, field, other, low, high, inner_hidden, inner_grad, first_w, second_w,
    hidden, pre_grad, send, stack, back, pre, grad,
):
    core = place[0]
    put_own(stack, 1, 1, field, False)
    put_faces(stack, core, 1, 4, other, 0, 8, False)
    put_halo(stack, core, 0, low, 1, False)
    put_halo(stack, core, 5, high, 1, False)
    put_own(back, 1, 1, cot, True)
    put_faces(back, core, 1, 4, other, 8, 7, True)
    put_halo(back, core, 0, low, 0, True)
    put_halo(back, core, 5, high, 0, True)
    conv_into(pre, lambda a: [(a, 1), (a + 3, 1)], stack, first_w)
    conv_back_into(grad, lambda a: [(a, 1), (a + 3, 1)], back, second_w)
    for i in range(2):
        rows = slice(i * 256, (i + 1) * 256)
        value, slope = gelu_and_slope(pre[rows])
        hidden[3 * i] = value.astype(BF).reshape(8, 32, 256)
        pre_grad[3 * i] = (grad[rows] * slope).astype(BF).reshape(8, 32, 256)
        hidden[1 + i] = inner_hidden[i]
        pre_grad[1 + i] = inner_grad[i]

    @pl.when(core == 0)
    def _():
        send[:, 0:8] = hidden[...]
        send[:, 8:9] = pre_grad[:, 7:8]

    @pl.when(core == 1)
    def _():
        send[:, 0:8] = pre_grad[...]
        send[:, 8:9] = hidden[:, 0:1]


def last_kernel(
    place, hid, pre_grad, other, low, high, field, cot, first_w, second_w, out, field_grad,
    stack, back, total, grad,
):
    core = place[0]
    put_own(stack, 1, 1, hid, False)
    put_faces(stack, core, 1, 4, other, 8, 7, False)
    put_halo(stack, core, 0, low, 0, False)
    put_halo(stack, core, 5, high, 0, False)
    put_own(back, 1, 1, pre_grad, True)
    put_faces(back, core, 1, 4, other, 0, 8, True)
    put_halo(back, core, 0, low, 1, True)
    put_halo(back, core, 5, high, 1, True)
    conv_into(total, lambda a: [(a, 4)], stack, second_w)
    conv_back_into(grad, lambda a: [(a, 4)], back, first_w)
    for i in range(4):
        rows = slice(i * 256, (i + 1) * 256)
        one = field[i].astype(F32).reshape(256, 256) + total[rows]
        out[i] = one.astype(BF).reshape(8, 32, 256)
        two = cot[i].astype(F32).reshape(256, 256) + grad[rows]
        field_grad[i] = two.astype(BF).reshape(8, 32, 256)


def weight_kernel(
    place, cot, field, low1, high1, other1, edges, hid, pre_grad, other2,
    own, send1, send2, send3, stack, turned, local, flat, tiles,
):
    core = place[0]

    def fill(value, which, half, flip):
        near, far = 1 + 8 * half, 9 - 8 * half
        put_own(stack, 1, near, value, flip)
        put(stack, 0, near, low1[which, 0:8], flip)
        put(stack, 5, near, high1[which, 0:8], flip)
        put(stack, 0, far, edges[0], flip)
        put(stack, 5, far, edges[1], flip)

        def step(i, _):
            put(stack, i + 1, far, other1[i, 0:8], flip)
            return 0

        lax.fori_loop(0, 4, step, 0)
        for i in range(6):
            stack[i, 0:1] = jnp.zeros((1, 32, 768), BF)
            stack[i, 17:18] = jnp.zeros((1, 32, 768), BF)

    flat[:, 6912:7040] = jnp.zeros((256, 128), BF)

    @pl.when(core == 0)
    def _():
        fill(field, 1, 0, False)
        for i in range(4):
            turned[:, i * 512 : i * 512 + 256] = pre_grad[i].reshape(256, 256).T
            turned[:, i * 512 + 256 : i * 512 + 512] = other2[i, 0:8].reshape(256, 256).T

        def block(k, _):
            a, b = k // 3, k % 3
            rows = stack[pl.ds(a, 4), pl.ds(b, 16)].reshape(2048, 768)
            term = jnp.dot(turned[...], rows, preferred_element_type=F32)
            flat[:, pl.ds(pl.multiple_of(k * 768, 768), 768)] = (term * 0.125).astype(BF)
            return 0

        lax.fori_loop(0, 9, block, 0)

    @pl.when(core == 1)
    def _():
        fill(cot, 0, 1, True)
        for i in range(4):
            local[i * 512 : i * 512 + 256] = other2[i, 0:8].reshape(256, 256)
            local[i * 512 + 256 : i * 512 + 512] = hid[i].reshape(256, 256)

        def block(k, _):
            a, b = 2 - k // 3, 2 - k % 3
            rows = stack[pl.ds(a, 4), pl.ds(b, 16)].reshape(2048, 768)
            term = lax.dot_general(
                rows, local[...], (((0,), (0,)), ((), ())), preferred_element_type=F32
            )
            term = (term * 0.125).astype(BF)
            for c in range(3):
                lanes = pl.ds(pl.multiple_of((k * 3 + c) * 256, 256), 256)
                flat[:, lanes] = term[c * 256 : (c + 1) * 256]
            return 0

        lax.fori_loop(0, 9, block, 0)

    for k in range(8):
        tiles[k] = flat[:, k * 864 : k * 864 + LANES]
    x, y, z = place[1], place[2], place[3]
    zero = core == 0
    for first, ref in enumerate((own, send1, send2, send3)):

        def pick(i, _):
            second, third = i // 4, i % 4
            to_x = lax.rem(x + jnp.where(zero, first, third), 4)
            to_y = lax.rem(y + jnp.where(zero, second, first), 4)
            to_z = lax.rem(z + jnp.where(zero, third, second), 4)
            to_dp = to_y * 2 + to_z // 2
            to_px = to_x * 2 + lax.rem(to_z, 2)
            ref[i] = tiles[to_dp, pl.ds(pl.multiple_of(to_px * 32, 32), 32), :]
            return 0

        lax.fori_loop(0, 16, pick, 0)


def call(kernel, name, flops, args, outs, scratch, limit):
    whole = pl.BlockSpec(memory_space=pltpu.VMEM)
    return pl.pallas_call(
        kernel,
        name=name,
        out_shape=outs,
        in_specs=[pl.BlockSpec(memory_space=pltpu.SMEM)] + [whole] * (len(args) - 1),
        out_specs=[whole] * len(outs),
        scratch_shapes=scratch,
        compiler_params=pltpu.CompilerParams(vmem_limit_bytes=limit * 2**20),
        cost_estimate=pl.CostEstimate(
            flops=flops, bytes_accessed=8 * 2**20, transcendentals=0
        ),
    )(*args)


def swap_cores(value):
    return lax.ppermute(value, "py", [(0, 1), (1, 0)])


def swap_slabs(first, second, first_face, second_face):
    count = lax.axis_size("px")
    forward = [(i, i + 1) for i in range(count - 1)]
    backward = [(i + 1, i) for i in range(count - 1)]

    def slab(i):
        return jnp.stack(
            [
                jnp.concatenate([first[i], first_face[i]], axis=0),
                jnp.concatenate([second[i], second_face[i]], axis=0),
            ]
        )

    return lax.ppermute(slab(3), "px", forward), lax.ppermute(slab(0), "px", backward)


def hop(parts, stage):
    return [
        lax.ppermute(part, ALL, hop_pairs(stage, distance))
        for part, distance in zip(parts, (1, 3, 2))
    ]


def reduce_tiles(own, got, core):
    total = own.astype(F32)
    for part in got:
        total = total + part.astype(F32)
    got = hop([total[4 * d : 4 * d + 4].astype(BF) for d in (1, 3, 2)], 1)
    total = total[0:4]
    for part in got:
        total = total + part.astype(F32)
    got = hop([total[d] for d in (1, 3, 2)], 2)
    total = total[0] + got[0] + got[1] + got[2]
    keep = jnp.where(core == 0, total[:16], total[16:])
    give = jnp.where(core == 0, total[16:], total[:16])
    other = swap_cores(give)
    first = jnp.where(core == 0, keep, other)[:, :864]
    second = jnp.where(core == 0, other, keep)[:, :864]
    return first.T, second.T


def body(fields, cotangent, first_weight, second_weight):
    shape = jax.ShapeDtypeStruct
    core = lax.axis_index("py")
    dp, px = lax.axis_index("dp"), lax.axis_index("px")
    zero = core == 0
    two = jnp.int32(2)
    place = jnp.stack(
        [core, lax.div(px, two), lax.div(dp, two), lax.rem(dp, two) * 2 + lax.rem(px, two)]
    )
    field, cot = fields[0], cotangent[0]
    grid, half = shape((4, 8, 32, 256), BF), shape((2, 8, 32, 256), BF)

    def conv_scratch(slabs, rows):
        return [pltpu.VMEM((slabs, 10, 32, 768), BF)] * 2 + [pltpu.VMEM((rows, 256), F32)] * 2

    flops = 2 * 2 * 1024 * 6912 * 256
    other1 = swap_cores(
        jnp.where(
            zero,
            jnp.concatenate([cot, field[:, 7:8]], axis=1),
            jnp.concatenate([field, cot[:, 0:1]], axis=1),
        )
    )
    low1, high1 = swap_slabs(
        cot,
        field,
        jnp.where(zero, other1[:, 8:9], other1[:, 7:8]),
        jnp.where(zero, other1[:, 0:1], other1[:, 8:9]),
    )
    inner_hidden, inner_grad = call(
        inner_kernel,
        "inner",
        flops // 2,
        (place, cot, field, other1, first_weight, second_weight),
        [half, half],
        conv_scratch(4, 512),
        24,
    )
    hidden, pre_grad, send = call(
        outer_kernel,
        "outer",
        flops // 2,
        (
            place, cot, field, other1, low1, high1, inner_hidden, inner_grad,
            first_weight, second_weight,
        ),
        [grid, grid, shape((4, 9, 32, 256), BF)],
        conv_scratch(6, 512),
        26,
    )
    edges = swap_cores(
        jnp.where(
            zero,
            jnp.stack([low1[0, 0:8], high1[0, 0:8]]),
            jnp.stack([low1[1, 0:8], high1[1, 0:8]]),
        )
    )
    other2 = swap_cores(send)
    low2, high2 = swap_slabs(
        hidden,
        pre_grad,
        jnp.where(zero, other2[:, 8:9], other2[:, 7:8]),
        jnp.where(zero, other2[:, 0:1], other2[:, 8:9]),
    )
    own, send1, send2, send3 = call(
        weight_kernel,
        "weight_terms",
        flops,
        (place, cot, field, low1, high1, other1, edges, hidden, pre_grad, other2),
        [shape((16, 32, LANES), BF)] * 4,
        [
            pltpu.VMEM((6, 18, 32, 768), BF),
            pltpu.VMEM((256, 2048), BF),
            pltpu.VMEM((2048, 256), BF),
            pltpu.VMEM((256, 7040), BF),
            pltpu.VMEM((8, 256, LANES), BF),
        ],
        34,
    )
    got = hop((send1, send3, send2), 0)
    hidden, pre_grad, send1 = lax.optimization_barrier((hidden, pre_grad, send1))
    output, field_grad = call(
        last_kernel,
        "outputs",
        flops,
        (
            place, hidden, pre_grad, other2, low2, high2, field, cot,
            first_weight, second_weight,
        ),
        [grid, grid],
        conv_scratch(6, 1024),
        28,
    )
    own, output, field_grad = lax.optimization_barrier((own, output, field_grad))
    first_grad, second_grad = reduce_tiles(own, got, core)
    return output[None], field_grad[None], first_grad, second_grad


def solution(mesh):
    placed = P("dp", "px", "py", None, None)
    return jax.shard_map(
        body,
        mesh=mesh,
        in_specs=(placed, placed, P(), P()),
        out_specs=(placed, placed, P("dp", ("px", "py")), P("dp", ("px", "py"))),
        check_vma=False,
    )
```

```python
import jax
import jax.numpy as jnp
from jax import lax
from jax.experimental import pallas as pl
from jax.experimental.pallas import tpu as pltpu
from jax.sharding import PartitionSpec as P

BF = jnp.bfloat16
F32 = jnp.float32
ALL = ("dp", "px", "py")
X, Y, Z = 0, 1, 2
ORDER = ((X, Y, Z), (Y, Z, X))
LANES = 896


def device(x, y, z, core):
    x, y, z = x % 4, y % 4, z % 4
    return (y * 2 + z // 2) * 16 + (x * 2 + z % 2) * 2 + core


def hop_pairs(stage, distance):
    pairs = []
    for core in range(2):
        step = [0, 0, 0]
        step[ORDER[core][stage]] = distance
        for x in range(4):
            for y in range(4):
                for z in range(4):
                    pairs.append(
                        (
                            device(x, y, z, core),
                            device(x + step[0], y + step[1], z + step[2], core),
                        )
                    )
    return pairs


def shifted(block):
    wide = block.astype(F32)
    place = lax.broadcasted_iota(jnp.int32, wide.shape, 1)
    low = jnp.where(place == 0, 0.0, pltpu.roll(wide, 1, 1)).astype(BF)
    high = jnp.where(place == 31, 0.0, pltpu.roll(wide, 31, 1)).astype(BF)
    return low, high


def put(stack, row, start, block, flip):
    low, high = shifted(block)
    if flip:
        low, high = high, low
    rows = pl.ds(start, block.shape[0])
    stack[row, rows, :, 0:256] = low
    stack[row, rows, :, 256:512] = block
    stack[row, rows, :, 512:768] = high


def put_own(stack, slab, start, own, flip):
    def step(i, _):
        put(stack, i + slab, start, own[i], flip)
        return 0

    lax.fori_loop(0, own.shape[0], step, 0)


def put_faces(stack, core, slab, count, other, at_first, at_second, flip):
    at = jnp.where(core == 0, at_first, at_second)
    row = jnp.where(core == 0, 9, 0)

    def step(i, _):
        put(stack, i + slab, row, other[i, pl.ds(at, 1)], flip)
        stack[i + slab, pl.ds(9 - row, 1)] = jnp.zeros((1, 32, 768), BF)
        return 0

    lax.fori_loop(0, count, step, 0)


def put_halo(stack, core, slab, halo, which, flip):
    row = jnp.where(core == 0, 9, 0)
    put(stack, slab, 1, halo[which, 0:8], flip)
    put(stack, slab, row, halo[which, 8:9], flip)
    stack[slab, pl.ds(9 - row, 1)] = jnp.zeros((1, 32, 768), BF)


def term_of(rows, weight, k, back):
    if not back:
        return jnp.dot(rows, weight[k * 768 : (k + 1) * 768], preferred_element_type=F32)
    term = None
    for c in range(3):
        part = lax.dot_general(
            rows[:, c * 256 : (c + 1) * 256],
            weight[(k * 3 + c) * 256 : (k * 3 + c + 1) * 256],
            (((1,), (1,)), ((), ())),
            preferred_element_type=F32,
        )
        term = part if term is None else term + part
    return term


def conv_own(total, stack, weight, back):
    for a in (1, 0, 2):
        step = 1 - a if back else a - 1
        count = 4 - abs(step)
        to = max(0, -step)
        for b in range(3):
            at = 2 - b if back else b
            rows = stack[to + step : to + step + count, at : at + 8].reshape(count * 256, 768)
            term = term_of(rows, weight, a * 3 + b, back)
            span = slice(to * 256, (to + count) * 256)
            if a == 1 and b == 0:
                total[span] = term
            else:
                total[span] += term


def conv_edges(part, stack, weight, back):
    sums = []
    for side in range(2):
        a = 2 * side if not back else 2 - 2 * side
        total = part[side]
        for b in range(3):
            at = 2 - b if back else b
            rows = stack[side, at : at + 8].reshape(256, 768)
            total = total + term_of(rows, weight, a * 3 + b, back)
        sums.append(total)
    return sums


def gelu_and_slope(v):
    scale = 0.7978845608028654
    square = v * v
    t = jnp.tanh(scale * (v + 0.044715 * (square * v)))
    half = 0.5 * (1.0 + t)
    slope = half + 0.5 * v * (1.0 - t * t) * (scale * (1.0 + 3.0 * 0.044715 * square))
    return v * half, slope


def near_side(place):
    return 1 - lax.rem(place[3], 2)


def pack_kernel(place, cot, field, send, arrived):
    core = place[0]

    def pack(whole, row):
        copies = [
            pltpu.make_async_copy(whole, send.at[:, 0:8], arrived.at[0]),
            pltpu.make_async_copy(row, send.at[:, 8:9], arrived.at[1]),
        ]
        for copy in copies:
            copy.start()
        for copy in copies:
            copy.wait()

    @pl.when(core == 0)
    def _():
        pack(cot, field.at[:, 7:8])

    @pl.when(core == 1)
    def _():
        pack(field, cot.at[:, 0:1])


def inner_kernel(
    place, cot, field, other, first_hbm, second_hbm, hidden, pre_grad, part_pre, part_grad,
    first_w, second_w, stack, back, pre, grad, arrived,
):
    core = place[0]
    copies = [
        pltpu.make_async_copy(first_hbm, first_w, arrived.at[0]),
        pltpu.make_async_copy(second_hbm, second_w, arrived.at[1]),
    ]
    for copy in copies:
        copy.start()
    put_own(stack, 0, 1, field, False)
    put_faces(stack, core, 0, 4, other, 0, 8, False)
    put_own(back, 0, 1, cot, True)
    put_faces(back, core, 0, 4, other, 8, 7, True)
    copies[0].wait()
    conv_own(pre, stack, first_w, False)
    copies[1].wait()
    conv_own(grad, back, second_w, True)
    for i in range(2):
        rows = slice((i + 1) * 256, (i + 2) * 256)
        value, slope = gelu_and_slope(pre[rows])
        hidden[i] = value.astype(BF).reshape(8, 32, 256)
        pre_grad[i] = (grad[rows] * slope).astype(BF).reshape(8, 32, 256)
        rows = slice(i * 768, i * 768 + 256)
        part_pre[i] = pre[rows]
        part_grad[i] = grad[rows]


def outer_kernel(
    place, near, far, inner_hidden, inner_grad, part_pre, part_grad, first_w, second_w,
    hidden, pre_grad, send, stack, back,
):
    core = place[0]
    side = near_side(place)
    put_halo(stack, core, side, near, 1, False)
    put_halo(stack, core, 1 - side, far, 1, False)
    put_halo(back, core, side, near, 0, True)
    put_halo(back, core, 1 - side, far, 0, True)
    pre = conv_edges(part_pre, stack, first_w, False)
    grad = conv_edges(part_grad, back, second_w, True)
    for i in range(2):
        value, slope = gelu_and_slope(pre[i])
        hidden[3 * i] = value.astype(BF).reshape(8, 32, 256)
        pre_grad[3 * i] = (grad[i] * slope).astype(BF).reshape(8, 32, 256)
        hidden[1 + i] = inner_hidden[i]
        pre_grad[1 + i] = inner_grad[i]

    @pl.when(core == 0)
    def _():
        send[:, 0:8] = hidden[...]
        send[:, 8:9] = pre_grad[:, 7:8]

    @pl.when(core == 1)
    def _():
        send[:, 0:8] = pre_grad[...]
        send[:, 8:9] = hidden[:, 0:1]


def last_inner_kernel(
    place, hid, pre_grad, other, field, cot, first_w, second_w,
    out, field_grad, part_out, part_grad, stack, back, total, grad,
):
    core = place[0]
    put_own(stack, 0, 1, hid, False)
    put_faces(stack, core, 0, 4, other, 8, 7, False)
    put_own(back, 0, 1, pre_grad, True)
    put_faces(back, core, 0, 4, other, 0, 8, True)
    conv_own(total, stack, second_w, False)
    conv_own(grad, back, first_w, True)
    for i in range(2):
        rows = slice((i + 1) * 256, (i + 2) * 256)
        one = field[i + 1].astype(F32).reshape(256, 256) + total[rows]
        out[i] = one.astype(BF).reshape(8, 32, 256)
        two = cot[i + 1].astype(F32).reshape(256, 256) + grad[rows]
        field_grad[i] = two.astype(BF).reshape(8, 32, 256)
        rows = slice(i * 768, i * 768 + 256)
        part_out[i] = total[rows]
        part_grad[i] = grad[rows]


def last_outer_kernel(
    place, near, far, inner_out, inner_grad, part_out, part_grad, field, cot, first_w, second_w,
    out, field_grad, stack, back,
):
    core = place[0]
    side = near_side(place)
    put_halo(stack, core, side, near, 0, False)
    put_halo(stack, core, 1 - side, far, 0, False)
    put_halo(back, core, side, near, 1, True)
    put_halo(back, core, 1 - side, far, 1, True)
    total = conv_edges(part_out, stack, second_w, False)
    grad = conv_edges(part_grad, back, first_w, True)
    for i in range(2):
        one = field[3 * i].astype(F32).reshape(256, 256) + total[i]
        out[3 * i] = one.astype(BF).reshape(8, 32, 256)
        two = cot[3 * i].astype(F32).reshape(256, 256) + grad[i]
        field_grad[3 * i] = two.astype(BF).reshape(8, 32, 256)
        out[1 + i] = inner_out[i]
        field_grad[1 + i] = inner_grad[i]


def weight_kernel(
    place, cot, field, near1, far1, other1, edges, hid, pre_grad, other2,
    own, send1, send2, send3, stack, turned, local, flat, tiles,
):
    core = place[0]

    def fill(value, which, half, flip):
        mine, others = 1 + 8 * half, 9 - 8 * half
        near = 5 * near_side(place)
        put_own(stack, 1, mine, value, flip)
        put(stack, near, mine, near1[which, 0:8], flip)
        put(stack, 5 - near, mine, far1[which, 0:8], flip)
        put(stack, near, others, edges[0], flip)
        put(stack, 5 - near, others, edges[1], flip)

        def step(i, _):
            put(stack, i + 1, others, other1[i, 0:8], flip)
            return 0

        lax.fori_loop(0, 4, step, 0)
        for i in range(6):
            stack[i, 0:1] = jnp.zeros((1, 32, 768), BF)
            stack[i, 17:18] = jnp.zeros((1, 32, 768), BF)

    flat[:, 6912:7040] = jnp.zeros((256, 128), BF)

    @pl.when(core == 0)
    def _():
        fill(field, 1, 0, False)
        for i in range(4):
            turned[:, i * 512 : i * 512 + 256] = pre_grad[i].reshape(256, 256).T
            turned[:, i * 512 + 256 : i * 512 + 512] = other2[i, 0:8].reshape(256, 256).T

        def block(k, _):
            a, b = k // 3, k % 3
            rows = stack[pl.ds(a, 4), pl.ds(b, 16)].reshape(2048, 768)
            term = jnp.dot(turned[...], rows, preferred_element_type=F32)
            flat[:, pl.ds(pl.multiple_of(k * 768, 768), 768)] = (term * 0.125).astype(BF)
            return 0

        lax.fori_loop(0, 9, block, 0, unroll=True)

    @pl.when(core == 1)
    def _():
        fill(cot, 0, 1, True)
        for i in range(4):
            local[i * 512 : i * 512 + 256] = other2[i, 0:8].reshape(256, 256)
            local[i * 512 + 256 : i * 512 + 512] = hid[i].reshape(256, 256)

        def block(k, _):
            a, b = 2 - k // 3, 2 - k % 3
            rows = stack[pl.ds(a, 4), pl.ds(b, 16)].reshape(2048, 768)
            term = lax.dot_general(
                rows, local[...], (((0,), (0,)), ((), ())), preferred_element_type=F32
            )
            term = (term * 0.125).astype(BF)
            for c in range(3):
                lanes = pl.ds(pl.multiple_of((k * 3 + c) * 256, 256), 256)
                flat[:, lanes] = term[c * 256 : (c + 1) * 256]
            return 0

        lax.fori_loop(0, 9, block, 0, unroll=True)

    for k in range(8):
        tiles[k] = flat[:, k * 864 : k * 864 + LANES]
    x, y, z = place[1], place[2], place[3]
    zero = core == 0
    for first, ref in enumerate((own, send1, send2, send3)):

        def pick(i, _):
            second, third = i // 4, i % 4
            to_x = lax.rem(x + jnp.where(zero, first, third), 4)
            to_y = lax.rem(y + jnp.where(zero, second, first), 4)
            to_z = lax.rem(z + jnp.where(zero, third, second), 4)
            to_dp = to_y * 2 + to_z // 2
            to_px = to_x * 2 + lax.rem(to_z, 2)
            ref[i] = tiles[to_dp, pl.ds(pl.multiple_of(to_px * 32, 32), 32), :]
            return 0

        lax.fori_loop(0, 16, pick, 0, unroll=8)


def call(kernel, name, flops, args, outs, scratch, limit, far=()):
    whole = pl.BlockSpec(memory_space=pltpu.VMEM)
    return pl.pallas_call(
        kernel,
        name=name,
        out_shape=outs,
        in_specs=[pl.BlockSpec(memory_space=pltpu.SMEM)]
        + [
            pl.BlockSpec(memory_space=pltpu.HBM) if i in far else whole
            for i in range(1, len(args))
        ],
        out_specs=[whole] * len(outs),
        scratch_shapes=scratch,
        compiler_params=pltpu.CompilerParams(vmem_limit_bytes=limit * 2**20),
        cost_estimate=pl.CostEstimate(
            flops=flops, bytes_accessed=8 * 2**20, transcendentals=0
        ),
    )(*args)


def swap_cores(value):
    return lax.ppermute(value, "py", [(0, 1), (1, 0)])


def swap_slabs(first, second, first_face, second_face, low_half):
    count = lax.axis_size("px")
    near = [(i, i ^ 1) for i in range(count)]
    far = [(i, i + 1 if i % 2 else i - 1) for i in range(1, count - 1)]

    def slab(i):
        return jnp.stack(
            [
                jnp.concatenate([first[i], first_face[i]], axis=0),
                jnp.concatenate([second[i], second_face[i]], axis=0),
            ]
        )

    low, high = slab(0), slab(3)
    got_far = lax.ppermute(jnp.where(low_half, low, high), "px", far)
    got_near = lax.ppermute(jnp.where(low_half, high, low), "px", near)
    return got_near, got_far


def hop(parts, stage):
    return [
        lax.ppermute(part, ALL, hop_pairs(stage, distance))
        for part, distance in zip(parts, (1, 3, 2))
    ]


def reduce_tiles(own, got, core):
    total = own.astype(F32)
    for part in got:
        total = total + part.astype(F32)
    got = hop([total[4 * d : 4 * d + 4].astype(BF) for d in (1, 3, 2)], 1)
    total = total[0:4]
    for part in got:
        total = total + part.astype(F32)
    got = hop([total[d] for d in (1, 3, 2)], 2)
    total = total[0] + got[0] + got[1] + got[2]
    keep = jnp.where(core == 0, total[:16], total[16:])
    give = jnp.where(core == 0, total[16:], total[:16])
    other = swap_cores(give)
    first = jnp.where(core == 0, keep, other)[:, :864]
    second = jnp.where(core == 0, other, keep)[:, :864]
    return first.T, second.T


def body(fields, cotangent, first_weight, second_weight):
    shape = jax.ShapeDtypeStruct
    core = lax.axis_index("py")
    dp, px = lax.axis_index("dp"), lax.axis_index("px")
    zero = core == 0
    two = jnp.int32(2)
    place = jnp.stack(
        [core, lax.div(px, two), lax.div(dp, two), lax.rem(dp, two) * 2 + lax.rem(px, two)]
    )
    field, cot = fields[0], cotangent[0]
    grid, half = shape((4, 8, 32, 256), BF), shape((2, 8, 32, 256), BF)

    part = shape((2, 256, 256), F32)
    low_half = lax.rem(px, two) == 0
    own_scratch = [pltpu.VMEM((4, 10, 32, 768), BF)] * 2 + [pltpu.VMEM((1024, 256), F32)] * 2
    edge_scratch = [pltpu.VMEM((2, 10, 32, 768), BF)] * 2
    weights = (first_weight, second_weight)
    flops = 2 * 2 * 1024 * 6912 * 256
    (sent1,) = call(
        pack_kernel,
        "pack",
        0,
        (place, cot, field),
        [shape((4, 9, 32, 256), BF)],
        [pltpu.SemaphoreType.DMA((2,))],
        56,
        (1, 2),
    )
    other1 = swap_cores(sent1)
    near1, far1 = swap_slabs(
        cot,
        field,
        jnp.where(zero, other1[:, 8:9], other1[:, 7:8]),
        jnp.where(zero, other1[:, 0:1], other1[:, 8:9]),
        low_half,
    )
    inner = call(
        inner_kernel,
        "inner",
        flops * 5 // 6,
        (place, cot, field, other1, *weights),
        [half, half, part, part, shape((6912, 256), BF), shape((6912, 256), BF)],
        own_scratch + [pltpu.SemaphoreType.DMA((2,))],
        42,
        (4, 5),
    )
    inner, weights = inner[:4], inner[4:]
    hidden, pre_grad, sent2 = call(
        outer_kernel,
        "outer",
        flops // 6,
        (place, near1, far1, *inner, *weights),
        [grid, grid, shape((4, 9, 32, 256), BF)],
        edge_scratch,
        24,
    )
    edges = swap_cores(
        jnp.where(
            zero,
            jnp.stack([near1[0, 0:8], far1[0, 0:8]]),
            jnp.stack([near1[1, 0:8], far1[1, 0:8]]),
        )
    )
    other2 = swap_cores(sent2)
    own, send1, send2, send3 = call(
        weight_kernel,
        "weight_terms",
        flops,
        (place, cot, field, near1, far1, other1, edges, hidden, pre_grad, other2),
        [shape((16, 32, LANES), BF)] * 4,
        [
            pltpu.VMEM((6, 18, 32, 768), BF),
            pltpu.VMEM((256, 2048), BF),
            pltpu.VMEM((2048, 256), BF),
            pltpu.VMEM((256, 7040), BF),
            pltpu.VMEM((8, 256, LANES), BF),
        ],
        34,
    )
    got = hop((send1, send3, send2), 0)
    hidden, pre_grad, other2, own = lax.optimization_barrier((hidden, pre_grad, other2, own))
    near2, far2 = swap_slabs(
        hidden,
        pre_grad,
        jnp.where(zero, other2[:, 8:9], other2[:, 7:8]),
        jnp.where(zero, other2[:, 0:1], other2[:, 8:9]),
        low_half,
    )
    last = call(
        last_inner_kernel,
        "outputs_inner",
        flops * 5 // 6,
        (place, hidden, pre_grad, other2, field, cot, *weights),
        [half, half, part, part],
        own_scratch,
        26,
    )
    output, field_grad = call(
        last_outer_kernel,
        "outputs_outer",
        flops // 6,
        (place, near2, far2, *last, field, cot, *weights),
        [grid, grid],
        edge_scratch,
        24,
    )
    own, output, field_grad = lax.optimization_barrier((own, output, field_grad))
    first_grad, second_grad = reduce_tiles(own, got, core)
    return output[None], field_grad[None], first_grad, second_grad


def solution(mesh):
    placed = P("dp", "px", "py", None, None)
    return jax.shard_map(
        body,
        mesh=mesh,
        in_specs=(placed, placed, P(), P()),
        out_specs=(placed, placed, P("dp", ("px", "py")), P("dp", ("px", "py"))),
        check_vma=False,
    )
```

```python
import jax
import jax.numpy as jnp
from jax import lax
from jax.experimental import pallas as pl
from jax.experimental.pallas import tpu as pltpu
from jax.sharding import PartitionSpec as P

BF = jnp.bfloat16
F32 = jnp.float32
ALL = ("dp", "px", "py")
X, Y, Z = 0, 1, 2
ORDER = ((X, Y, Z), (Y, Z, X))
LANES = 896


def device(x, y, z, core):
    x, y, z = x % 4, y % 4, z % 4
    return (y * 2 + z // 2) * 16 + (x * 2 + z % 2) * 2 + core


def hop_pairs(stage, distance):
    pairs = []
    for core in range(2):
        step = [0, 0, 0]
        step[ORDER[core][stage]] = distance
        for x in range(4):
            for y in range(4):
                for z in range(4):
                    pairs.append(
                        (
                            device(x, y, z, core),
                            device(x + step[0], y + step[1], z + step[2], core),
                        )
                    )
    return pairs


def shifted(block):
    wide = block.astype(F32)
    place = lax.broadcasted_iota(jnp.int32, wide.shape, 1)
    low = jnp.where(place == 0, 0.0, pltpu.roll(wide, 1, 1)).astype(BF)
    high = jnp.where(place == 31, 0.0, pltpu.roll(wide, 31, 1)).astype(BF)
    return low, high


def put(stack, row, start, block, flip):
    low, high = shifted(block)
    if flip:
        low, high = high, low
    rows = pl.ds(start, block.shape[0])
    stack[row, rows, :, 0:256] = low
    stack[row, rows, :, 256:512] = block
    stack[row, rows, :, 512:768] = high


def put_own(stack, slab, start, own, flip):
    def step(i, _):
        put(stack, i + slab, start, own[i], flip)
        return 0

    lax.fori_loop(0, own.shape[0], step, 0)


def put_faces(stack, core, slab, count, other, at_first, at_second, flip):
    at = jnp.where(core == 0, at_first, at_second)
    row = jnp.where(core == 0, 9, 0)

    def step(i, _):
        put(stack, i + slab, row, other[i, pl.ds(at, 1)], flip)
        stack[i + slab, pl.ds(9 - row, 1)] = jnp.zeros((1, 32, 768), BF)
        return 0

    lax.fori_loop(0, count, step, 0)


def put_halo(stack, core, slab, halo, which, flip):
    row = jnp.where(core == 0, 9, 0)
    put(stack, slab, 1, halo[which, 0:8], flip)
    put(stack, slab, row, halo[which, 8:9], flip)
    stack[slab, pl.ds(9 - row, 1)] = jnp.zeros((1, 32, 768), BF)


def term_of(rows, weight, k, back):
    if not back:
        return jnp.dot(rows, weight[k * 768 : (k + 1) * 768], preferred_element_type=F32)
    term = None
    for c in range(3):
        part = lax.dot_general(
            rows[:, c * 256 : (c + 1) * 256],
            weight[(k * 3 + c) * 256 : (k * 3 + c + 1) * 256],
            (((1,), (1,)), ((), ())),
            preferred_element_type=F32,
        )
        term = part if term is None else term + part
    return term


def conv_own(total, stack, weight, back):
    for a in (1, 0, 2):
        step = 1 - a if back else a - 1
        count = 4 - abs(step)
        to = max(0, -step)
        for b in range(3):
            at = 2 - b if back else b
            rows = stack[to + step : to + step + count, at : at + 8].reshape(count * 256, 768)
            term = term_of(rows, weight, a * 3 + b, back)
            span = slice(to * 256, (to + count) * 256)
            if a == 1 and b == 0:
                total[span] = term
            else:
                total[span] += term


def conv_edges(part, stack, weight, back):
    sums = []
    for side in range(2):
        a = 2 * side if not back else 2 - 2 * side
        total = part[side]
        for b in range(3):
            at = 2 - b if back else b
            rows = stack[side, at : at + 8].reshape(256, 768)
            total = total + term_of(rows, weight, a * 3 + b, back)
        sums.append(total)
    return sums


def gelu_and_slope(v):
    scale = 0.7978845608028654
    square = v * v
    t = jnp.tanh(scale * (v + 0.044715 * (square * v)))
    half = 0.5 * (1.0 + t)
    slope = half + 0.5 * v * (1.0 - t * t) * (scale * (1.0 + 3.0 * 0.044715 * square))
    return v * half, slope


def near_side(place):
    return 1 - lax.rem(place[3], 2)


def pack_kernel(place, cot, field, send, arrived):
    core = place[0]

    def pack(whole, row):
        copies = [
            pltpu.make_async_copy(whole, send.at[:, 0:8], arrived.at[0]),
            pltpu.make_async_copy(row, send.at[:, 8:9], arrived.at[1]),
        ]
        for copy in copies:
            copy.start()
        for copy in copies:
            copy.wait()

    @pl.when(core == 0)
    def _():
        pack(cot, field.at[:, 7:8])

    @pl.when(core == 1)
    def _():
        pack(field, cot.at[:, 0:1])


def inner_kernel(
    place, cot, field, other, first_hbm, second_hbm, hidden, pre_grad, part_pre, part_grad,
    first_w, second_w, stack, back, pre, grad, arrived,
):
    core = place[0]
    copies = [
        pltpu.make_async_copy(first_hbm, first_w, arrived.at[0]),
        pltpu.make_async_copy(second_hbm, second_w, arrived.at[1]),
    ]
    for copy in copies:
        copy.start()
    put_own(stack, 0, 1, field, False)
    put_faces(stack, core, 0, 4, other, 0, 8, False)
    put_own(back, 0, 1, cot, True)
    put_faces(back, core, 0, 4, other, 8, 7, True)
    for copy in copies:
        copy.wait()
    conv_own(pre, stack, first_w, False)
    conv_own(grad, back, second_w, True)
    for i in range(2):
        rows = slice((i + 1) * 256, (i + 2) * 256)
        value, slope = gelu_and_slope(pre[rows])
        hidden[i] = value.astype(BF).reshape(8, 32, 256)
        pre_grad[i] = (grad[rows] * slope).astype(BF).reshape(8, 32, 256)
        rows = slice(i * 768, i * 768 + 256)
        part_pre[i] = pre[rows]
        part_grad[i] = grad[rows]


def outer_kernel(
    place, near, far, inner_hidden, inner_grad, part_pre, part_grad, first_w, second_w,
    hidden, pre_grad, send, stack, back,
):
    core = place[0]
    side = near_side(place)
    put_halo(stack, core, side, near, 1, False)
    put_halo(stack, core, 1 - side, far, 1, False)
    put_halo(back, core, side, near, 0, True)
    put_halo(back, core, 1 - side, far, 0, True)
    pre = conv_edges(part_pre, stack, first_w, False)
    grad = conv_edges(part_grad, back, second_w, True)
    for i in range(2):
        value, slope = gelu_and_slope(pre[i])
        hidden[3 * i] = value.astype(BF).reshape(8, 32, 256)
        pre_grad[3 * i] = (grad[i] * slope).astype(BF).reshape(8, 32, 256)
        hidden[1 + i] = inner_hidden[i]
        pre_grad[1 + i] = inner_grad[i]

    @pl.when(core == 0)
    def _():
        send[:, 0:8] = hidden[...]
        send[:, 8:9] = pre_grad[:, 7:8]

    @pl.when(core == 1)
    def _():
        send[:, 0:8] = pre_grad[...]
        send[:, 8:9] = hidden[:, 0:1]


def last_inner_kernel(
    place, hid, pre_grad, other, field, cot, first_w, second_w,
    out, field_grad, part_out, part_grad, stack, back, total, grad,
):
    core = place[0]
    put_own(stack, 0, 1, hid, False)
    put_faces(stack, core, 0, 4, other, 8, 7, False)
    put_own(back, 0, 1, pre_grad, True)
    put_faces(back, core, 0, 4, other, 0, 8, True)
    conv_own(total, stack, second_w, False)
    conv_own(grad, back, first_w, True)
    for i in range(2):
        rows = slice((i + 1) * 256, (i + 2) * 256)
        one = field[i + 1].astype(F32).reshape(256, 256) + total[rows]
        out[i] = one.astype(BF).reshape(8, 32, 256)
        two = cot[i + 1].astype(F32).reshape(256, 256) + grad[rows]
        field_grad[i] = two.astype(BF).reshape(8, 32, 256)
        rows = slice(i * 768, i * 768 + 256)
        part_out[i] = total[rows]
        part_grad[i] = grad[rows]


def last_outer_kernel(
    place, near, far, inner_out, inner_grad, part_out, part_grad, field, cot, first_w, second_w,
    out, field_grad, stack, back,
):
    core = place[0]
    side = near_side(place)
    put_halo(stack, core, side, near, 0, False)
    put_halo(stack, core, 1 - side, far, 0, False)
    put_halo(back, core, side, near, 1, True)
    put_halo(back, core, 1 - side, far, 1, True)
    total = conv_edges(part_out, stack, second_w, False)
    grad = conv_edges(part_grad, back, first_w, True)
    for i in range(2):
        one = field[3 * i].astype(F32).reshape(256, 256) + total[i]
        out[3 * i] = one.astype(BF).reshape(8, 32, 256)
        two = cot[3 * i].astype(F32).reshape(256, 256) + grad[i]
        field_grad[3 * i] = two.astype(BF).reshape(8, 32, 256)
        out[1 + i] = inner_out[i]
        field_grad[1 + i] = inner_grad[i]


def weight_kernel(
    place, cot, field, near1, far1, other1, edges, hid, pre_grad, other2,
    own, send1, send2, send3, stack, turned, local, flat, tiles,
):
    core = place[0]

    def fill(value, which, half, flip):
        mine, others = 1 + 8 * half, 9 - 8 * half
        near = 5 * near_side(place)
        put_own(stack, 1, mine, value, flip)
        put(stack, near, mine, near1[which, 0:8], flip)
        put(stack, 5 - near, mine, far1[which, 0:8], flip)
        put(stack, near, others, edges[0], flip)
        put(stack, 5 - near, others, edges[1], flip)

        def step(i, _):
            put(stack, i + 1, others, other1[i, 0:8], flip)
            return 0

        lax.fori_loop(0, 4, step, 0)
        for i in range(6):
            stack[i, 0:1] = jnp.zeros((1, 32, 768), BF)
            stack[i, 17:18] = jnp.zeros((1, 32, 768), BF)

    flat[:, 6912:7040] = jnp.zeros((256, 128), BF)

    @pl.when(core == 0)
    def _():
        fill(field, 1, 0, False)
        for i in range(4):
            turned[:, i * 512 : i * 512 + 256] = pre_grad[i].reshape(256, 256).T
            turned[:, i * 512 + 256 : i * 512 + 512] = other2[i, 0:8].reshape(256, 256).T

        def block(k, _):
            a, b = k // 3, k % 3
            rows = stack[pl.ds(a, 4), pl.ds(b, 16)].reshape(2048, 768)
            term = jnp.dot(turned[...], rows, preferred_element_type=F32)
            flat[:, pl.ds(pl.multiple_of(k * 768, 768), 768)] = (term * 0.125).astype(BF)
            return 0

        lax.fori_loop(0, 9, block, 0, unroll=True)

    @pl.when(core == 1)
    def _():
        fill(cot, 0, 1, True)
        for i in range(4):
            local[i * 512 : i * 512 + 256] = other2[i, 0:8].reshape(256, 256)
            local[i * 512 + 256 : i * 512 + 512] = hid[i].reshape(256, 256)

        def block(k, _):
            a, b = 2 - k // 3, 2 - k % 3
            rows = stack[pl.ds(a, 4), pl.ds(b, 16)].reshape(2048, 768)
            term = lax.dot_general(
                rows, local[...], (((0,), (0,)), ((), ())), preferred_element_type=F32
            )
            term = (term * 0.125).astype(BF)
            for c in range(3):
                lanes = pl.ds(pl.multiple_of((k * 3 + c) * 256, 256), 256)
                flat[:, lanes] = term[c * 256 : (c + 1) * 256]
            return 0

        lax.fori_loop(0, 9, block, 0, unroll=True)

    for k in range(8):
        tiles[k] = flat[:, k * 864 : k * 864 + LANES]
    x, y, z = place[1], place[2], place[3]
    zero = core == 0
    for first, ref in enumerate((own, send1, send2, send3)):

        def pick(i, _):
            second, third = i // 4, i % 4
            to_x = lax.rem(x + jnp.where(zero, first, third), 4)
            to_y = lax.rem(y + jnp.where(zero, second, first), 4)
            to_z = lax.rem(z + jnp.where(zero, third, second), 4)
            to_dp = to_y * 2 + to_z // 2
            to_px = to_x * 2 + lax.rem(to_z, 2)
            ref[i] = tiles[to_dp, pl.ds(pl.multiple_of(to_px * 32, 32), 32), :]
            return 0

        lax.fori_loop(0, 16, pick, 0, unroll=8)


def call(kernel, name, flops, args, outs, scratch, limit, far=()):
    whole = pl.BlockSpec(memory_space=pltpu.VMEM)
    return pl.pallas_call(
        kernel,
        name=name,
        out_shape=outs,
        in_specs=[pl.BlockSpec(memory_space=pltpu.SMEM)]
        + [
            pl.BlockSpec(memory_space=pltpu.HBM) if i in far else whole
            for i in range(1, len(args))
        ],
        out_specs=[whole] * len(outs),
        scratch_shapes=scratch,
        compiler_params=pltpu.CompilerParams(vmem_limit_bytes=limit * 2**20),
        cost_estimate=pl.CostEstimate(
            flops=flops, bytes_accessed=8 * 2**20, transcendentals=0
        ),
    )(*args)


def swap_cores(value):
    return lax.ppermute(value, "py", [(0, 1), (1, 0)])


def swap_slabs(first, second, first_face, second_face, low_half):
    count = lax.axis_size("px")
    near = [(i, i ^ 1) for i in range(count)]
    far = [(i, i + 1 if i % 2 else i - 1) for i in range(1, count - 1)]

    def slab(i):
        return jnp.stack(
            [
                jnp.concatenate([first[i], first_face[i]], axis=0),
                jnp.concatenate([second[i], second_face[i]], axis=0),
            ]
        )

    low, high = slab(0), slab(3)
    got_far = lax.ppermute(jnp.where(low_half, low, high), "px", far)
    got_near = lax.ppermute(jnp.where(low_half, high, low), "px", near)
    return got_near, got_far


def hop(parts, stage):
    return [
        lax.ppermute(part, ALL, hop_pairs(stage, distance))
        for part, distance in zip(parts, (1, 3, 2))
    ]


def reduce_tiles(own, got, core):
    total = own.astype(F32)
    for part in got:
        total = total + part.astype(F32)
    got = hop([total[4 * d : 4 * d + 4].astype(BF) for d in (1, 3, 2)], 1)
    total = total[0:4]
    for part in got:
        total = total + part.astype(F32)
    got = hop([total[d] for d in (1, 3, 2)], 2)
    total = total[0] + got[0] + got[1] + got[2]
    keep = jnp.where(core == 0, total[:16], total[16:])
    give = jnp.where(core == 0, total[16:], total[:16])
    other = swap_cores(give)
    first = jnp.where(core == 0, keep, other)[:, :864]
    second = jnp.where(core == 0, other, keep)[:, :864]
    return first.T, second.T


def body(fields, cotangent, first_weight, second_weight):
    shape = jax.ShapeDtypeStruct
    core = lax.axis_index("py")
    dp, px = lax.axis_index("dp"), lax.axis_index("px")
    zero = core == 0
    two = jnp.int32(2)
    place = jnp.stack(
        [core, lax.div(px, two), lax.div(dp, two), lax.rem(dp, two) * 2 + lax.rem(px, two)]
    )
    field, cot = fields[0], cotangent[0]
    grid, half = shape((4, 8, 32, 256), BF), shape((2, 8, 32, 256), BF)

    part = shape((2, 256, 256), F32)
    low_half = lax.rem(px, two) == 0
    own_scratch = [pltpu.VMEM((4, 10, 32, 768), BF)] * 2 + [pltpu.VMEM((1024, 256), F32)] * 2
    edge_scratch = [pltpu.VMEM((2, 10, 32, 768), BF)] * 2
    weights = (first_weight, second_weight)
    flops = 2 * 2 * 1024 * 6912 * 256
    (sent1,) = call(
        pack_kernel,
        "pack",
        0,
        (place, cot, field),
        [shape((4, 9, 32, 256), BF)],
        [pltpu.SemaphoreType.DMA((2,))],
        56,
        (1, 2),
    )
    other1 = swap_cores(sent1)
    near1, far1 = swap_slabs(
        cot,
        field,
        jnp.where(zero, other1[:, 8:9], other1[:, 7:8]),
        jnp.where(zero, other1[:, 0:1], other1[:, 8:9]),
        low_half,
    )
    inner = call(
        inner_kernel,
        "inner",
        flops * 5 // 6,
        (place, cot, field, other1, *weights),
        [half, half, part, part, shape((6912, 256), BF), shape((6912, 256), BF)],
        own_scratch + [pltpu.SemaphoreType.DMA((2,))],
        42,
        (4, 5),
    )
    inner, weights = inner[:4], inner[4:]
    hidden, pre_grad, sent2 = call(
        outer_kernel,
        "outer",
        flops // 6,
        (place, near1, far1, *inner, *weights),
        [grid, grid, shape((4, 9, 32, 256), BF)],
        edge_scratch,
        24,
    )
    edges = swap_cores(
        jnp.where(
            zero,
            jnp.stack([near1[0, 0:8], far1[0, 0:8]]),
            jnp.stack([near1[1, 0:8], far1[1, 0:8]]),
        )
    )
    other2 = swap_cores(sent2)
    near2, far2 = swap_slabs(
        hidden,
        pre_grad,
        jnp.where(zero, other2[:, 8:9], other2[:, 7:8]),
        jnp.where(zero, other2[:, 0:1], other2[:, 8:9]),
        low_half,
    )
    own, send1, send2, send3 = call(
        weight_kernel,
        "weight_terms",
        flops,
        (place, cot, field, near1, far1, other1, edges, hidden, pre_grad, other2),
        [shape((16, 32, LANES), BF)] * 4,
        [
            pltpu.VMEM((6, 18, 32, 768), BF),
            pltpu.VMEM((256, 2048), BF),
            pltpu.VMEM((2048, 256), BF),
            pltpu.VMEM((256, 7040), BF),
            pltpu.VMEM((8, 256, LANES), BF),
        ],
        34,
    )
    send1, near2, far2 = lax.optimization_barrier((send1, near2, far2))
    got = hop((send1, send3, send2), 0)
    hidden, pre_grad, other2, own = lax.optimization_barrier((hidden, pre_grad, other2, own))
    last = call(
        last_inner_kernel,
        "outputs_inner",
        flops * 5 // 6,
        (place, hidden, pre_grad, other2, field, cot, *weights),
        [half, half, part, part],
        own_scratch,
        26,
    )
    output, field_grad = call(
        last_outer_kernel,
        "outputs_outer",
        flops // 6,
        (place, near2, far2, *last, field, cot, *weights),
        [grid, grid],
        edge_scratch,
        24,
    )
    own, output, field_grad = lax.optimization_barrier((own, output, field_grad))
    first_grad, second_grad = reduce_tiles(own, got, core)
    return output[None], field_grad[None], first_grad, second_grad


def solution(mesh):
    placed = P("dp", "px", "py", None, None)
    return jax.shard_map(
        body,
        mesh=mesh,
        in_specs=(placed, placed, P(), P()),
        out_specs=(placed, placed, P("dp", ("px", "py")), P("dp", ("px", "py"))),
        check_vma=False,
    )
```

```python
import jax
import jax.numpy as jnp
from jax import lax
from jax.experimental import pallas as pl
from jax.experimental.pallas import tpu as pltpu
from jax.sharding import PartitionSpec as P

BF = jnp.bfloat16
F32 = jnp.float32
ALL = ("dp", "px", "py")
X, Y, Z = 0, 1, 2
ORDER = ((X, Z), (Z, X))
LANES = 896


def device(x, y, z, core):
    x, y, z = x % 4, y % 4, z % 4
    return (y * 2 + z // 2) * 16 + (x * 2 + z % 2) * 2 + core


LAST_GROUPS = [
    [device(x, y, z, core) for y in range(4) for core in range(2)]
    for x in range(4)
    for z in range(4)
]


def hop_pairs(stage, distance):
    pairs = []
    for core in range(2):
        step = [0, 0, 0]
        step[ORDER[core][stage]] = distance
        for x in range(4):
            for y in range(4):
                for z in range(4):
                    pairs.append(
                        (
                            device(x, y, z, core),
                            device(x + step[0], y + step[1], z + step[2], core),
                        )
                    )
    return pairs


def shifted(block):
    wide = block.astype(F32)
    place = lax.broadcasted_iota(jnp.int32, wide.shape, 1)
    low = jnp.where(place == 0, 0.0, pltpu.roll(wide, 1, 1)).astype(BF)
    high = jnp.where(place == 31, 0.0, pltpu.roll(wide, 31, 1)).astype(BF)
    return low, high


def put(stack, row, start, block, flip):
    low, high = shifted(block)
    if flip:
        low, high = high, low
    rows = pl.ds(start, block.shape[0])
    stack[row, rows, :, 0:256] = low
    stack[row, rows, :, 256:512] = block
    stack[row, rows, :, 512:768] = high


def put_own(stack, slab, start, own, flip):
    def step(i, _):
        put(stack, i + slab, start, own[i], flip)
        return 0

    lax.fori_loop(0, own.shape[0], step, 0)


def put_faces(stack, core, slab, count, other, at_first, at_second, flip):
    at = jnp.where(core == 0, at_first, at_second)
    row = jnp.where(core == 0, 9, 0)

    def step(i, _):
        put(stack, i + slab, row, other[i, pl.ds(at, 1)], flip)
        stack[i + slab, pl.ds(9 - row, 1)] = jnp.zeros((1, 32, 768), BF)
        return 0

    lax.fori_loop(0, count, step, 0)


def put_halo(stack, core, slab, halo, which, flip):
    row = jnp.where(core == 0, 9, 0)
    put(stack, slab, 1, halo[which, 0:8], flip)
    put(stack, slab, row, halo[which, 8:9], flip)
    stack[slab, pl.ds(9 - row, 1)] = jnp.zeros((1, 32, 768), BF)


def term_of(rows, weight, k, back):
    if not back:
        return jnp.dot(rows, weight[k * 768 : (k + 1) * 768], preferred_element_type=F32)
    term = None
    for c in range(3):
        part = lax.dot_general(
            rows[:, c * 256 : (c + 1) * 256],
            weight[(k * 3 + c) * 256 : (k * 3 + c + 1) * 256],
            (((1,), (1,)), ((), ())),
            preferred_element_type=F32,
        )
        term = part if term is None else term + part
    return term


def conv_own(total, stack, weight, back):
    for a in (1, 0, 2):
        step = 1 - a if back else a - 1
        count = 4 - abs(step)
        to = max(0, -step)
        for b in range(3):
            at = 2 - b if back else b
            rows = stack[to + step : to + step + count, at : at + 8].reshape(count * 256, 768)
            term = term_of(rows, weight, a * 3 + b, back)
            span = slice(to * 256, (to + count) * 256)
            if a == 1 and b == 0:
                total[span] = term
            else:
                total[span] += term


def conv_edges(part, stack, weight, back):
    sums = []
    for side in range(2):
        a = 2 * side if not back else 2 - 2 * side
        total = part[side]
        for b in range(3):
            at = 2 - b if back else b
            rows = stack[side, at : at + 8].reshape(256, 768)
            total = total + term_of(rows, weight, a * 3 + b, back)
        sums.append(total)
    return sums


def gelu_and_slope(v):
    scale = 0.7978845608028654
    square = v * v
    t = jnp.tanh(scale * (v + 0.044715 * (square * v)))
    half = 0.5 * (1.0 + t)
    slope = half + 0.5 * v * (1.0 - t * t) * (scale * (1.0 + 3.0 * 0.044715 * square))
    return v * half, slope


def near_side(place):
    return 1 - lax.rem(place[3], 2)


def pack_kernel(place, cot, field, send, arrived):
    core = place[0]

    def pack(whole, row):
        copies = [
            pltpu.make_async_copy(whole, send.at[:, 0:8], arrived.at[0]),
            pltpu.make_async_copy(row, send.at[:, 8:9], arrived.at[1]),
        ]
        for copy in copies:
            copy.start()
        for copy in copies:
            copy.wait()

    @pl.when(core == 0)
    def _():
        pack(cot, field.at[:, 7:8])

    @pl.when(core == 1)
    def _():
        pack(field, cot.at[:, 0:1])


def inner_kernel(
    place, cot, field, other, first_hbm, second_hbm, hidden, pre_grad, part_pre, part_grad,
    first_w, second_w, stack, back, pre, grad, arrived,
):
    core = place[0]
    copies = [
        pltpu.make_async_copy(first_hbm, first_w, arrived.at[0]),
        pltpu.make_async_copy(second_hbm, second_w, arrived.at[1]),
    ]
    for copy in copies:
        copy.start()
    put_own(stack, 0, 1, field, False)
    put_faces(stack, core, 0, 4, other, 0, 8, False)
    put_own(back, 0, 1, cot, True)
    put_faces(back, core, 0, 4, other, 8, 7, True)
    for copy in copies:
        copy.wait()
    conv_own(pre, stack, first_w, False)
    conv_own(grad, back, second_w, True)
    for i in range(2):
        rows = slice((i + 1) * 256, (i + 2) * 256)
        value, slope = gelu_and_slope(pre[rows])
        hidden[i] = value.astype(BF).reshape(8, 32, 256)
        pre_grad[i] = (grad[rows] * slope).astype(BF).reshape(8, 32, 256)
        rows = slice(i * 768, i * 768 + 256)
        part_pre[i] = pre[rows]
        part_grad[i] = grad[rows]


def outer_kernel(
    place, near, far, inner_hidden, inner_grad, part_pre, part_grad, first_w, second_w,
    hidden, pre_grad, send, stack, back,
):
    core = place[0]
    side = near_side(place)
    put_halo(stack, core, side, near, 1, False)
    put_halo(stack, core, 1 - side, far, 1, False)
    put_halo(back, core, side, near, 0, True)
    put_halo(back, core, 1 - side, far, 0, True)
    pre = conv_edges(part_pre, stack, first_w, False)
    grad = conv_edges(part_grad, back, second_w, True)
    for i in range(2):
        value, slope = gelu_and_slope(pre[i])
        hidden[3 * i] = value.astype(BF).reshape(8, 32, 256)
        pre_grad[3 * i] = (grad[i] * slope).astype(BF).reshape(8, 32, 256)
        hidden[1 + i] = inner_hidden[i]
        pre_grad[1 + i] = inner_grad[i]

    @pl.when(core == 0)
    def _():
        send[:, 0:8] = hidden[...]
        send[:, 8:9] = pre_grad[:, 7:8]

    @pl.when(core == 1)
    def _():
        send[:, 0:8] = pre_grad[...]
        send[:, 8:9] = hidden[:, 0:1]


def last_inner_kernel(
    place, hid, pre_grad, other, field, cot, first_w, second_w,
    out, field_grad, part_out, part_grad, stack, back, total, grad,
):
    core = place[0]
    put_own(stack, 0, 1, hid, False)
    put_faces(stack, core, 0, 4, other, 8, 7, False)
    put_own(back, 0, 1, pre_grad, True)
    put_faces(back, core, 0, 4, other, 0, 8, True)
    conv_own(total, stack, second_w, False)
    conv_own(grad, back, first_w, True)
    for i in range(2):
        rows = slice((i + 1) * 256, (i + 2) * 256)
        one = field[i + 1].astype(F32).reshape(256, 256) + total[rows]
        out[i] = one.astype(BF).reshape(8, 32, 256)
        two = cot[i + 1].astype(F32).reshape(256, 256) + grad[rows]
        field_grad[i] = two.astype(BF).reshape(8, 32, 256)
        rows = slice(i * 768, i * 768 + 256)
        part_out[i] = total[rows]
        part_grad[i] = grad[rows]


def last_outer_kernel(
    place, near, far, inner_out, inner_grad, part_out, part_grad, field, cot, first_w, second_w,
    out, field_grad, stack, back,
):
    core = place[0]
    side = near_side(place)
    put_halo(stack, core, side, near, 0, False)
    put_halo(stack, core, 1 - side, far, 0, False)
    put_halo(back, core, side, near, 1, True)
    put_halo(back, core, 1 - side, far, 1, True)
    total = conv_edges(part_out, stack, second_w, False)
    grad = conv_edges(part_grad, back, first_w, True)
    for i in range(2):
        one = field[3 * i].astype(F32).reshape(256, 256) + total[i]
        out[3 * i] = one.astype(BF).reshape(8, 32, 256)
        two = cot[3 * i].astype(F32).reshape(256, 256) + grad[i]
        field_grad[3 * i] = two.astype(BF).reshape(8, 32, 256)
        out[1 + i] = inner_out[i]
        field_grad[1 + i] = inner_grad[i]


def weight_kernel(
    place, cot, field, near1, far1, other1, edges, hid, pre_grad, other2,
    own, send1, send2, send3, stack, turned, local, flat, tiles,
):
    core = place[0]

    def fill(value, which, half, flip):
        mine, others = 1 + 8 * half, 9 - 8 * half
        near = 5 * near_side(place)
        put_own(stack, 1, mine, value, flip)
        put(stack, near, mine, near1[which, 0:8], flip)
        put(stack, 5 - near, mine, far1[which, 0:8], flip)
        put(stack, near, others, edges[0], flip)
        put(stack, 5 - near, others, edges[1], flip)

        def step(i, _):
            put(stack, i + 1, others, other1[i, 0:8], flip)
            return 0

        lax.fori_loop(0, 4, step, 0)
        for i in range(6):
            stack[i, 0:1] = jnp.zeros((1, 32, 768), BF)
            stack[i, 17:18] = jnp.zeros((1, 32, 768), BF)

    flat[:, 6912:7040] = jnp.zeros((256, 128), BF)

    @pl.when(core == 0)
    def _():
        fill(field, 1, 0, False)
        for i in range(4):
            turned[:, i * 512 : i * 512 + 256] = pre_grad[i].reshape(256, 256).T
            turned[:, i * 512 + 256 : i * 512 + 512] = other2[i, 0:8].reshape(256, 256).T

        def block(k, _):
            a, b = k // 3, k % 3
            rows = stack[pl.ds(a, 4), pl.ds(b, 16)].reshape(2048, 768)
            term = jnp.dot(turned[...], rows, preferred_element_type=F32)
            flat[:, pl.ds(pl.multiple_of(k * 768, 768), 768)] = (term * 0.125).astype(BF)
            return 0

        lax.fori_loop(0, 9, block, 0, unroll=True)

    @pl.when(core == 1)
    def _():
        fill(cot, 0, 1, True)
        for i in range(4):
            local[i * 512 : i * 512 + 256] = other2[i, 0:8].reshape(256, 256)
            local[i * 512 + 256 : i * 512 + 512] = hid[i].reshape(256, 256)

        def block(k, _):
            a, b = 2 - k // 3, 2 - k % 3
            rows = stack[pl.ds(a, 4), pl.ds(b, 16)].reshape(2048, 768)
            term = lax.dot_general(
                rows, local[...], (((0,), (0,)), ((), ())), preferred_element_type=F32
            )
            term = (term * 0.125).astype(BF)
            for c in range(3):
                lanes = pl.ds(pl.multiple_of((k * 3 + c) * 256, 256), 256)
                flat[:, lanes] = term[c * 256 : (c + 1) * 256]
            return 0

        lax.fori_loop(0, 9, block, 0, unroll=True)

    for k in range(8):
        tiles[k] = flat[:, k * 864 : k * 864 + LANES]
    x, z = place[1], place[3]
    zero = core == 0
    for first, ref in enumerate((own, send1, send2, send3)):

        def pick(i, _):
            second, third = i // 4, i % 4
            to_x = lax.rem(x + jnp.where(zero, first, second), 4)
            to_z = lax.rem(z + jnp.where(zero, second, first), 4)
            to_dp = third * 2 + to_z // 2
            to_px = to_x * 2 + lax.rem(to_z, 2)
            ref[i] = tiles[to_dp, pl.ds(pl.multiple_of(to_px * 32, 32), 32), :]
            return 0

        lax.fori_loop(0, 16, pick, 0, unroll=8)


def call(kernel, name, flops, args, outs, scratch, limit, far=()):
    whole = pl.BlockSpec(memory_space=pltpu.VMEM)
    return pl.pallas_call(
        kernel,
        name=name,
        out_shape=outs,
        in_specs=[pl.BlockSpec(memory_space=pltpu.SMEM)]
        + [
            pl.BlockSpec(memory_space=pltpu.HBM) if i in far else whole
            for i in range(1, len(args))
        ],
        out_specs=[whole] * len(outs),
        scratch_shapes=scratch,
        compiler_params=pltpu.CompilerParams(vmem_limit_bytes=limit * 2**20),
        cost_estimate=pl.CostEstimate(
            flops=flops, bytes_accessed=8 * 2**20, transcendentals=0
        ),
    )(*args)


def swap_cores(value):
    return lax.ppermute(value, "py", [(0, 1), (1, 0)])


def swap_slabs(first, second, first_face, second_face, low_half):
    count = lax.axis_size("px")
    near = [(i, i ^ 1) for i in range(count)]
    far = [(i, i + 1 if i % 2 else i - 1) for i in range(1, count - 1)]

    def slab(i):
        return jnp.stack(
            [
                jnp.concatenate([first[i], first_face[i]], axis=0),
                jnp.concatenate([second[i], second_face[i]], axis=0),
            ]
        )

    low, high = slab(0), slab(3)
    got_far = lax.ppermute(jnp.where(low_half, low, high), "px", far)
    got_near = lax.ppermute(jnp.where(low_half, high, low), "px", near)
    return got_near, got_far


def hop(parts, stage):
    return [
        lax.ppermute(part, ALL, hop_pairs(stage, distance))
        for part, distance in zip(parts, (1, 3, 2))
    ]


def reduce_tiles(own, got):
    total = own.astype(F32)
    for part in got:
        total = total + part.astype(F32)
    got = hop([total[4 * d : 4 * d + 4].astype(BF) for d in (1, 3, 2)], 1)
    total = total[0:4]
    for part in got:
        total = total + part.astype(F32)
    parts = lax.all_to_all(
        total.reshape(8, 16, LANES), ALL, 0, 0, tiled=True, axis_index_groups=LAST_GROUPS
    )
    sums = parts.reshape(4, 2, 16, LANES).sum(axis=0)
    return sums[0, :, :864].T, sums[1, :, :864].T


def body(fields, cotangent, first_weight, second_weight):
    shape = jax.ShapeDtypeStruct
    core = lax.axis_index("py")
    dp, px = lax.axis_index("dp"), lax.axis_index("px")
    zero = core == 0
    two = jnp.int32(2)
    place = jnp.stack(
        [core, lax.div(px, two), lax.div(dp, two), lax.rem(dp, two) * 2 + lax.rem(px, two)]
    )
    field, cot = fields[0], cotangent[0]
    grid, half = shape((4, 8, 32, 256), BF), shape((2, 8, 32, 256), BF)

    part = shape((2, 256, 256), F32)
    low_half = lax.rem(px, two) == 0
    own_scratch = [pltpu.VMEM((4, 10, 32, 768), BF)] * 2 + [pltpu.VMEM((1024, 256), F32)] * 2
    edge_scratch = [pltpu.VMEM((2, 10, 32, 768), BF)] * 2
    weights = (first_weight, second_weight)
    flops = 2 * 2 * 1024 * 6912 * 256
    (sent1,) = call(
        pack_kernel,
        "pack",
        0,
        (core.astype(jnp.int32).reshape(1), cot, field),
        [shape((4, 9, 32, 256), BF)],
        [pltpu.SemaphoreType.DMA((2,))],
        40,
        (1, 2),
    )
    other1 = swap_cores(sent1)
    near1, far1 = swap_slabs(
        cot,
        field,
        jnp.where(zero, other1[:, 8:9], other1[:, 7:8]),
        jnp.where(zero, other1[:, 0:1], other1[:, 8:9]),
        low_half,
    )
    inner = call(
        inner_kernel,
        "inner",
        flops * 5 // 6,
        (place, cot, field, other1, *weights),
        [half, half, part, part, shape((6912, 256), BF), shape((6912, 256), BF)],
        own_scratch + [pltpu.SemaphoreType.DMA((2,))],
        38,
        (4, 5),
    )
    inner, weights = inner[:4], inner[4:]
    hidden, pre_grad, sent2 = call(
        outer_kernel,
        "outer",
        flops // 6,
        (place, near1, far1, *inner, *weights),
        [grid, grid, shape((4, 9, 32, 256), BF)],
        edge_scratch,
        24,
    )
    edges = swap_cores(
        jnp.where(
            zero,
            jnp.stack([near1[0, 0:8], far1[0, 0:8]]),
            jnp.stack([near1[1, 0:8], far1[1, 0:8]]),
        )
    )
    other2 = swap_cores(sent2)
    near2, far2 = swap_slabs(
        hidden,
        pre_grad,
        jnp.where(zero, other2[:, 8:9], other2[:, 7:8]),
        jnp.where(zero, other2[:, 0:1], other2[:, 8:9]),
        low_half,
    )
    own, send1, send2, send3 = call(
        weight_kernel,
        "weight_terms",
        flops,
        (place, cot, field, near1, far1, other1, edges, hidden, pre_grad, other2),
        [shape((16, 32, LANES), BF)] * 4,
        [
            pltpu.VMEM((6, 18, 32, 768), BF),
            pltpu.VMEM((256, 2048), BF),
            pltpu.VMEM((2048, 256), BF),
            pltpu.VMEM((256, 7040), BF),
            pltpu.VMEM((8, 256, LANES), BF),
        ],
        34,
    )
    send1, near2, far2 = lax.optimization_barrier((send1, near2, far2))
    got = hop((send1, send3, send2), 0)
    hidden, pre_grad, other2, own = lax.optimization_barrier((hidden, pre_grad, other2, own))
    last = call(
        last_inner_kernel,
        "outputs_inner",
        flops * 5 // 6,
        (place, hidden, pre_grad, other2, field, cot, *weights),
        [half, half, part, part],
        own_scratch,
        26,
    )
    output, field_grad = call(
        last_outer_kernel,
        "outputs_outer",
        flops // 6,
        (place, near2, far2, *last, field, cot, *weights),
        [grid, grid],
        edge_scratch,
        24,
    )
    own, output, field_grad = lax.optimization_barrier((own, output, field_grad))
    first_grad, second_grad = reduce_tiles(own, got)
    return output[None], field_grad[None], first_grad, second_grad


def solution(mesh):
    placed = P("dp", "px", "py", None, None)
    return jax.shard_map(
        body,
        mesh=mesh,
        in_specs=(placed, placed, P(), P()),
        out_specs=(placed, placed, P("dp", ("px", "py")), P("dp", ("px", "py"))),
        check_vma=False,
    )
```

```python
import jax
import jax.numpy as jnp
from jax import lax
from jax.experimental import pallas as pl
from jax.experimental.pallas import tpu as pltpu
from jax.sharding import PartitionSpec as P

BF = jnp.bfloat16
F32 = jnp.float32
ALL = ("dp", "px", "py")
X, Y, Z = 0, 1, 2
ORDER = ((X, Y, Z), (Y, Z, X))
LANES = 896


def device(x, y, z, core):
    x, y, z = x % 4, y % 4, z % 4
    return (y * 2 + z // 2) * 16 + (x * 2 + z % 2) * 2 + core


def hop_pairs(stage, distance):
    pairs = []
    for core in range(2):
        step = [0, 0, 0]
        step[ORDER[core][stage]] = distance
        for x in range(4):
            for y in range(4):
                for z in range(4):
                    pairs.append(
                        (
                            device(x, y, z, core),
                            device(x + step[0], y + step[1], z + step[2], core),
                        )
                    )
    return pairs


def shifted(block):
    wide = block.astype(F32)
    place = lax.broadcasted_iota(jnp.int32, wide.shape, 1)
    low = jnp.where(place == 0, 0.0, pltpu.roll(wide, 1, 1)).astype(BF)
    high = jnp.where(place == 31, 0.0, pltpu.roll(wide, 31, 1)).astype(BF)
    return low, high


def put(stack, row, start, block, flip):
    low, high = shifted(block)
    if flip:
        low, high = high, low
    rows = pl.ds(start, block.shape[0])
    stack[row, rows, :, 0:256] = low
    stack[row, rows, :, 256:512] = block
    stack[row, rows, :, 512:768] = high


def put_own(stack, slab, start, own, flip):
    def step(i, _):
        put(stack, i + slab, start, own[i], flip)
        return 0

    lax.fori_loop(0, own.shape[0], step, 0)


def put_faces(stack, core, slab, count, other, at_first, at_second, flip):
    at = jnp.where(core == 0, at_first, at_second)
    row = jnp.where(core == 0, 9, 0)

    def step(i, _):
        put(stack, i + slab, row, other[i, pl.ds(at, 1)], flip)
        stack[i + slab, pl.ds(9 - row, 1)] = jnp.zeros((1, 32, 768), BF)
        return 0

    lax.fori_loop(0, count, step, 0)


def put_halo(stack, core, slab, halo, which, flip):
    row = jnp.where(core == 0, 9, 0)
    put(stack, slab, 1, halo[which, 0:8], flip)
    put(stack, slab, row, halo[which, 8:9], flip)
    stack[slab, pl.ds(9 - row, 1)] = jnp.zeros((1, 32, 768), BF)


def term_of(rows, weight, k, back):
    if not back:
        return jnp.dot(rows, weight[k * 768 : (k + 1) * 768], preferred_element_type=F32)
    term = None
    for c in range(3):
        part = lax.dot_general(
            rows[:, c * 256 : (c + 1) * 256],
            weight[(k * 3 + c) * 256 : (k * 3 + c + 1) * 256],
            (((1,), (1,)), ((), ())),
            preferred_element_type=F32,
        )
        term = part if term is None else term + part
    return term


def conv_own(total, stack, weight, back):
    for a in (1, 0, 2):
        step = 1 - a if back else a - 1
        count = 4 - abs(step)
        to = max(0, -step)
        for b in range(3):
            at = 2 - b if back else b
            rows = stack[to + step : to + step + count, at : at + 8].reshape(count * 256, 768)
            term = term_of(rows, weight, a * 3 + b, back)
            span = slice(to * 256, (to + count) * 256)
            if a == 1 and b == 0:
                total[span] = term
            else:
                total[span] += term


def conv_edges(part, stack, weight, back):
    sums = []
    for side in range(2):
        a = 2 * side if not back else 2 - 2 * side
        total = part[side]
        for b in range(3):
            at = 2 - b if back else b
            rows = stack[side, at : at + 8].reshape(256, 768)
            total = total + term_of(rows, weight, a * 3 + b, back)
        sums.append(total)
    return sums


def gelu_and_slope(v):
    scale = 0.7978845608028654
    square = v * v
    t = jnp.tanh(scale * (v + 0.044715 * (square * v)))
    half = 0.5 * (1.0 + t)
    slope = half + 0.5 * v * (1.0 - t * t) * (scale * (1.0 + 3.0 * 0.044715 * square))
    return v * half, slope


def near_side(place):
    return 1 - lax.rem(place[3], 2)


def pack_kernel(place, cot, field, send, arrived):
    core = place[0]

    def pack(whole, row):
        copies = [
            pltpu.make_async_copy(whole, send.at[:, 0:8], arrived.at[0]),
            pltpu.make_async_copy(row, send.at[:, 8:9], arrived.at[1]),
        ]
        for copy in copies:
            copy.start()
        for copy in copies:
            copy.wait()

    @pl.when(core == 0)
    def _():
        pack(cot, field.at[:, 7:8])

    @pl.when(core == 1)
    def _():
        pack(field, cot.at[:, 0:1])


def inner_kernel(
    place, cot, field, other, first_hbm, second_hbm, hidden, pre_grad, part_pre, part_grad,
    first_w, second_w, stack, back, pre, grad, arrived,
):
    core = place[0]
    copies = [
        pltpu.make_async_copy(first_hbm, first_w, arrived.at[0]),
        pltpu.make_async_copy(second_hbm, second_w, arrived.at[1]),
    ]
    for copy in copies:
        copy.start()
    put_own(stack, 0, 1, field, False)
    put_faces(stack, core, 0, 4, other, 0, 8, False)
    put_own(back, 0, 1, cot, True)
    put_faces(back, core, 0, 4, other, 8, 7, True)
    for copy in copies:
        copy.wait()
    conv_own(pre, stack, first_w, False)
    conv_own(grad, back, second_w, True)
    for i in range(2):
        rows = slice((i + 1) * 256, (i + 2) * 256)
        value, slope = gelu_and_slope(pre[rows])
        hidden[i] = value.astype(BF).reshape(8, 32, 256)
        pre_grad[i] = (grad[rows] * slope).astype(BF).reshape(8, 32, 256)
        rows = slice(i * 768, i * 768 + 256)
        part_pre[i] = pre[rows]
        part_grad[i] = grad[rows]


def outer_kernel(
    place, near, far, inner_hidden, inner_grad, part_pre, part_grad, first_w, second_w,
    hidden, pre_grad, send, stack, back,
):
    core = place[0]
    side = near_side(place)
    put_halo(stack, core, side, near, 1, False)
    put_halo(stack, core, 1 - side, far, 1, False)
    put_halo(back, core, side, near, 0, True)
    put_halo(back, core, 1 - side, far, 0, True)
    pre = conv_edges(part_pre, stack, first_w, False)
    grad = conv_edges(part_grad, back, second_w, True)
    for i in range(2):
        value, slope = gelu_and_slope(pre[i])
        hidden[3 * i] = value.astype(BF).reshape(8, 32, 256)
        pre_grad[3 * i] = (grad[i] * slope).astype(BF).reshape(8, 32, 256)
        hidden[1 + i] = inner_hidden[i]
        pre_grad[1 + i] = inner_grad[i]

    @pl.when(core == 0)
    def _():
        send[:, 0:8] = hidden[...]
        send[:, 8:9] = pre_grad[:, 7:8]

    @pl.when(core == 1)
    def _():
        send[:, 0:8] = pre_grad[...]
        send[:, 8:9] = hidden[:, 0:1]


def last_inner_kernel(
    place, hid, pre_grad, other, field, cot, first_w, second_w,
    out, field_grad, part_out, part_grad, stack, back, total, grad,
):
    core = place[0]
    put_own(stack, 0, 1, hid, False)
    put_faces(stack, core, 0, 4, other, 8, 7, False)
    put_own(back, 0, 1, pre_grad, True)
    put_faces(back, core, 0, 4, other, 0, 8, True)
    conv_own(total, stack, second_w, False)
    conv_own(grad, back, first_w, True)
    for i in range(2):
        rows = slice((i + 1) * 256, (i + 2) * 256)
        one = field[i + 1].astype(F32).reshape(256, 256) + total[rows]
        out[i] = one.astype(BF).reshape(8, 32, 256)
        two = cot[i + 1].astype(F32).reshape(256, 256) + grad[rows]
        field_grad[i] = two.astype(BF).reshape(8, 32, 256)
        rows = slice(i * 768, i * 768 + 256)
        part_out[i] = total[rows]
        part_grad[i] = grad[rows]


def last_outer_kernel(
    place, near, far, inner_out, inner_grad, part_out, part_grad, field, cot, first_w, second_w,
    out, field_grad, stack, back,
):
    core = place[0]
    side = near_side(place)
    put_halo(stack, core, side, near, 0, False)
    put_halo(stack, core, 1 - side, far, 0, False)
    put_halo(back, core, side, near, 1, True)
    put_halo(back, core, 1 - side, far, 1, True)
    total = conv_edges(part_out, stack, second_w, False)
    grad = conv_edges(part_grad, back, first_w, True)
    for i in range(2):
        one = field[3 * i].astype(F32).reshape(256, 256) + total[i]
        out[3 * i] = one.astype(BF).reshape(8, 32, 256)
        two = cot[3 * i].astype(F32).reshape(256, 256) + grad[i]
        field_grad[3 * i] = two.astype(BF).reshape(8, 32, 256)
        out[1 + i] = inner_out[i]
        field_grad[1 + i] = inner_grad[i]


def chip_kernel(place, cot, field, other, chip):
    core = place[0]

    def fill(value, half, flip):
        put_own(chip, 0, 1 + 8 * half, value, flip)

        def step(i, _):
            put(chip, i, 9 - 8 * half, other[i, 0:8], flip)
            chip[i, 0:1] = jnp.zeros((1, 32, 768), BF)
            chip[i, 17:18] = jnp.zeros((1, 32, 768), BF)
            return 0

        lax.fori_loop(0, 4, step, 0)

    @pl.when(core == 0)
    def _():
        fill(field, 0, False)

    @pl.when(core == 1)
    def _():
        fill(cot, 1, True)


def weight_kernel(
    place, chip, near1, far1, edges, hid, pre_grad, other2,
    own, send1, send2, send3, sides, turned, local, flat, tiles,
):
    core = place[0]
    near = near_side(place)

    def fill(which, half, flip):
        mine, others = 1 + 8 * half, 9 - 8 * half
        put(sides, near, mine, near1[which, 0:8], flip)
        put(sides, 1 - near, mine, far1[which, 0:8], flip)
        put(sides, near, others, edges[0], flip)
        put(sides, 1 - near, others, edges[1], flip)
        for i in range(2):
            sides[i, 0:1] = jnp.zeros((1, 32, 768), BF)
            sides[i, 17:18] = jnp.zeros((1, 32, 768), BF)

    def windows(a, b):
        rows = slice(b, b + 16)
        if a == 1:
            return [(0, chip[0:4, rows].reshape(2048, 768))]
        if a == 0:
            return [
                (0, sides[0, rows].reshape(512, 768)),
                (512, chip[0:3, rows].reshape(1536, 768)),
            ]
        return [
            (0, chip[1:4, rows].reshape(1536, 768)),
            (1536, sides[1, rows].reshape(512, 768)),
        ]

    flat[:, 6912:7040] = jnp.zeros((256, 128), BF)

    @pl.when(core == 0)
    def _():
        fill(1, 0, False)
        for i in range(4):
            turned[:, i * 512 : i * 512 + 256] = pre_grad[i].reshape(256, 256).T
            turned[:, i * 512 + 256 : i * 512 + 512] = other2[i, 0:8].reshape(256, 256).T
        for k in range(9):
            term = None
            for at, rows in windows(k // 3, k % 3):
                part = jnp.dot(
                    turned[:, at : at + rows.shape[0]], rows, preferred_element_type=F32
                )
                term = part if term is None else term + part
            flat[:, k * 768 : (k + 1) * 768] = (term * 0.125).astype(BF)

    @pl.when(core == 1)
    def _():
        fill(0, 1, True)
        for i in range(4):
            local[i * 512 : i * 512 + 256] = other2[i, 0:8].reshape(256, 256)
            local[i * 512 + 256 : i * 512 + 512] = hid[i].reshape(256, 256)
        for k in range(9):
            term = None
            for at, rows in windows(2 - k // 3, 2 - k % 3):
                part = lax.dot_general(
                    rows,
                    local[at : at + rows.shape[0]],
                    (((0,), (0,)), ((), ())),
                    preferred_element_type=F32,
                )
                term = part if term is None else term + part
            term = (term * 0.125).astype(BF)
            for c in range(3):
                lanes = slice((k * 3 + c) * 256, (k * 3 + c + 1) * 256)
                flat[:, lanes] = term[c * 256 : (c + 1) * 256]

    for k in range(8):
        tiles[k] = flat[:, k * 864 : k * 864 + LANES]
    x, y, z = place[1], place[2], place[3]
    zero = core == 0
    for first, ref in enumerate((own, send1, send2, send3)):

        def pick(i, _):
            second, third = i // 4, i % 4
            to_x = lax.rem(x + jnp.where(zero, first, third), 4)
            to_y = lax.rem(y + jnp.where(zero, second, first), 4)
            to_z = lax.rem(z + jnp.where(zero, third, second), 4)
            to_dp = to_y * 2 + to_z // 2
            to_px = to_x * 2 + lax.rem(to_z, 2)
            ref[i] = tiles[to_dp, pl.ds(pl.multiple_of(to_px * 32, 32), 32), :]
            return 0

        lax.fori_loop(0, 16, pick, 0, unroll=True)


def call(kernel, name, flops, args, outs, scratch, limit, far=()):
    whole = pl.BlockSpec(memory_space=pltpu.VMEM)
    return pl.pallas_call(
        kernel,
        name=name,
        out_shape=outs,
        in_specs=[pl.BlockSpec(memory_space=pltpu.SMEM)]
        + [
            pl.BlockSpec(memory_space=pltpu.HBM) if i in far else whole
            for i in range(1, len(args))
        ],
        out_specs=[whole] * len(outs),
        scratch_shapes=scratch,
        compiler_params=pltpu.CompilerParams(vmem_limit_bytes=limit * 2**20),
        cost_estimate=pl.CostEstimate(
            flops=flops, bytes_accessed=8 * 2**20, transcendentals=0
        ),
    )(*args)


def swap_cores(value):
    return lax.ppermute(value, "py", [(0, 1), (1, 0)])


def swap_slabs(first, second, first_face, second_face, low_half):
    count = lax.axis_size("px")
    near = [(i, i ^ 1) for i in range(count)]
    far = [(i, i + 1 if i % 2 else i - 1) for i in range(1, count - 1)]

    def slab(i):
        return jnp.stack(
            [
                jnp.concatenate([first[i], first_face[i]], axis=0),
                jnp.concatenate([second[i], second_face[i]], axis=0),
            ]
        )

    low, high = slab(0), slab(3)
    got_far = lax.ppermute(jnp.where(low_half, low, high), "px", far)
    got_near = lax.ppermute(jnp.where(low_half, high, low), "px", near)
    return got_near, got_far


def hop(parts, stage):
    return [
        lax.ppermute(part, ALL, hop_pairs(stage, distance))
        for part, distance in zip(parts, (1, 3, 2))
    ]


def reduce_tiles(own, got, core):
    total = own.astype(F32)
    for part in got:
        total = total + part.astype(F32)
    got = hop([total[4 * d : 4 * d + 4].astype(BF) for d in (1, 3, 2)], 1)
    total = total[0:4]
    for part in got:
        total = total + part.astype(F32)
    got = hop([total[d] for d in (1, 3, 2)], 2)
    total = total[0] + got[0] + got[1] + got[2]
    keep = jnp.where(core == 0, total[:16], total[16:])
    give = jnp.where(core == 0, total[16:], total[:16])
    other = swap_cores(give)
    first = jnp.where(core == 0, keep, other)[:, :864]
    second = jnp.where(core == 0, other, keep)[:, :864]
    return first.T, second.T


def body(fields, cotangent, first_weight, second_weight):
    shape = jax.ShapeDtypeStruct
    core = lax.axis_index("py")
    dp, px = lax.axis_index("dp"), lax.axis_index("px")
    zero = core == 0
    two = jnp.int32(2)
    place = jnp.stack(
        [core, lax.div(px, two), lax.div(dp, two), lax.rem(dp, two) * 2 + lax.rem(px, two)]
    )
    field, cot = fields[0], cotangent[0]
    grid, half = shape((4, 8, 32, 256), BF), shape((2, 8, 32, 256), BF)

    part = shape((2, 256, 256), F32)
    low_half = lax.rem(px, two) == 0
    own_scratch = [pltpu.VMEM((4, 10, 32, 768), BF)] * 2 + [pltpu.VMEM((1024, 256), F32)] * 2
    edge_scratch = [pltpu.VMEM((2, 10, 32, 768), BF)] * 2
    weights = (first_weight, second_weight)
    flops = 2 * 2 * 1024 * 6912 * 256
    (sent1,) = call(
        pack_kernel,
        "pack",
        0,
        (core.astype(jnp.int32).reshape(1), cot, field),
        [shape((4, 9, 32, 256), BF)],
        [pltpu.SemaphoreType.DMA((2,))],
        40,
        (1, 2),
    )
    other1 = swap_cores(sent1)
    near1, far1 = swap_slabs(
        cot,
        field,
        jnp.where(zero, other1[:, 8:9], other1[:, 7:8]),
        jnp.where(zero, other1[:, 0:1], other1[:, 8:9]),
        low_half,
    )
    inner = call(
        inner_kernel,
        "inner",
        flops * 5 // 6,
        (place, cot, field, other1, *weights),
        [half, half, part, part, shape((6912, 256), BF), shape((6912, 256), BF)],
        own_scratch + [pltpu.SemaphoreType.DMA((2,))],
        38,
        (4, 5),
    )
    inner, weights = inner[:4], inner[4:]
    inner_hidden, beside = lax.optimization_barrier((inner[0], other1))
    (chip,) = call(
        chip_kernel,
        "chip",
        flops // 8,
        (place, cot, field, beside),
        [shape((4, 18, 32, 768), BF)],
        [],
        12,
    )
    inner_hidden, chip = lax.optimization_barrier((inner_hidden, chip))
    inner = (inner_hidden, *inner[1:])
    hidden, pre_grad, sent2 = call(
        outer_kernel,
        "outer",
        flops // 6,
        (place, near1, far1, *inner, *weights),
        [grid, grid, shape((4, 9, 32, 256), BF)],
        edge_scratch,
        24,
    )
    edges = swap_cores(
        jnp.where(
            zero,
            jnp.stack([near1[0, 0:8], far1[0, 0:8]]),
            jnp.stack([near1[1, 0:8], far1[1, 0:8]]),
        )
    )
    other2 = swap_cores(sent2)
    near2, far2 = swap_slabs(
        hidden,
        pre_grad,
        jnp.where(zero, other2[:, 8:9], other2[:, 7:8]),
        jnp.where(zero, other2[:, 0:1], other2[:, 8:9]),
        low_half,
    )
    own, send1, send2, send3 = call(
        weight_kernel,
        "weight_terms",
        flops,
        (place, chip, near1, far1, edges, hidden, pre_grad, other2),
        [shape((16, 32, LANES), BF)] * 4,
        [
            pltpu.VMEM((2, 18, 32, 768), BF),
            pltpu.VMEM((256, 2048), BF),
            pltpu.VMEM((2048, 256), BF),
            pltpu.VMEM((256, 7040), BF),
            pltpu.VMEM((8, 256, LANES), BF),
        ],
        34,
    )
    send1, near2, far2 = lax.optimization_barrier((send1, near2, far2))
    got = hop((send1, send3, send2), 0)
    hidden, pre_grad, other2, own = lax.optimization_barrier((hidden, pre_grad, other2, own))
    last = call(
        last_inner_kernel,
        "outputs_inner",
        flops * 5 // 6,
        (place, hidden, pre_grad, other2, field, cot, *weights),
        [half, half, part, part],
        own_scratch,
        26,
    )
    output, field_grad = call(
        last_outer_kernel,
        "outputs_outer",
        flops // 6,
        (place, near2, far2, *last, field, cot, *weights),
        [grid, grid],
        edge_scratch,
        24,
    )
    own, output, field_grad = lax.optimization_barrier((own, output, field_grad))
    first_grad, second_grad = reduce_tiles(own, got, core)
    return output[None], field_grad[None], first_grad, second_grad


def solution(mesh):
    placed = P("dp", "px", "py", None, None)
    return jax.shard_map(
        body,
        mesh=mesh,
        in_specs=(placed, placed, P(), P()),
        out_specs=(placed, placed, P("dp", ("px", "py")), P("dp", ("px", "py"))),
        check_vma=False,
    )
```

```python
import jax
import jax.numpy as jnp
from jax import lax
from jax.experimental import pallas as pl
from jax.experimental.pallas import tpu as pltpu
from jax.sharding import PartitionSpec as P

BF = jnp.bfloat16
F32 = jnp.float32
ALL = ("dp", "px", "py")
X, Y, Z = 0, 1, 2
ORDER = ((X, Y, Z), (Z, X, Y))
LANES = 896


def device(x, y, z, core):
    x, y, z = x % 4, y % 4, z % 4
    return (y * 2 + z // 2) * 16 + (x * 2 + z % 2) * 2 + core


def hop_pairs(stage, distance):
    pairs = []
    for core in range(2):
        step = [0, 0, 0]
        step[ORDER[core][stage]] = distance
        for x in range(4):
            for y in range(4):
                for z in range(4):
                    pairs.append(
                        (
                            device(x, y, z, core),
                            device(x + step[0], y + step[1], z + step[2], core),
                        )
                    )
    return pairs


def shifted(block):
    wide = block.astype(F32)
    place = lax.broadcasted_iota(jnp.int32, wide.shape, 1)
    low = jnp.where(place == 0, 0.0, pltpu.roll(wide, 1, 1)).astype(BF)
    high = jnp.where(place == 31, 0.0, pltpu.roll(wide, 31, 1)).astype(BF)
    return low, high


def put(stack, row, start, block, flip):
    low, high = shifted(block)
    if flip:
        low, high = high, low
    rows = pl.ds(start, block.shape[0])
    stack[row, rows, :, 0:256] = low
    stack[row, rows, :, 256:512] = block
    stack[row, rows, :, 512:768] = high


def put_own(stack, slab, start, own, flip):
    def step(i, _):
        put(stack, i + slab, start, own[i], flip)
        return 0

    lax.fori_loop(0, own.shape[0], step, 0)


def put_faces(stack, core, slab, count, other, at_first, at_second, flip):
    at = jnp.where(core == 0, at_first, at_second)
    row = jnp.where(core == 0, 9, 0)

    def step(i, _):
        put(stack, i + slab, row, other[i, pl.ds(at, 1)], flip)
        stack[i + slab, pl.ds(9 - row, 1)] = jnp.zeros((1, 32, 768), BF)
        return 0

    lax.fori_loop(0, count, step, 0)


def put_halo(stack, core, slab, halo, which, flip):
    row = jnp.where(core == 0, 9, 0)
    put(stack, slab, 1, halo[which, 0:8], flip)
    put(stack, slab, row, halo[which, 8:9], flip)
    stack[slab, pl.ds(9 - row, 1)] = jnp.zeros((1, 32, 768), BF)


def term_of(rows, weight, k, back):
    if not back:
        return jnp.dot(rows, weight[k * 768 : (k + 1) * 768], preferred_element_type=F32)
    term = None
    for c in range(3):
        part = lax.dot_general(
            rows[:, c * 256 : (c + 1) * 256],
            weight[(k * 3 + c) * 256 : (k * 3 + c + 1) * 256],
            (((1,), (1,)), ((), ())),
            preferred_element_type=F32,
        )
        term = part if term is None else term + part
    return term


def conv_own(total, stack, weight, back):
    for a in (1, 0, 2):
        step = 1 - a if back else a - 1
        count = 4 - abs(step)
        to = max(0, -step)
        for b in range(3):
            at = 2 - b if back else b
            rows = stack[to + step : to + step + count, at : at + 8].reshape(count * 256, 768)
            term = term_of(rows, weight, a * 3 + b, back)
            span = slice(to * 256, (to + count) * 256)
            if a == 1 and b == 0:
                total[span] = term
            else:
                total[span] += term


def conv_edges(part, stack, weight, back):
    sums = []
    for side in range(2):
        a = 2 * side if not back else 2 - 2 * side
        total = part[side]
        for b in range(3):
            at = 2 - b if back else b
            rows = stack[side, at : at + 8].reshape(256, 768)
            total = total + term_of(rows, weight, a * 3 + b, back)
        sums.append(total)
    return sums


def gelu_and_slope(v):
    scale = 0.7978845608028654
    square = v * v
    t = jnp.tanh(scale * (v + 0.044715 * (square * v)))
    half = 0.5 * (1.0 + t)
    slope = half + 0.5 * v * (1.0 - t * t) * (scale * (1.0 + 3.0 * 0.044715 * square))
    return v * half, slope


def near_side(place):
    return 1 - lax.rem(place[3], 2)


def pack_kernel(place, cot, field, send, arrived):
    core = place[0]

    def pack(whole, row):
        copies = [
            pltpu.make_async_copy(whole, send.at[:, 0:8], arrived.at[0]),
            pltpu.make_async_copy(row, send.at[:, 8:9], arrived.at[1]),
        ]
        for copy in copies:
            copy.start()
        for copy in copies:
            copy.wait()

    @pl.when(core == 0)
    def _():
        pack(cot, field.at[:, 7:8])

    @pl.when(core == 1)
    def _():
        pack(field, cot.at[:, 0:1])


def inner_kernel(
    place, cot, field, other, first_hbm, second_hbm, hidden, pre_grad, part_pre, part_grad,
    first_w, second_w, stack, back, pre, grad, arrived,
):
    core = place[0]
    copies = [
        pltpu.make_async_copy(first_hbm, first_w, arrived.at[0]),
        pltpu.make_async_copy(second_hbm, second_w, arrived.at[1]),
    ]
    for copy in copies:
        copy.start()
    put_own(stack, 0, 1, field, False)
    put_faces(stack, core, 0, 4, other, 0, 8, False)
    put_own(back, 0, 1, cot, True)
    put_faces(back, core, 0, 4, other, 8, 7, True)
    for copy in copies:
        copy.wait()
    conv_own(pre, stack, first_w, False)
    conv_own(grad, back, second_w, True)
    for i in range(2):
        rows = slice((i + 1) * 256, (i + 2) * 256)
        value, slope = gelu_and_slope(pre[rows])
        hidden[i] = value.astype(BF).reshape(8, 32, 256)
        pre_grad[i] = (grad[rows] * slope).astype(BF).reshape(8, 32, 256)
        rows = slice(i * 768, i * 768 + 256)
        part_pre[i] = pre[rows]
        part_grad[i] = grad[rows]


def outer_kernel(
    place, near, far, inner_hidden, inner_grad, part_pre, part_grad, first_w, second_w,
    hidden, pre_grad, send, stack, back,
):
    core = place[0]
    side = near_side(place)
    put_halo(stack, core, side, near, 1, False)
    put_halo(stack, core, 1 - side, far, 1, False)
    put_halo(back, core, side, near, 0, True)
    put_halo(back, core, 1 - side, far, 0, True)
    pre = conv_edges(part_pre, stack, first_w, False)
    grad = conv_edges(part_grad, back, second_w, True)
    for i in range(2):
        value, slope = gelu_and_slope(pre[i])
        hidden[3 * i] = value.astype(BF).reshape(8, 32, 256)
        pre_grad[3 * i] = (grad[i] * slope).astype(BF).reshape(8, 32, 256)
        hidden[1 + i] = inner_hidden[i]
        pre_grad[1 + i] = inner_grad[i]

    @pl.when(core == 0)
    def _():
        send[:, 0:8] = hidden[...]
        send[:, 8:9] = pre_grad[:, 7:8]

    @pl.when(core == 1)
    def _():
        send[:, 0:8] = pre_grad[...]
        send[:, 8:9] = hidden[:, 0:1]


def last_inner_kernel(
    place, hid, pre_grad, other, field, cot, first_w, second_w,
    out, field_grad, part_out, part_grad, stack, back, total, grad,
):
    core = place[0]
    put_own(stack, 0, 1, hid, False)
    put_faces(stack, core, 0, 4, other, 8, 7, False)
    put_own(back, 0, 1, pre_grad, True)
    put_faces(back, core, 0, 4, other, 0, 8, True)
    conv_own(total, stack, second_w, False)
    conv_own(grad, back, first_w, True)
    for i in range(2):
        rows = slice((i + 1) * 256, (i + 2) * 256)
        one = field[i + 1].astype(F32).reshape(256, 256) + total[rows]
        out[i] = one.astype(BF).reshape(8, 32, 256)
        two = cot[i + 1].astype(F32).reshape(256, 256) + grad[rows]
        field_grad[i] = two.astype(BF).reshape(8, 32, 256)
        rows = slice(i * 768, i * 768 + 256)
        part_out[i] = total[rows]
        part_grad[i] = grad[rows]


def last_outer_kernel(
    place, near, far, inner_out, inner_grad, part_out, part_grad, field, cot, first_w, second_w,
    out, field_grad, stack, back,
):
    core = place[0]
    side = near_side(place)
    put_halo(stack, core, side, near, 0, False)
    put_halo(stack, core, 1 - side, far, 0, False)
    put_halo(back, core, side, near, 1, True)
    put_halo(back, core, 1 - side, far, 1, True)
    total = conv_edges(part_out, stack, second_w, False)
    grad = conv_edges(part_grad, back, first_w, True)
    for i in range(2):
        one = field[3 * i].astype(F32).reshape(256, 256) + total[i]
        out[3 * i] = one.astype(BF).reshape(8, 32, 256)
        two = cot[3 * i].astype(F32).reshape(256, 256) + grad[i]
        field_grad[3 * i] = two.astype(BF).reshape(8, 32, 256)
        out[1 + i] = inner_out[i]
        field_grad[1 + i] = inner_grad[i]


def chip_kernel(place, cot, field, other, chip):
    core = place[0]

    def fill(value, half, flip):
        put_own(chip, 0, 1 + 8 * half, value, flip)

        def step(i, _):
            put(chip, i, 9 - 8 * half, other[i, 0:8], flip)
            chip[i, 0:1] = jnp.zeros((1, 32, 768), BF)
            chip[i, 17:18] = jnp.zeros((1, 32, 768), BF)
            return 0

        lax.fori_loop(0, 4, step, 0)

    @pl.when(core == 0)
    def _():
        fill(field, 0, False)

    @pl.when(core == 1)
    def _():
        fill(cot, 1, True)


def windows(chip, sides, a, b):
    rows = slice(b, b + 16)
    if a == 1:
        return [(0, chip[0:4, rows].reshape(2048, 768))]
    if a == 0:
        return [
            (0, sides[0, rows].reshape(512, 768)),
            (512, chip[0:3, rows].reshape(1536, 768)),
        ]
    return [
        (0, chip[1:4, rows].reshape(1536, 768)),
        (1536, sides[1, rows].reshape(512, 768)),
    ]


def terms_of_first(flat, base, steps, chip, sides, turned):
    for k in steps:
        term = None
        for at, rows in windows(chip, sides, k // 3, k % 3):
            part = jnp.dot(turned[:, at : at + rows.shape[0]], rows, preferred_element_type=F32)
            term = part if term is None else term + part
        flat[:, k * 768 - base : (k + 1) * 768 - base] = (term * 0.125).astype(BF)


def terms_of_second(flat, base, steps, chip, sides, local):
    for k in steps:
        term = None
        for at, rows in windows(chip, sides, 2 - k // 3, 2 - k % 3):
            part = lax.dot_general(
                rows,
                local[at : at + rows.shape[0]],
                (((0,), (0,)), ((), ())),
                preferred_element_type=F32,
            )
            term = part if term is None else term + part
        term = (term * 0.125).astype(BF)
        for c in range(3):
            start = (k * 3 + c) * 256 - base
            flat[:, start : start + 256] = term[c * 256 : (c + 1) * 256]


def give_tiles(place, flat, tiles, outs):
    for k in range(4):
        tiles[k] = flat[:, k * 864 : k * 864 + LANES]
    x, z = place[1], place[3]
    zero = place[0] == 0
    for first, ref in enumerate(outs):
        for i in range(8):
            other, high = i // 2, i % 2
            to_x = lax.rem(x + jnp.where(zero, first, other), 4)
            to_z = lax.rem(z + jnp.where(zero, other, first), 4)
            row = high * 2 + lax.div(to_z, 2)
            to_px = to_x * 2 + lax.rem(to_z, 2)
            ref[i] = tiles[row, pl.ds(pl.multiple_of(to_px * 32, 32), 32), :]


def weight_kernel(
    place, chip, near1, far1, edges, hid, pre_grad, other2,
    own, send1, send2, send3, sides, turned, local, rest, flat, tiles,
):
    core = place[0]
    near = near_side(place)

    def fill(which, half, flip):
        mine, others = 1 + 8 * half, 9 - 8 * half
        put(sides, near, mine, near1[which, 0:8], flip)
        put(sides, 1 - near, mine, far1[which, 0:8], flip)
        put(sides, near, others, edges[0], flip)
        put(sides, 1 - near, others, edges[1], flip)
        for i in range(2):
            sides[i, 0:1] = jnp.zeros((1, 32, 768), BF)
            sides[i, 17:18] = jnp.zeros((1, 32, 768), BF)

    @pl.when(core == 0)
    def _():
        fill(1, 0, False)
        for i in range(4):
            turned[:, i * 512 : i * 512 + 256] = pre_grad[i].reshape(256, 256).T
            turned[:, i * 512 + 256 : i * 512 + 512] = other2[i, 0:8].reshape(256, 256).T
        terms_of_first(flat, 0, range(5), chip, sides, turned)

    @pl.when(core == 1)
    def _():
        fill(0, 1, True)
        for i in range(4):
            local[i * 512 : i * 512 + 256] = other2[i, 0:8].reshape(256, 256)
            local[i * 512 + 256 : i * 512 + 512] = hid[i].reshape(256, 256)
        terms_of_second(flat, 0, range(5), chip, sides, local)

    rest[...] = flat[:, 3456:3840]
    give_tiles(place, flat, tiles, (own, send1, send2, send3))


def weight_rest_kernel(
    place, chip, sides, turned, local, rest, own, send1, send2, send3, flat, tiles
):
    core = place[0]
    flat[:, 0:384] = rest[...]
    flat[:, 3456:3584] = jnp.zeros((256, 128), BF)

    @pl.when(core == 0)
    def _():
        terms_of_first(flat, 3456, range(5, 9), chip, sides, turned)

    @pl.when(core == 1)
    def _():
        terms_of_second(flat, 3456, range(5, 9), chip, sides, local)

    give_tiles(place, flat, tiles, (own, send1, send2, send3))


def sum_kernel(place, *refs):
    ins, (keep, send1, send2, send3, sums) = refs[:8], refs[8:]
    for half in range(2):
        for i in range(8):
            total = ins[4 * half][i].astype(F32)
            for ref in ins[4 * half + 1 : 4 * half + 4]:
                total = total + ref[i].astype(F32)
            sums[half * 8 + i] = total
    zero, y = place[0] == 0, place[2]
    for second, ref in enumerate((keep, send1, send2, send3)):
        for third in range(4):
            to_y = lax.rem(y + jnp.where(zero, second, third), 4)
            other = jnp.where(zero, third, second)
            at = lax.div(to_y, 2) * 8 + other * 2 + lax.rem(to_y, 2)
            ref[third] = sums[at].astype(ref.dtype)


def call(kernel, name, flops, args, outs, scratch, limit, far=()):
    whole = pl.BlockSpec(memory_space=pltpu.VMEM)
    return pl.pallas_call(
        kernel,
        name=name,
        out_shape=outs,
        in_specs=[pl.BlockSpec(memory_space=pltpu.SMEM)]
        + [
            pl.BlockSpec(memory_space=pltpu.HBM) if i in far else whole
            for i in range(1, len(args))
        ],
        out_specs=[whole] * len(outs),
        scratch_shapes=scratch,
        compiler_params=pltpu.CompilerParams(vmem_limit_bytes=limit * 2**20),
        cost_estimate=pl.CostEstimate(
            flops=flops, bytes_accessed=8 * 2**20, transcendentals=0
        ),
    )(*args)


def swap_cores(value):
    return lax.ppermute(value, "py", [(0, 1), (1, 0)])


def swap_slabs(first, second, first_face, second_face, low_half):
    count = lax.axis_size("px")
    near = [(i, i ^ 1) for i in range(count)]
    far = [(i, i + 1 if i % 2 else i - 1) for i in range(1, count - 1)]

    def slab(i):
        return jnp.stack(
            [
                jnp.concatenate([first[i], first_face[i]], axis=0),
                jnp.concatenate([second[i], second_face[i]], axis=0),
            ]
        )

    low, high = slab(0), slab(3)
    got_far = lax.ppermute(jnp.where(low_half, low, high), "px", far)
    got_near = lax.ppermute(jnp.where(low_half, high, low), "px", near)
    return got_near, got_far


def hop(parts, stage):
    return [
        lax.ppermute(part, ALL, hop_pairs(stage, distance))
        for part, distance in zip(parts, (1, 3, 2))
    ]


def reduce_tiles(place, halves, core):
    shape = jax.ShapeDtypeStruct
    keep, send1, send2, send3 = call(
        sum_kernel,
        "sum",
        0,
        (place, *halves),
        [shape((4, 32, LANES), F32)] + [shape((4, 32, LANES), BF)] * 3,
        [pltpu.VMEM((16, 32, LANES), F32)],
        16,
    )
    total = keep
    for part in hop((send1, send3, send2), 1):
        total = total + part.astype(F32)
    got = hop([total[d] for d in (1, 3, 2)], 2)
    total = total[0] + got[0] + got[1] + got[2]
    keep = jnp.where(core == 0, total[:16], total[16:])
    give = jnp.where(core == 0, total[16:], total[:16])
    other = swap_cores(give)
    first = jnp.where(core == 0, keep, other)[:, :864]
    second = jnp.where(core == 0, other, keep)[:, :864]
    return first.T, second.T


def body(fields, cotangent, first_weight, second_weight):
    shape = jax.ShapeDtypeStruct
    core = lax.axis_index("py")
    dp, px = lax.axis_index("dp"), lax.axis_index("px")
    zero = core == 0
    two = jnp.int32(2)
    place = jnp.stack(
        [core, lax.div(px, two), lax.div(dp, two), lax.rem(dp, two) * 2 + lax.rem(px, two)]
    )
    field, cot = fields[0], cotangent[0]
    grid, half = shape((4, 8, 32, 256), BF), shape((2, 8, 32, 256), BF)

    part = shape((2, 256, 256), F32)
    low_half = lax.rem(px, two) == 0
    own_scratch = [pltpu.VMEM((4, 10, 32, 768), BF)] * 2 + [pltpu.VMEM((1024, 256), F32)] * 2
    edge_scratch = [pltpu.VMEM((2, 10, 32, 768), BF)] * 2
    weights = (first_weight, second_weight)
    flops = 2 * 2 * 1024 * 6912 * 256
    (sent1,) = call(
        pack_kernel,
        "pack",
        0,
        (core.astype(jnp.int32).reshape(1), cot, field),
        [shape((4, 9, 32, 256), BF)],
        [pltpu.SemaphoreType.DMA((2,))],
        40,
        (1, 2),
    )
    other1 = swap_cores(sent1)
    near1, far1 = swap_slabs(
        cot,
        field,
        jnp.where(zero, other1[:, 8:9], other1[:, 7:8]),
        jnp.where(zero, other1[:, 0:1], other1[:, 8:9]),
        low_half,
    )
    inner = call(
        inner_kernel,
        "inner",
        flops * 5 // 6,
        (place, cot, field, other1, *weights),
        [half, half, part, part, shape((6912, 256), BF), shape((6912, 256), BF)],
        own_scratch + [pltpu.SemaphoreType.DMA((2,))],
        38,
        (4, 5),
    )
    inner, weights = inner[:4], inner[4:]
    inner_hidden, beside = lax.optimization_barrier((inner[0], other1))
    (chip,) = call(
        chip_kernel,
        "chip",
        flops // 8,
        (place, cot, field, beside),
        [shape((4, 18, 32, 768), BF)],
        [],
        12,
    )
    inner_hidden, chip = lax.optimization_barrier((inner_hidden, chip))
    inner = (inner_hidden, *inner[1:])
    hidden, pre_grad, sent2 = call(
        outer_kernel,
        "outer",
        flops // 6,
        (place, near1, far1, *inner, *weights),
        [grid, grid, shape((4, 9, 32, 256), BF)],
        edge_scratch,
        24,
    )
    edges = swap_cores(
        jnp.where(
            zero,
            jnp.stack([near1[0, 0:8], far1[0, 0:8]]),
            jnp.stack([near1[1, 0:8], far1[1, 0:8]]),
        )
    )
    other2 = swap_cores(sent2)
    near2, far2 = swap_slabs(
        hidden,
        pre_grad,
        jnp.where(zero, other2[:, 8:9], other2[:, 7:8]),
        jnp.where(zero, other2[:, 0:1], other2[:, 8:9]),
        low_half,
    )
    tiles = [shape((8, 32, LANES), BF)] * 4
    own1, *sent1, sides, turned, local, rest = call(
        weight_kernel,
        "weight_terms",
        flops * 5 // 9,
        (place, chip, near1, far1, edges, hidden, pre_grad, other2),
        tiles
        + [
            shape((2, 18, 32, 768), BF),
            shape((256, 2048), BF),
            shape((2048, 256), BF),
            shape((256, 384), BF),
        ],
        [pltpu.VMEM((256, 3840), BF), pltpu.VMEM((4, 256, LANES), BF)],
        26,
    )
    got1 = hop((sent1[0], sent1[2], sent1[1]), 0)
    rest, near2, far2 = lax.optimization_barrier((rest, near2, far2))
    own2, *sent2 = call(
        weight_rest_kernel,
        "weight_terms_rest",
        flops * 4 // 9,
        (place, chip, sides, turned, local, rest),
        tiles,
        [pltpu.VMEM((256, 3584), BF), pltpu.VMEM((4, 256, LANES), BF)],
        26,
    )
    got2 = hop((sent2[0], sent2[2], sent2[1]), 0)
    hidden, pre_grad, other2, own2, *got1 = lax.optimization_barrier(
        (hidden, pre_grad, other2, own2, *got1)
    )
    last = call(
        last_inner_kernel,
        "outputs_inner",
        flops * 5 // 6,
        (place, hidden, pre_grad, other2, field, cot, *weights),
        [half, half, part, part],
        own_scratch,
        26,
    )
    output, field_grad = call(
        last_outer_kernel,
        "outputs_outer",
        flops // 6,
        (place, near2, far2, *last, field, cot, *weights),
        [grid, grid],
        edge_scratch,
        24,
    )
    own2, output, field_grad = lax.optimization_barrier((own2, output, field_grad))
    first_grad, second_grad = reduce_tiles(place, (own1, *got1, own2, *got2), core)
    return output[None], field_grad[None], first_grad, second_grad


def solution(mesh):
    placed = P("dp", "px", "py", None, None)
    return jax.shard_map(
        body,
        mesh=mesh,
        in_specs=(placed, placed, P(), P()),
        out_specs=(placed, placed, P("dp", ("px", "py")), P("dp", ("px", "py"))),
        check_vma=False,
    )
```

```python
import jax
import jax.numpy as jnp
from jax import lax
from jax.experimental import pallas as pl
from jax.experimental.pallas import tpu as pltpu
from jax.sharding import PartitionSpec as P

BF = jnp.bfloat16
F32 = jnp.float32
ALL = ("dp", "px", "py")
X, Y, Z = 0, 1, 2
ORDER = ((X, Y, Z), (Y, Z, X))
EARLY, LATE = (0, 3, 5, 8), (1, 2, 4, 6, 7)
LANES = 896


def device(x, y, z, core):
    x, y, z = x % 4, y % 4, z % 4
    return (y * 2 + z // 2) * 16 + (x * 2 + z % 2) * 2 + core


def hop_pairs(stage, distance):
    pairs = []
    for core in range(2):
        step = [0, 0, 0]
        step[ORDER[core][stage]] = distance
        for x in range(4):
            for y in range(4):
                for z in range(4):
                    pairs.append(
                        (
                            device(x, y, z, core),
                            device(x + step[0], y + step[1], z + step[2], core),
                        )
                    )
    return pairs


def shifted(block):
    wide = block.astype(F32)
    place = lax.broadcasted_iota(jnp.int32, wide.shape, 1)
    low = jnp.where(place == 0, 0.0, pltpu.roll(wide, 1, 1)).astype(BF)
    high = jnp.where(place == 31, 0.0, pltpu.roll(wide, 31, 1)).astype(BF)
    return low, high


def put(stack, row, start, block, flip):
    low, high = shifted(block)
    if flip:
        low, high = high, low
    rows = pl.ds(start, block.shape[0])
    stack[row, rows, :, 0:256] = low
    stack[row, rows, :, 256:512] = block
    stack[row, rows, :, 512:768] = high


def put_own(stack, slab, start, own, flip):
    def step(i, _):
        put(stack, i + slab, start, own[i], flip)
        return 0

    lax.fori_loop(0, own.shape[0], step, 0)


def put_faces(stack, core, slab, count, other, at_first, at_second, flip):
    at = jnp.where(core == 0, at_first, at_second)
    row = jnp.where(core == 0, 9, 0)

    def step(i, _):
        put(stack, i + slab, row, other[i, pl.ds(at, 1)], flip)
        stack[i + slab, pl.ds(9 - row, 1)] = jnp.zeros((1, 32, 768), BF)
        return 0

    lax.fori_loop(0, count, step, 0)


def put_halo(stack, core, slab, halo, which, flip):
    row = jnp.where(core == 0, 9, 0)
    put(stack, slab, 1, halo[which, 0:8], flip)
    put(stack, slab, row, halo[which, 8:9], flip)
    stack[slab, pl.ds(9 - row, 1)] = jnp.zeros((1, 32, 768), BF)


def term_of(rows, weight, k, back):
    if not back:
        return jnp.dot(rows, weight[k * 768 : (k + 1) * 768], preferred_element_type=F32)
    term = None
    for c in range(3):
        part = lax.dot_general(
            rows[:, c * 256 : (c + 1) * 256],
            weight[(k * 3 + c) * 256 : (k * 3 + c + 1) * 256],
            (((1,), (1,)), ((), ())),
            preferred_element_type=F32,
        )
        term = part if term is None else term + part
    return term


def conv_own(total, stack, weight, back):
    for a in (1, 0, 2):
        step = 1 - a if back else a - 1
        count = 4 - abs(step)
        to = max(0, -step)
        for b in range(3):
            at = 2 - b if back else b
            rows = stack[to + step : to + step + count, at : at + 8].reshape(count * 256, 768)
            term = term_of(rows, weight, a * 3 + b, back)
            span = slice(to * 256, (to + count) * 256)
            if a == 1 and b == 0:
                total[span] = term
            else:
                total[span] += term


def conv_edges(part, stack, weight, back):
    sums = []
    for side in range(2):
        a = 2 * side if not back else 2 - 2 * side
        total = part[side]
        for b in range(3):
            at = 2 - b if back else b
            rows = stack[side, at : at + 8].reshape(256, 768)
            total = total + term_of(rows, weight, a * 3 + b, back)
        sums.append(total)
    return sums


def gelu_and_slope(v):
    scale = 0.7978845608028654
    square = v * v
    t = jnp.tanh(scale * (v + 0.044715 * (square * v)))
    half = 0.5 * (1.0 + t)
    slope = half + 0.5 * v * (1.0 - t * t) * (scale * (1.0 + 3.0 * 0.044715 * square))
    return v * half, slope


def near_side(place):
    return 1 - lax.rem(place[3], 2)


def pack_kernel(place, cot, field, send, arrived):
    core = place[0]

    def pack(whole, row):
        copies = [
            pltpu.make_async_copy(whole, send.at[:, 0:8], arrived.at[0]),
            pltpu.make_async_copy(row, send.at[:, 8:9], arrived.at[1]),
        ]
        for copy in copies:
            copy.start()
        for copy in copies:
            copy.wait()

    @pl.when(core == 0)
    def _():
        pack(cot, field.at[:, 7:8])

    @pl.when(core == 1)
    def _():
        pack(field, cot.at[:, 0:1])


def inner_kernel(
    place, cot, field, other, first_hbm, second_hbm, hidden, pre_grad, part_pre, part_grad,
    first_w, second_w, stack, back, pre, grad, arrived,
):
    core = place[0]
    copies = [
        pltpu.make_async_copy(first_hbm, first_w, arrived.at[0]),
        pltpu.make_async_copy(second_hbm, second_w, arrived.at[1]),
    ]
    for copy in copies:
        copy.start()
    put_own(stack, 0, 1, field, False)
    put_faces(stack, core, 0, 4, other, 0, 8, False)
    put_own(back, 0, 1, cot, True)
    put_faces(back, core, 0, 4, other, 8, 7, True)
    for copy in copies:
        copy.wait()
    conv_own(pre, stack, first_w, False)
    conv_own(grad, back, second_w, True)
    for i in range(2):
        rows = slice((i + 1) * 256, (i + 2) * 256)
        value, slope = gelu_and_slope(pre[rows])
        hidden[i] = value.astype(BF).reshape(8, 32, 256)
        pre_grad[i] = (grad[rows] * slope).astype(BF).reshape(8, 32, 256)
        rows = slice(i * 768, i * 768 + 256)
        part_pre[i] = pre[rows]
        part_grad[i] = grad[rows]


def outer_kernel(
    place, near, far, inner_hidden, inner_grad, part_pre, part_grad, first_w, second_w,
    hidden, pre_grad, send, stack, back,
):
    core = place[0]
    side = near_side(place)
    put_halo(stack, core, side, near, 1, False)
    put_halo(stack, core, 1 - side, far, 1, False)
    put_halo(back, core, side, near, 0, True)
    put_halo(back, core, 1 - side, far, 0, True)
    pre = conv_edges(part_pre, stack, first_w, False)
    grad = conv_edges(part_grad, back, second_w, True)
    for i in range(2):
        value, slope = gelu_and_slope(pre[i])
        hidden[3 * i] = value.astype(BF).reshape(8, 32, 256)
        pre_grad[3 * i] = (grad[i] * slope).astype(BF).reshape(8, 32, 256)
        hidden[1 + i] = inner_hidden[i]
        pre_grad[1 + i] = inner_grad[i]

    @pl.when(core == 0)
    def _():
        send[:, 0:8] = hidden[...]
        send[:, 8:9] = pre_grad[:, 7:8]

    @pl.when(core == 1)
    def _():
        send[:, 0:8] = pre_grad[...]
        send[:, 8:9] = hidden[:, 0:1]


def last_inner_kernel(
    place, hid, pre_grad, other, field, cot, first_w, second_w,
    out, field_grad, part_out, part_grad, stack, back, total, grad,
):
    core = place[0]
    put_own(stack, 0, 1, hid, False)
    put_faces(stack, core, 0, 4, other, 8, 7, False)
    put_own(back, 0, 1, pre_grad, True)
    put_faces(back, core, 0, 4, other, 0, 8, True)
    conv_own(total, stack, second_w, False)
    conv_own(grad, back, first_w, True)
    for i in range(2):
        rows = slice((i + 1) * 256, (i + 2) * 256)
        one = field[i + 1].astype(F32).reshape(256, 256) + total[rows]
        out[i] = one.astype(BF).reshape(8, 32, 256)
        two = cot[i + 1].astype(F32).reshape(256, 256) + grad[rows]
        field_grad[i] = two.astype(BF).reshape(8, 32, 256)
        rows = slice(i * 768, i * 768 + 256)
        part_out[i] = total[rows]
        part_grad[i] = grad[rows]


def last_outer_kernel(
    place, near, far, inner_out, inner_grad, part_out, part_grad, field, cot, first_w, second_w,
    out, field_grad, stack, back,
):
    core = place[0]
    side = near_side(place)
    put_halo(stack, core, side, near, 0, False)
    put_halo(stack, core, 1 - side, far, 0, False)
    put_halo(back, core, side, near, 1, True)
    put_halo(back, core, 1 - side, far, 1, True)
    total = conv_edges(part_out, stack, second_w, False)
    grad = conv_edges(part_grad, back, first_w, True)
    for i in range(2):
        one = field[3 * i].astype(F32).reshape(256, 256) + total[i]
        out[3 * i] = one.astype(BF).reshape(8, 32, 256)
        two = cot[3 * i].astype(F32).reshape(256, 256) + grad[i]
        field_grad[3 * i] = two.astype(BF).reshape(8, 32, 256)
        out[1 + i] = inner_out[i]
        field_grad[1 + i] = inner_grad[i]


def chip_kernel(place, cot, field, other, chip):
    core = place[0]

    def fill(value, half, flip):
        put_own(chip, 0, 1 + 8 * half, value, flip)

        def step(i, _):
            put(chip, i, 9 - 8 * half, other[i, 0:8], flip)
            chip[i, 0:1] = jnp.zeros((1, 32, 768), BF)
            chip[i, 17:18] = jnp.zeros((1, 32, 768), BF)
            return 0

        lax.fori_loop(0, 4, step, 0)

    @pl.when(core == 0)
    def _():
        fill(field, 0, False)

    @pl.when(core == 1)
    def _():
        fill(cot, 1, True)


def windows(chip, sides, a, b):
    rows = slice(b, b + 16)
    if a == 1:
        return [(0, chip[0:4, rows].reshape(2048, 768))]
    if a == 0:
        return [
            (0, sides[0, rows].reshape(512, 768)),
            (512, chip[0:3, rows].reshape(1536, 768)),
        ]
    return [
        (0, chip[1:4, rows].reshape(1536, 768)),
        (1536, sides[1, rows].reshape(512, 768)),
    ]


def terms_of_first(flat, steps, chip, sides, turned):
    for j, k in enumerate(steps):
        term = None
        for at, rows in windows(chip, sides, k // 3, k % 3):
            part = jnp.dot(turned[:, at : at + rows.shape[0]], rows, preferred_element_type=F32)
            term = part if term is None else term + part
        flat[:, j * 768 : (j + 1) * 768] = (term * 0.125).astype(BF)


def terms_of_second(flat, steps, chip, sides, local):
    for j, k in enumerate(steps):
        term = None
        for at, rows in windows(chip, sides, 2 - k // 3, 2 - k % 3):
            part = lax.dot_general(
                rows,
                local[at : at + rows.shape[0]],
                (((0,), (0,)), ((), ())),
                preferred_element_type=F32,
            )
            term = part if term is None else term + part
        term = (term * 0.125).astype(BF)
        for c in range(3):
            start = (j * 3 + c) * 256
            flat[:, start : start + 256] = term[c * 256 : (c + 1) * 256]


def give_tiles(place, flat, tiles, width, outs):
    for k in range(4):
        tiles[k] = flat[:, k * width : (k + 1) * width]
    x, y = place[1], place[2]
    zero = place[0] == 0
    for first, ref in enumerate(outs):
        for i in range(8):
            to_x = jnp.where(zero, lax.rem(x + first, 4), i // 2)
            to_y = jnp.where(zero, i // 2, lax.rem(y + first, 4))
            to_px = to_x * 2 + i % 2
            ref[i] = tiles[to_y, pl.ds(pl.multiple_of(to_px * 32, 32), 32), :]


def weight_kernel(
    place, chip, near1, far1, edges, hid, pre_grad, other2,
    own, send1, send2, send3, sides, turned, local, flat, tiles,
):
    core = place[0]
    near = near_side(place)

    def fill(which, half, flip):
        mine, others = 1 + 8 * half, 9 - 8 * half
        put(sides, near, mine, near1[which, 0:8], flip)
        put(sides, 1 - near, mine, far1[which, 0:8], flip)
        put(sides, near, others, edges[0], flip)
        put(sides, 1 - near, others, edges[1], flip)
        for i in range(2):
            sides[i, 0:1] = jnp.zeros((1, 32, 768), BF)
            sides[i, 17:18] = jnp.zeros((1, 32, 768), BF)

    @pl.when(core == 0)
    def _():
        fill(1, 0, False)
        for i in range(4):
            turned[:, i * 512 : i * 512 + 256] = pre_grad[i].reshape(256, 256).T
            turned[:, i * 512 + 256 : i * 512 + 512] = other2[i, 0:8].reshape(256, 256).T
        terms_of_first(flat, EARLY, chip, sides, turned)

    @pl.when(core == 1)
    def _():
        fill(0, 1, True)
        for i in range(4):
            local[i * 512 : i * 512 + 256] = other2[i, 0:8].reshape(256, 256)
            local[i * 512 + 256 : i * 512 + 512] = hid[i].reshape(256, 256)
        terms_of_second(flat, EARLY, chip, sides, local)

    give_tiles(place, flat, tiles, 768, (own, send1, send2, send3))


def weight_rest_kernel(
    place, chip, sides, turned, local, own, send1, send2, send3, flat, tiles
):
    core = place[0]

    @pl.when(core == 0)
    def _():
        terms_of_first(flat, LATE, chip, sides, turned)

    @pl.when(core == 1)
    def _():
        terms_of_second(flat, LATE, chip, sides, local)

    give_tiles(place, flat, tiles, 960, (own, send1, send2, send3))


def sum_kernel(place, *refs):
    ins, (keep, send1, send2, send3, whole, tiles) = refs[:8], refs[8:]
    core, x, y, z = place[0], place[1], place[2], place[3]
    zero = core == 0

    def add(refs, i):
        total = refs[0][i].astype(F32)
        for ref in refs[1:]:
            total = total + ref[i].astype(F32)
        return total

    def join(i, row):
        early, late = add(ins[0:4], i), add(ins[4:8], i)
        before = (0, 576, 384, 960)[row]
        if before:
            whole[i, :, 0:before] = late[:, 0:before]
        whole[i, :, before : before + 768] = early
        if before < 960:
            whole[i, :, before + 768 : 1728] = late[:, before:960]

    @pl.when(zero)
    def _():
        for i in range(8):
            join(i, i // 2)

    for row in range(4):

        @pl.when(jnp.logical_and(core == 1, y == row))
        def _():
            for i in range(8):
                join(i, row)

    for i in range(8):
        whole[i, :, 1728:1792] = jnp.zeros((32, 64), F32)
        for high in range(2):
            tiles[i * 2 + high] = whole[i, :, high * 864 : high * 864 + LANES]
    for second, ref in enumerate((keep, send1, send2, send3)):
        for third in range(4):
            to_z = lax.rem(z + jnp.where(zero, third, second), 4)
            other = jnp.where(zero, lax.rem(y + second, 4), lax.rem(x + third, 4))
            at = (other * 2 + lax.rem(to_z, 2)) * 2 + lax.div(to_z, 2)
            ref[third] = tiles[at].astype(ref.dtype)


def call(kernel, name, flops, args, outs, scratch, limit, far=()):
    whole = pl.BlockSpec(memory_space=pltpu.VMEM)
    return pl.pallas_call(
        kernel,
        name=name,
        out_shape=outs,
        in_specs=[pl.BlockSpec(memory_space=pltpu.SMEM)]
        + [
            pl.BlockSpec(memory_space=pltpu.HBM) if i in far else whole
            for i in range(1, len(args))
        ],
        out_specs=[whole] * len(outs),
        scratch_shapes=scratch,
        compiler_params=pltpu.CompilerParams(vmem_limit_bytes=limit * 2**20),
        cost_estimate=pl.CostEstimate(
            flops=flops, bytes_accessed=8 * 2**20, transcendentals=0
        ),
    )(*args)


def swap_cores(value):
    return lax.ppermute(value, "py", [(0, 1), (1, 0)])


def swap_slabs(first, second, first_face, second_face, low_half):
    count = lax.axis_size("px")
    near = [(i, i ^ 1) for i in range(count)]
    far = [(i, i + 1 if i % 2 else i - 1) for i in range(1, count - 1)]

    def slab(i):
        return jnp.stack(
            [
                jnp.concatenate([first[i], first_face[i]], axis=0),
                jnp.concatenate([second[i], second_face[i]], axis=0),
            ]
        )

    low, high = slab(0), slab(3)
    got_far = lax.ppermute(jnp.where(low_half, low, high), "px", far)
    got_near = lax.ppermute(jnp.where(low_half, high, low), "px", near)
    return got_near, got_far


def hop(parts, stage):
    return [
        lax.ppermute(part, ALL, hop_pairs(stage, distance))
        for part, distance in zip(parts, (1, 3, 2))
    ]


def reduce_tiles(place, halves, core):
    shape = jax.ShapeDtypeStruct
    keep, send1, send2, send3 = call(
        sum_kernel,
        "sum",
        0,
        (place, *halves),
        [shape((4, 32, LANES), F32)] + [shape((4, 32, LANES), BF)] * 3,
        [pltpu.VMEM((8, 32, 1792), F32), pltpu.VMEM((16, 32, LANES), F32)],
        18,
    )
    total = keep
    for part in hop((send1, send3, send2), 1):
        total = total + part.astype(F32)
    got = hop([total[d] for d in (1, 3, 2)], 2)
    total = total[0] + got[0] + got[1] + got[2]
    keep = jnp.where(core == 0, total[:16], total[16:])
    give = jnp.where(core == 0, total[16:], total[:16])
    other = swap_cores(give)
    first = jnp.where(core == 0, keep, other)[:, :864]
    second = jnp.where(core == 0, other, keep)[:, :864]
    return first.T, second.T


def body(fields, cotangent, first_weight, second_weight):
    shape = jax.ShapeDtypeStruct
    core = lax.axis_index("py")
    dp, px = lax.axis_index("dp"), lax.axis_index("px")
    zero = core == 0
    two = jnp.int32(2)
    place = jnp.stack(
        [core, lax.div(px, two), lax.div(dp, two), lax.rem(dp, two) * 2 + lax.rem(px, two)]
    )
    field, cot = fields[0], cotangent[0]
    grid, half = shape((4, 8, 32, 256), BF), shape((2, 8, 32, 256), BF)

    part = shape((2, 256, 256), F32)
    low_half = lax.rem(px, two) == 0
    own_scratch = [pltpu.VMEM((4, 10, 32, 768), BF)] * 2 + [pltpu.VMEM((1024, 256), F32)] * 2
    edge_scratch = [pltpu.VMEM((2, 10, 32, 768), BF)] * 2
    weights = (first_weight, second_weight)
    flops = 2 * 2 * 1024 * 6912 * 256
    (sent1,) = call(
        pack_kernel,
        "pack",
        0,
        (core.astype(jnp.int32).reshape(1), cot, field),
        [shape((4, 9, 32, 256), BF)],
        [pltpu.SemaphoreType.DMA((2,))],
        40,
        (1, 2),
    )
    other1 = swap_cores(sent1)
    near1, far1 = swap_slabs(
        cot,
        field,
        jnp.where(zero, other1[:, 8:9], other1[:, 7:8]),
        jnp.where(zero, other1[:, 0:1], other1[:, 8:9]),
        low_half,
    )
    inner = call(
        inner_kernel,
        "inner",
        flops * 5 // 6,
        (place, cot, field, other1, *weights),
        [half, half, part, part, shape((6912, 256), BF), shape((6912, 256), BF)],
        own_scratch + [pltpu.SemaphoreType.DMA((2,))],
        38,
        (4, 5),
    )
    inner, weights = inner[:4], inner[4:]
    inner_hidden, beside = lax.optimization_barrier((inner[0], other1))
    (chip,) = call(
        chip_kernel,
        "chip",
        flops // 8,
        (place, cot, field, beside),
        [shape((4, 18, 32, 768), BF)],
        [],
        12,
    )
    inner_hidden, chip = lax.optimization_barrier((inner_hidden, chip))
    inner = (inner_hidden, *inner[1:])
    hidden, pre_grad, sent2 = call(
        outer_kernel,
        "outer",
        flops // 6,
        (place, near1, far1, *inner, *weights),
        [grid, grid, shape((4, 9, 32, 256), BF)],
        edge_scratch,
        24,
    )
    edges = swap_cores(
        jnp.where(
            zero,
            jnp.stack([near1[0, 0:8], far1[0, 0:8]]),
            jnp.stack([near1[1, 0:8], far1[1, 0:8]]),
        )
    )
    other2 = swap_cores(sent2)
    near2, far2 = swap_slabs(
        hidden,
        pre_grad,
        jnp.where(zero, other2[:, 8:9], other2[:, 7:8]),
        jnp.where(zero, other2[:, 0:1], other2[:, 8:9]),
        low_half,
    )
    own1, *sent1, sides, turned, local = call(
        weight_kernel,
        "weight_terms",
        flops * 4 // 9,
        (place, chip, near1, far1, edges, hidden, pre_grad, other2),
        [shape((8, 32, 768), BF)] * 4
        + [shape((2, 18, 32, 768), BF), shape((256, 2048), BF), shape((2048, 256), BF)],
        [pltpu.VMEM((256, 3072), BF), pltpu.VMEM((4, 256, 768), BF)],
        26,
    )
    got1 = hop((sent1[0], sent1[2], sent1[1]), 0)
    turned, local, near2, far2 = lax.optimization_barrier((turned, local, near2, far2))
    own2, *sent2 = call(
        weight_rest_kernel,
        "weight_terms_rest",
        flops * 5 // 9,
        (place, chip, sides, turned, local),
        [shape((8, 32, 960), BF)] * 4,
        [pltpu.VMEM((256, 3840), BF), pltpu.VMEM((4, 256, 960), BF)],
        26,
    )
    got2 = hop((sent2[0], sent2[2], sent2[1]), 0)
    hidden, pre_grad, other2, own2, *got1 = lax.optimization_barrier(
        (hidden, pre_grad, other2, own2, *got1)
    )
    last = call(
        last_inner_kernel,
        "outputs_inner",
        flops * 5 // 6,
        (place, hidden, pre_grad, other2, field, cot, *weights),
        [half, half, part, part],
        own_scratch,
        26,
    )
    output, field_grad = call(
        last_outer_kernel,
        "outputs_outer",
        flops // 6,
        (place, near2, far2, *last, field, cot, *weights),
        [grid, grid],
        edge_scratch,
        24,
    )
    own2, output, field_grad = lax.optimization_barrier((own2, output, field_grad))
    first_grad, second_grad = reduce_tiles(place, (own1, *got1, own2, *got2), core)
    return output[None], field_grad[None], first_grad, second_grad


def solution(mesh):
    placed = P("dp", "px", "py", None, None)
    return jax.shard_map(
        body,
        mesh=mesh,
        in_specs=(placed, placed, P(), P()),
        out_specs=(placed, placed, P("dp", ("px", "py")), P("dp", ("px", "py"))),
        check_vma=False,
    )
```

```python
import jax
import jax.numpy as jnp
from jax import lax
from jax.experimental import pallas as pl
from jax.experimental.pallas import tpu as pltpu
from jax.sharding import PartitionSpec as P

BF = jnp.bfloat16
F32 = jnp.float32
ALL = ("dp", "px", "py")
X, Y, Z = 0, 1, 2
ORDER = ((X, Y, Z), (Y, Z, X))
EARLY, LATE = (0, 3, 5, 8), (1, 2, 4, 6, 7)
LANES = 896


def device(x, y, z, core):
    x, y, z = x % 4, y % 4, z % 4
    return (y * 2 + z // 2) * 16 + (x * 2 + z % 2) * 2 + core


def hop_pairs(stage, distance):
    pairs = []
    for core in range(2):
        step = [0, 0, 0]
        step[ORDER[core][stage]] = distance
        for x in range(4):
            for y in range(4):
                for z in range(4):
                    pairs.append(
                        (
                            device(x, y, z, core),
                            device(x + step[0], y + step[1], z + step[2], core),
                        )
                    )
    return pairs


def shifted(block):
    wide = block.astype(F32)
    place = lax.broadcasted_iota(jnp.int32, wide.shape, 1)
    low = jnp.where(place == 0, 0.0, pltpu.roll(wide, 1, 1)).astype(BF)
    high = jnp.where(place == 31, 0.0, pltpu.roll(wide, 31, 1)).astype(BF)
    return low, high


def put(stack, row, start, block, flip):
    low, high = shifted(block)
    if flip:
        low, high = high, low
    rows = pl.ds(start, block.shape[0])
    stack[row, rows, :, 0:256] = low
    stack[row, rows, :, 256:512] = block
    stack[row, rows, :, 512:768] = high


def put_own(stack, slab, start, own, flip):
    def step(i, _):
        put(stack, i + slab, start, own[i], flip)
        return 0

    lax.fori_loop(0, own.shape[0], step, 0)


def put_faces(stack, core, slab, count, other, at_first, at_second, flip):
    at = jnp.where(core == 0, at_first, at_second)
    row = jnp.where(core == 0, 9, 0)

    def step(i, _):
        put(stack, i + slab, row, other[i, pl.ds(at, 1)], flip)
        stack[i + slab, pl.ds(9 - row, 1)] = jnp.zeros((1, 32, 768), BF)
        return 0

    lax.fori_loop(0, count, step, 0)


def put_halo(stack, core, slab, halo, which, flip):
    row = jnp.where(core == 0, 9, 0)
    put(stack, slab, 1, halo[which, 0:8], flip)
    put(stack, slab, row, halo[which, 8:9], flip)
    stack[slab, pl.ds(9 - row, 1)] = jnp.zeros((1, 32, 768), BF)


def term_of(rows, weight, k, back):
    if not back:
        return jnp.dot(rows, weight[k * 768 : (k + 1) * 768], preferred_element_type=F32)
    term = None
    for c in range(3):
        part = lax.dot_general(
            rows[:, c * 256 : (c + 1) * 256],
            weight[(k * 3 + c) * 256 : (k * 3 + c + 1) * 256],
            (((1,), (1,)), ((), ())),
            preferred_element_type=F32,
        )
        term = part if term is None else term + part
    return term


def conv_own(total, stack, weight, back):
    for a in (1, 0, 2):
        step = 1 - a if back else a - 1
        count = 4 - abs(step)
        to = max(0, -step)
        for b in range(3):
            at = 2 - b if back else b
            rows = stack[to + step : to + step + count, at : at + 8].reshape(count * 256, 768)
            term = term_of(rows, weight, a * 3 + b, back)
            span = slice(to * 256, (to + count) * 256)
            if a == 1 and b == 0:
                total[span] = term
            else:
                total[span] += term


def conv_edges(part, stack, weight, back):
    sums = []
    for side in range(2):
        a = 2 * side if not back else 2 - 2 * side
        total = part[side]
        for b in range(3):
            at = 2 - b if back else b
            rows = stack[side, at : at + 8].reshape(256, 768)
            total = total + term_of(rows, weight, a * 3 + b, back)
        sums.append(total)
    return sums


def gelu_and_slope(v):
    scale = 0.7978845608028654
    square = v * v
    t = jnp.tanh(scale * (v + 0.044715 * (square * v)))
    half = 0.5 * (1.0 + t)
    slope = half + 0.5 * v * (1.0 - t * t) * (scale * (1.0 + 3.0 * 0.044715 * square))
    return v * half, slope


def near_side(place):
    return 1 - lax.rem(place[3], 2)


def pack_kernel(place, cot, field, send, arrived):
    core = place[0]

    def pack(whole, row):
        copies = [
            pltpu.make_async_copy(whole, send.at[:, 0:8], arrived.at[0]),
            pltpu.make_async_copy(row, send.at[:, 8:9], arrived.at[1]),
        ]
        for copy in copies:
            copy.start()
        for copy in copies:
            copy.wait()

    @pl.when(core == 0)
    def _():
        pack(cot, field.at[:, 7:8])

    @pl.when(core == 1)
    def _():
        pack(field, cot.at[:, 0:1])


def inner_kernel(
    place, cot, field, other, first_hbm, second_hbm, hidden, pre_grad, part_pre, part_grad,
    first_w, second_w, stack, back, pre, grad, arrived,
):
    core = place[0]
    copies = [
        pltpu.make_async_copy(first_hbm, first_w, arrived.at[0]),
        pltpu.make_async_copy(second_hbm, second_w, arrived.at[1]),
    ]
    for copy in copies:
        copy.start()
    put_own(stack, 0, 1, field, False)
    put_faces(stack, core, 0, 4, other, 0, 8, False)
    put_own(back, 0, 1, cot, True)
    put_faces(back, core, 0, 4, other, 8, 7, True)
    for copy in copies:
        copy.wait()
    conv_own(pre, stack, first_w, False)
    conv_own(grad, back, second_w, True)
    for i in range(2):
        rows = slice((i + 1) * 256, (i + 2) * 256)
        value, slope = gelu_and_slope(pre[rows])
        hidden[i] = value.astype(BF).reshape(8, 32, 256)
        pre_grad[i] = (grad[rows] * slope).astype(BF).reshape(8, 32, 256)
        rows = slice(i * 768, i * 768 + 256)
        part_pre[i] = pre[rows]
        part_grad[i] = grad[rows]


def outer_kernel(
    place, near, far, inner_hidden, inner_grad, part_pre, part_grad, first_w, second_w,
    hidden, pre_grad, send, stack, back,
):
    core = place[0]
    side = near_side(place)
    put_halo(stack, core, side, near, 1, False)
    put_halo(stack, core, 1 - side, far, 1, False)
    put_halo(back, core, side, near, 0, True)
    put_halo(back, core, 1 - side, far, 0, True)
    pre = conv_edges(part_pre, stack, first_w, False)
    grad = conv_edges(part_grad, back, second_w, True)
    for i in range(2):
        value, slope = gelu_and_slope(pre[i])
        hidden[3 * i] = value.astype(BF).reshape(8, 32, 256)
        pre_grad[3 * i] = (grad[i] * slope).astype(BF).reshape(8, 32, 256)
        hidden[1 + i] = inner_hidden[i]
        pre_grad[1 + i] = inner_grad[i]

    @pl.when(core == 0)
    def _():
        send[:, 0:8] = hidden[...]
        send[:, 8:9] = pre_grad[:, 7:8]

    @pl.when(core == 1)
    def _():
        send[:, 0:8] = pre_grad[...]
        send[:, 8:9] = hidden[:, 0:1]


def last_inner_kernel(
    place, hid, pre_grad, other, field, cot, first_w, second_w,
    out, field_grad, part_out, part_grad, stack, back, total, grad,
):
    core = place[0]
    put_own(stack, 0, 1, hid, False)
    put_faces(stack, core, 0, 4, other, 8, 7, False)
    put_own(back, 0, 1, pre_grad, True)
    put_faces(back, core, 0, 4, other, 0, 8, True)
    conv_own(total, stack, second_w, False)
    conv_own(grad, back, first_w, True)
    for i in range(2):
        rows = slice((i + 1) * 256, (i + 2) * 256)
        one = field[i + 1].astype(F32).reshape(256, 256) + total[rows]
        out[i] = one.astype(BF).reshape(8, 32, 256)
        two = cot[i + 1].astype(F32).reshape(256, 256) + grad[rows]
        field_grad[i] = two.astype(BF).reshape(8, 32, 256)
        rows = slice(i * 768, i * 768 + 256)
        part_out[i] = total[rows]
        part_grad[i] = grad[rows]


def last_outer_kernel(
    place, near, far, inner_out, inner_grad, part_out, part_grad, field, cot, first_w, second_w,
    out, field_grad, stack, back,
):
    core = place[0]
    side = near_side(place)
    put_halo(stack, core, side, near, 0, False)
    put_halo(stack, core, 1 - side, far, 0, False)
    put_halo(back, core, side, near, 1, True)
    put_halo(back, core, 1 - side, far, 1, True)
    total = conv_edges(part_out, stack, second_w, False)
    grad = conv_edges(part_grad, back, first_w, True)
    for i in range(2):
        one = field[3 * i].astype(F32).reshape(256, 256) + total[i]
        out[3 * i] = one.astype(BF).reshape(8, 32, 256)
        two = cot[3 * i].astype(F32).reshape(256, 256) + grad[i]
        field_grad[3 * i] = two.astype(BF).reshape(8, 32, 256)
        out[1 + i] = inner_out[i]
        field_grad[1 + i] = inner_grad[i]


def chip_kernel(place, cot, field, other, chip):
    core = place[0]

    def fill(value, half, flip):
        put_own(chip, 0, 1 + 8 * half, value, flip)

        def step(i, _):
            put(chip, i, 9 - 8 * half, other[i, 0:8], flip)
            chip[i, 0:1] = jnp.zeros((1, 32, 768), BF)
            chip[i, 17:18] = jnp.zeros((1, 32, 768), BF)
            return 0

        lax.fori_loop(0, 4, step, 0)

    @pl.when(core == 0)
    def _():
        fill(field, 0, False)

    @pl.when(core == 1)
    def _():
        fill(cot, 1, True)


def windows(chip, sides, a, b):
    rows = slice(b, b + 16)
    if a == 1:
        return [(0, chip[0:4, rows].reshape(2048, 768))]
    if a == 0:
        return [
            (0, sides[0, rows].reshape(512, 768)),
            (512, chip[0:3, rows].reshape(1536, 768)),
        ]
    return [
        (0, chip[1:4, rows].reshape(1536, 768)),
        (1536, sides[1, rows].reshape(512, 768)),
    ]


def terms_of_first(flat, steps, chip, sides, turned):
    for j, k in enumerate(steps):
        term = None
        for at, rows in windows(chip, sides, k // 3, k % 3):
            part = jnp.dot(turned[:, at : at + rows.shape[0]], rows, preferred_element_type=F32)
            term = part if term is None else term + part
        flat[:, j * 768 : (j + 1) * 768] = (term * 0.125).astype(BF)


def terms_of_second(flat, steps, chip, sides, local):
    for j, k in enumerate(steps):
        term = None
        for at, rows in windows(chip, sides, 2 - k // 3, 2 - k % 3):
            part = lax.dot_general(
                rows,
                local[at : at + rows.shape[0]],
                (((0,), (0,)), ((), ())),
                preferred_element_type=F32,
            )
            term = part if term is None else term + part
        term = (term * 0.125).astype(BF)
        for c in range(3):
            start = (j * 3 + c) * 256
            flat[:, start : start + 256] = term[c * 256 : (c + 1) * 256]


def give_tiles(place, flat, tiles, width, outs):
    for k in range(4):
        tiles[k] = flat[:, k * width : (k + 1) * width]
    x, y = place[1], place[2]
    zero = place[0] == 0
    for first, ref in enumerate(outs):
        for i in range(8):
            to_x = jnp.where(zero, lax.rem(x + first, 4), i // 2)
            to_y = jnp.where(zero, i // 2, lax.rem(y + first, 4))
            to_px = to_x * 2 + i % 2
            ref[i] = tiles[to_y, pl.ds(pl.multiple_of(to_px * 32, 32), 32), :]


def weight_kernel(
    place, chip, near1, far1, edges, hid, pre_grad, other2,
    own, send1, send2, send3, sides, turned, local, flat, tiles,
):
    core = place[0]
    near = near_side(place)

    def fill(which, half, flip):
        mine, others = 1 + 8 * half, 9 - 8 * half
        put(sides, near, mine, near1[which, 0:8], flip)
        put(sides, 1 - near, mine, far1[which, 0:8], flip)
        put(sides, near, others, edges[0], flip)
        put(sides, 1 - near, others, edges[1], flip)
        for i in range(2):
            sides[i, 0:1] = jnp.zeros((1, 32, 768), BF)
            sides[i, 17:18] = jnp.zeros((1, 32, 768), BF)

    @pl.when(core == 0)
    def _():
        fill(1, 0, False)
        for i in range(4):
            turned[:, i * 512 : i * 512 + 256] = pre_grad[i].reshape(256, 256).T
            turned[:, i * 512 + 256 : i * 512 + 512] = other2[i, 0:8].reshape(256, 256).T
        terms_of_first(flat, EARLY, chip, sides, turned)

    @pl.when(core == 1)
    def _():
        fill(0, 1, True)
        for i in range(4):
            local[i * 512 : i * 512 + 256] = other2[i, 0:8].reshape(256, 256)
            local[i * 512 + 256 : i * 512 + 512] = hid[i].reshape(256, 256)
        terms_of_second(flat, EARLY, chip, sides, local)

    give_tiles(place, flat, tiles, 768, (own, send1, send2, send3))


def weight_rest_kernel(
    place, chip, sides, turned, local, own, send1, send2, send3, flat, tiles
):
    core = place[0]

    @pl.when(core == 0)
    def _():
        terms_of_first(flat, LATE, chip, sides, turned)

    @pl.when(core == 1)
    def _():
        terms_of_second(flat, LATE, chip, sides, local)

    give_tiles(place, flat, tiles, 960, (own, send1, send2, send3))


def sum_kernel(place, *refs):
    ins, (keep, send1, send2, send3, whole, tiles) = refs[:8], refs[8:]
    core, x, y, z = place[0], place[1], place[2], place[3]
    zero = core == 0

    def add(refs, i):
        total = refs[0][i].astype(F32)
        for ref in refs[1:]:
            total = total + ref[i].astype(F32)
        return total

    def join(i, row):
        early, late = add(ins[0:4], i), add(ins[4:8], i)
        before = (0, 576, 384, 960)[row]
        if before:
            whole[i, :, 0:before] = late[:, 0:before]
        whole[i, :, before : before + 768] = early
        if before < 960:
            whole[i, :, before + 768 : 1728] = late[:, before:960]

    @pl.when(zero)
    def _():
        for i in range(8):
            join(i, i // 2)

    for row in range(4):

        @pl.when(jnp.logical_and(core == 1, y == row))
        def _():
            for i in range(8):
                join(i, row)

    for i in range(8):
        whole[i, :, 1728:1792] = jnp.zeros((32, 64), F32)
        for high in range(2):
            tiles[i * 2 + high] = whole[i, :, high * 864 : high * 864 + LANES]
    for second, ref in enumerate((keep, send1, send2, send3)):
        for third in range(4):
            to_z = lax.rem(z + jnp.where(zero, third, second), 4)
            other = jnp.where(zero, lax.rem(y + second, 4), lax.rem(x + third, 4))
            at = (other * 2 + lax.rem(to_z, 2)) * 2 + lax.div(to_z, 2)
            ref[third] = tiles[at].astype(ref.dtype)


def call(kernel, name, flops, args, outs, scratch, limit, far=()):
    whole = pl.BlockSpec(memory_space=pltpu.VMEM)
    return pl.pallas_call(
        kernel,
        name=name,
        out_shape=outs,
        in_specs=[pl.BlockSpec(memory_space=pltpu.SMEM)]
        + [
            pl.BlockSpec(memory_space=pltpu.HBM) if i in far else whole
            for i in range(1, len(args))
        ],
        out_specs=[whole] * len(outs),
        scratch_shapes=scratch,
        compiler_params=pltpu.CompilerParams(vmem_limit_bytes=limit * 2**20),
        cost_estimate=pl.CostEstimate(
            flops=flops, bytes_accessed=8 * 2**20, transcendentals=0
        ),
    )(*args)


def swap_cores(value):
    return lax.ppermute(value, "py", [(0, 1), (1, 0)])


def swap_slabs(first, second, first_face, second_face, low_half):
    count = lax.axis_size("px")
    near = [(i, i ^ 1) for i in range(count)]
    far = [(i, i + 1 if i % 2 else i - 1) for i in range(1, count - 1)]

    def slab(i):
        return jnp.stack(
            [
                jnp.concatenate([first[i], first_face[i]], axis=0),
                jnp.concatenate([second[i], second_face[i]], axis=0),
            ]
        )

    low, high = slab(0), slab(3)
    got_far = lax.ppermute(jnp.where(low_half, low, high), "px", far)
    got_near = lax.ppermute(jnp.where(low_half, high, low), "px", near)
    return got_near, got_far


def hop(parts, stage):
    return [
        lax.ppermute(part, ALL, hop_pairs(stage, distance))
        for part, distance in zip(parts, (1, 3, 2))
    ]


def reduce_tiles(place, halves, core):
    shape = jax.ShapeDtypeStruct
    keep, send1, send2, send3 = call(
        sum_kernel,
        "sum",
        0,
        (place, *halves),
        [shape((4, 32, LANES), F32)] + [shape((4, 32, LANES), BF)] * 3,
        [pltpu.VMEM((8, 32, 1792), F32), pltpu.VMEM((16, 32, LANES), F32)],
        18,
    )
    total = keep
    for part in hop((send1, send3, send2), 1):
        total = total + part.astype(F32)
    got = hop([total[d] for d in (1, 3, 2)], 2)
    total = total[0] + got[0] + got[1] + got[2]
    keep = jnp.where(core == 0, total[:16], total[16:])
    give = jnp.where(core == 0, total[16:], total[:16])
    other = swap_cores(give)
    first = jnp.where(core == 0, keep, other)[:, :864]
    second = jnp.where(core == 0, other, keep)[:, :864]
    return first.T, second.T


def body(fields, cotangent, first_weight, second_weight):
    shape = jax.ShapeDtypeStruct
    core = lax.axis_index("py")
    dp, px = lax.axis_index("dp"), lax.axis_index("px")
    zero = core == 0
    two = jnp.int32(2)
    place = jnp.stack(
        [core, lax.div(px, two), lax.div(dp, two), lax.rem(dp, two) * 2 + lax.rem(px, two)]
    )
    field, cot = fields[0], cotangent[0]
    grid, half = shape((4, 8, 32, 256), BF), shape((2, 8, 32, 256), BF)

    part = shape((2, 256, 256), F32)
    low_half = lax.rem(px, two) == 0
    own_scratch = [pltpu.VMEM((4, 10, 32, 768), BF)] * 2 + [pltpu.VMEM((1024, 256), F32)] * 2
    edge_scratch = [pltpu.VMEM((2, 10, 32, 768), BF)] * 2
    weights = (first_weight, second_weight)
    flops = 2 * 2 * 1024 * 6912 * 256
    (sent1,) = call(
        pack_kernel,
        "pack",
        0,
        (core.astype(jnp.int32).reshape(1), cot, field),
        [shape((4, 9, 32, 256), BF)],
        [pltpu.SemaphoreType.DMA((2,))],
        40,
        (1, 2),
    )
    other1 = swap_cores(sent1)
    near1, far1 = swap_slabs(
        cot,
        field,
        jnp.where(zero, other1[:, 8:9], other1[:, 7:8]),
        jnp.where(zero, other1[:, 0:1], other1[:, 8:9]),
        low_half,
    )
    inner = call(
        inner_kernel,
        "inner",
        flops * 5 // 6,
        (place, cot, field, other1, *weights),
        [half, half, part, part, shape((6912, 256), BF), shape((6912, 256), BF)],
        own_scratch + [pltpu.SemaphoreType.DMA((2,))],
        38,
        (4, 5),
    )
    inner, weights = inner[:4], inner[4:]
    inner_hidden, beside = lax.optimization_barrier((inner[0], other1))
    (chip,) = call(
        chip_kernel,
        "chip",
        flops // 8,
        (place, cot, field, beside),
        [shape((4, 18, 32, 768), BF)],
        [],
        12,
    )
    inner_hidden, chip = lax.optimization_barrier((inner_hidden, chip))
    inner = (inner_hidden, *inner[1:])
    hidden, pre_grad, sent2 = call(
        outer_kernel,
        "outer",
        flops // 6,
        (place, near1, far1, *inner, *weights),
        [grid, grid, shape((4, 9, 32, 256), BF)],
        edge_scratch,
        24,
    )
    edges = swap_cores(
        jnp.where(
            zero,
            jnp.stack([near1[0, 0:8], far1[0, 0:8]]),
            jnp.stack([near1[1, 0:8], far1[1, 0:8]]),
        )
    )
    other2 = swap_cores(sent2)
    near2, far2 = swap_slabs(
        hidden,
        pre_grad,
        jnp.where(zero, other2[:, 8:9], other2[:, 7:8]),
        jnp.where(zero, other2[:, 0:1], other2[:, 8:9]),
        low_half,
    )
    own1, *sent1, sides, turned, local = call(
        weight_kernel,
        "weight_terms",
        flops * 4 // 9,
        (place, chip, near1, far1, edges, hidden, pre_grad, other2),
        [shape((8, 32, 768), BF)] * 4
        + [shape((2, 18, 32, 768), BF), shape((256, 2048), BF), shape((2048, 256), BF)],
        [pltpu.VMEM((256, 3072), BF), pltpu.VMEM((4, 256, 768), BF)],
        26,
    )
    got1 = hop((sent1[0], sent1[2], sent1[1]), 0)
    own2, *sent2 = call(
        weight_rest_kernel,
        "weight_terms_rest",
        flops * 5 // 9,
        (place, chip, sides, turned, local),
        [shape((8, 32, 960), BF)] * 4,
        [pltpu.VMEM((256, 3840), BF), pltpu.VMEM((4, 256, 960), BF)],
        26,
    )
    got2 = hop((sent2[0], sent2[2], sent2[1]), 0)
    hidden, pre_grad, other2, own2, *got1 = lax.optimization_barrier(
        (hidden, pre_grad, other2, own2, *got1)
    )
    last = call(
        last_inner_kernel,
        "outputs_inner",
        flops * 5 // 6,
        (place, hidden, pre_grad, other2, field, cot, *weights),
        [half, half, part, part],
        own_scratch,
        26,
    )
    output, field_grad = call(
        last_outer_kernel,
        "outputs_outer",
        flops // 6,
        (place, near2, far2, *last, field, cot, *weights),
        [grid, grid],
        edge_scratch,
        24,
    )
    own2, output, field_grad = lax.optimization_barrier((own2, output, field_grad))
    first_grad, second_grad = reduce_tiles(place, (own1, *got1, own2, *got2), core)
    return output[None], field_grad[None], first_grad, second_grad


def solution(mesh):
    placed = P("dp", "px", "py", None, None)
    return jax.shard_map(
        body,
        mesh=mesh,
        in_specs=(placed, placed, P(), P()),
        out_specs=(placed, placed, P("dp", ("px", "py")), P("dp", ("px", "py"))),
        check_vma=False,
    )
```

```python
import jax
import jax.numpy as jnp
from jax import lax
from jax.experimental import pallas as pl
from jax.experimental.pallas import tpu as pltpu
from jax.sharding import PartitionSpec as P

BF = jnp.bfloat16
F32 = jnp.float32
ALL = ("dp", "px", "py")
X, Y, Z = 0, 1, 2
ORDER = ((X, Y, Z), (Y, Z, X))
EARLY, LATE = (0, 3, 5, 8), (1, 2, 4, 6, 7)
LANES = 896


def device(x, y, z, core):
    x, y, z = x % 4, y % 4, z % 4
    return (y * 2 + z // 2) * 16 + (x * 2 + z % 2) * 2 + core


def hop_pairs(stage, distance):
    pairs = []
    for core in range(2):
        step = [0, 0, 0]
        step[ORDER[core][stage]] = distance
        for x in range(4):
            for y in range(4):
                for z in range(4):
                    pairs.append(
                        (
                            device(x, y, z, core),
                            device(x + step[0], y + step[1], z + step[2], core),
                        )
                    )
    return pairs


def shifted(block):
    wide = block.astype(F32)
    place = lax.broadcasted_iota(jnp.int32, wide.shape, 1)
    low = jnp.where(place == 0, 0.0, pltpu.roll(wide, 1, 1)).astype(BF)
    high = jnp.where(place == 31, 0.0, pltpu.roll(wide, 31, 1)).astype(BF)
    return low, high


def put(stack, row, start, block, flip):
    low, high = shifted(block)
    if flip:
        low, high = high, low
    rows = pl.ds(start, block.shape[0])
    stack[row, rows, :, 0:256] = low
    stack[row, rows, :, 256:512] = block
    stack[row, rows, :, 512:768] = high


def put_own(stack, slab, start, own, flip):
    def step(i, _):
        put(stack, i + slab, start, own[i], flip)
        return 0

    lax.fori_loop(0, own.shape[0], step, 0)


def put_faces(stack, core, slab, count, other, at_first, at_second, flip):
    at = jnp.where(core == 0, at_first, at_second)
    row = jnp.where(core == 0, 9, 0)

    def step(i, _):
        put(stack, i + slab, row, other[i, pl.ds(at, 1)], flip)
        stack[i + slab, pl.ds(9 - row, 1)] = jnp.zeros((1, 32, 768), BF)
        return 0

    lax.fori_loop(0, count, step, 0)


def put_halo(stack, core, slab, halo, which, flip):
    row = jnp.where(core == 0, 9, 0)
    put(stack, slab, 1, halo[which, 0:8], flip)
    put(stack, slab, row, halo[which, 8:9], flip)
    stack[slab, pl.ds(9 - row, 1)] = jnp.zeros((1, 32, 768), BF)


def term_of(rows, weight, k, back):
    if not back:
        return jnp.dot(rows, weight[k * 768 : (k + 1) * 768], preferred_element_type=F32)
    term = None
    for c in range(3):
        part = lax.dot_general(
            rows[:, c * 256 : (c + 1) * 256],
            weight[(k * 3 + c) * 256 : (k * 3 + c + 1) * 256],
            (((1,), (1,)), ((), ())),
            preferred_element_type=F32,
        )
        term = part if term is None else term + part
    return term


def conv_own(total, stack, weight, back):
    for a in (1, 0, 2):
        step = 1 - a if back else a - 1
        count = 4 - abs(step)
        to = max(0, -step)
        for b in range(3):
            at = 2 - b if back else b
            rows = stack[to + step : to + step + count, at : at + 8].reshape(count * 256, 768)
            term = term_of(rows, weight, a * 3 + b, back)
            span = slice(to * 256, (to + count) * 256)
            if a == 1 and b == 0:
                total[span] = term
            else:
                total[span] += term


def conv_edges(part, stack, weight, back):
    sums = []
    for side in range(2):
        a = 2 * side if not back else 2 - 2 * side
        total = part[side]
        for b in range(3):
            at = 2 - b if back else b
            rows = stack[side, at : at + 8].reshape(256, 768)
            total = total + term_of(rows, weight, a * 3 + b, back)
        sums.append(total)
    return sums


def gelu_and_slope(v):
    scale = 0.7978845608028654
    square = v * v
    t = jnp.tanh(scale * (v + 0.044715 * (square * v)))
    half = 0.5 * (1.0 + t)
    slope = half + 0.5 * v * (1.0 - t * t) * (scale * (1.0 + 3.0 * 0.044715 * square))
    return v * half, slope


def near_side(place):
    return 1 - lax.rem(place[3], 2)


def pack_kernel(place, cot, field, send, edges, arrived):
    core = place[0]
    slabs = [
        pltpu.make_async_copy(whole.at[3 * i], edges.at[i, j], arrived.at[2 + 2 * i + j])
        for i in range(2)
        for j, whole in enumerate((cot, field))
    ]
    for copy in slabs:
        copy.start()

    def pack(whole, row):
        copies = [
            pltpu.make_async_copy(whole, send.at[:, 0:8], arrived.at[0]),
            pltpu.make_async_copy(row, send.at[:, 8:9], arrived.at[1]),
        ]
        for copy in copies:
            copy.start()
        for copy in copies:
            copy.wait()

    @pl.when(core == 0)
    def _():
        pack(cot, field.at[:, 7:8])

    @pl.when(core == 1)
    def _():
        pack(field, cot.at[:, 0:1])

    for copy in slabs:
        copy.wait()


def inner_kernel(
    place, cot, field, other, first_hbm, second_hbm, hidden, pre_grad, part_pre, part_grad,
    first_w, second_w, stack, back, pre, grad, arrived,
):
    core = place[0]
    copies = [
        pltpu.make_async_copy(first_hbm, first_w, arrived.at[0]),
        pltpu.make_async_copy(second_hbm, second_w, arrived.at[1]),
    ]
    for copy in copies:
        copy.start()
    put_own(stack, 0, 1, field, False)
    put_faces(stack, core, 0, 4, other, 0, 8, False)
    put_own(back, 0, 1, cot, True)
    put_faces(back, core, 0, 4, other, 8, 7, True)
    for copy in copies:
        copy.wait()
    conv_own(pre, stack, first_w, False)
    conv_own(grad, back, second_w, True)
    for i in range(2):
        rows = slice((i + 1) * 256, (i + 2) * 256)
        value, slope = gelu_and_slope(pre[rows])
        hidden[i] = value.astype(BF).reshape(8, 32, 256)
        pre_grad[i] = (grad[rows] * slope).astype(BF).reshape(8, 32, 256)
        rows = slice(i * 768, i * 768 + 256)
        part_pre[i] = pre[rows]
        part_grad[i] = grad[rows]


def outer_kernel(
    place, near, far, inner_hidden, inner_grad, part_pre, part_grad, first_w, second_w,
    hidden, pre_grad, send, stack, back,
):
    core = place[0]
    side = near_side(place)
    put_halo(stack, core, side, near, 1, False)
    put_halo(stack, core, 1 - side, far, 1, False)
    put_halo(back, core, side, near, 0, True)
    put_halo(back, core, 1 - side, far, 0, True)
    pre = conv_edges(part_pre, stack, first_w, False)
    grad = conv_edges(part_grad, back, second_w, True)
    for i in range(2):
        value, slope = gelu_and_slope(pre[i])
        hidden[3 * i] = value.astype(BF).reshape(8, 32, 256)
        pre_grad[3 * i] = (grad[i] * slope).astype(BF).reshape(8, 32, 256)
        hidden[1 + i] = inner_hidden[i]
        pre_grad[1 + i] = inner_grad[i]

    @pl.when(core == 0)
    def _():
        send[:, 0:8] = hidden[...]
        send[:, 8:9] = pre_grad[:, 7:8]

    @pl.when(core == 1)
    def _():
        send[:, 0:8] = pre_grad[...]
        send[:, 8:9] = hidden[:, 0:1]


def last_inner_kernel(
    place, hid, pre_grad, other, field, cot, first_w, second_w,
    out, field_grad, part_out, part_grad, stack, back, total, grad,
):
    core = place[0]
    put_own(stack, 0, 1, hid, False)
    put_faces(stack, core, 0, 4, other, 8, 7, False)
    put_own(back, 0, 1, pre_grad, True)
    put_faces(back, core, 0, 4, other, 0, 8, True)
    conv_own(total, stack, second_w, False)
    conv_own(grad, back, first_w, True)
    for i in range(2):
        rows = slice((i + 1) * 256, (i + 2) * 256)
        one = field[i + 1].astype(F32).reshape(256, 256) + total[rows]
        out[i] = one.astype(BF).reshape(8, 32, 256)
        two = cot[i + 1].astype(F32).reshape(256, 256) + grad[rows]
        field_grad[i] = two.astype(BF).reshape(8, 32, 256)
        rows = slice(i * 768, i * 768 + 256)
        part_out[i] = total[rows]
        part_grad[i] = grad[rows]


def last_outer_kernel(
    place, near, far, inner_out, inner_grad, part_out, part_grad, field, cot, first_w, second_w,
    out, field_grad, stack, back,
):
    core = place[0]
    side = near_side(place)
    put_halo(stack, core, side, near, 0, False)
    put_halo(stack, core, 1 - side, far, 0, False)
    put_halo(back, core, side, near, 1, True)
    put_halo(back, core, 1 - side, far, 1, True)
    total = conv_edges(part_out, stack, second_w, False)
    grad = conv_edges(part_grad, back, first_w, True)
    for i in range(2):
        one = field[3 * i].astype(F32).reshape(256, 256) + total[i]
        out[3 * i] = one.astype(BF).reshape(8, 32, 256)
        two = cot[3 * i].astype(F32).reshape(256, 256) + grad[i]
        field_grad[3 * i] = two.astype(BF).reshape(8, 32, 256)
        out[1 + i] = inner_out[i]
        field_grad[1 + i] = inner_grad[i]


def chip_kernel(place, cot, field, other, chip):
    core = place[0]

    def fill(value, half, flip):
        put_own(chip, 0, 1 + 8 * half, value, flip)

        def step(i, _):
            put(chip, i, 9 - 8 * half, other[i, 0:8], flip)
            chip[i, 0:1] = jnp.zeros((1, 32, 768), BF)
            chip[i, 17:18] = jnp.zeros((1, 32, 768), BF)
            return 0

        lax.fori_loop(0, 4, step, 0)

    @pl.when(core == 0)
    def _():
        fill(field, 0, False)

    @pl.when(core == 1)
    def _():
        fill(cot, 1, True)


def windows(chip, sides, a, b):
    rows = slice(b, b + 16)
    if a == 1:
        return [(0, chip[0:4, rows].reshape(2048, 768))]
    if a == 0:
        return [
            (0, sides[0, rows].reshape(512, 768)),
            (512, chip[0:3, rows].reshape(1536, 768)),
        ]
    return [
        (0, chip[1:4, rows].reshape(1536, 768)),
        (1536, sides[1, rows].reshape(512, 768)),
    ]


def terms_of_first(flat, steps, chip, sides, turned):
    for j, k in enumerate(steps):
        term = None
        for at, rows in windows(chip, sides, k // 3, k % 3):
            part = jnp.dot(turned[:, at : at + rows.shape[0]], rows, preferred_element_type=F32)
            term = part if term is None else term + part
        flat[:, j * 768 : (j + 1) * 768] = (term * 0.125).astype(BF)


def terms_of_second(flat, steps, chip, sides, local):
    for j, k in enumerate(steps):
        term = None
        for at, rows in windows(chip, sides, 2 - k // 3, 2 - k % 3):
            part = lax.dot_general(
                rows,
                local[at : at + rows.shape[0]],
                (((0,), (0,)), ((), ())),
                preferred_element_type=F32,
            )
            term = part if term is None else term + part
        term = (term * 0.125).astype(BF)
        for c in range(3):
            start = (j * 3 + c) * 256
            flat[:, start : start + 256] = term[c * 256 : (c + 1) * 256]


def give_tiles(place, flat, tiles, width, outs):
    for k in range(4):
        tiles[k] = flat[:, k * width : (k + 1) * width]
    x, y = place[1], place[2]
    zero = place[0] == 0
    for first, ref in enumerate(outs):
        for i in range(8):
            to_x = jnp.where(zero, lax.rem(x + first, 4), i // 2)
            to_y = jnp.where(zero, i // 2, lax.rem(y + first, 4))
            to_px = to_x * 2 + i % 2
            ref[i] = tiles[to_y, pl.ds(pl.multiple_of(to_px * 32, 32), 32), :]


def weight_kernel(
    place, chip, near1, far1, edges, hid, pre_grad, other2,
    own, send1, send2, send3, sides, turned, local, flat, tiles,
):
    core = place[0]
    near = near_side(place)

    def fill(which, half, flip):
        mine, others = 1 + 8 * half, 9 - 8 * half
        put(sides, near, mine, near1[which, 0:8], flip)
        put(sides, 1 - near, mine, far1[which, 0:8], flip)
        put(sides, near, others, edges[0], flip)
        put(sides, 1 - near, others, edges[1], flip)
        for i in range(2):
            sides[i, 0:1] = jnp.zeros((1, 32, 768), BF)
            sides[i, 17:18] = jnp.zeros((1, 32, 768), BF)

    @pl.when(core == 0)
    def _():
        fill(1, 0, False)
        for i in range(4):
            turned[:, i * 512 : i * 512 + 256] = pre_grad[i].reshape(256, 256).T
            turned[:, i * 512 + 256 : i * 512 + 512] = other2[i, 0:8].reshape(256, 256).T
        terms_of_first(flat, EARLY, chip, sides, turned)

    @pl.when(core == 1)
    def _():
        fill(0, 1, True)
        for i in range(4):
            local[i * 512 : i * 512 + 256] = other2[i, 0:8].reshape(256, 256)
            local[i * 512 + 256 : i * 512 + 512] = hid[i].reshape(256, 256)
        terms_of_second(flat, EARLY, chip, sides, local)

    give_tiles(place, flat, tiles, 768, (own, send1, send2, send3))


def weight_rest_kernel(
    place, chip, sides, turned, local, own, send1, send2, send3, flat, tiles
):
    core = place[0]

    @pl.when(core == 0)
    def _():
        terms_of_first(flat, LATE, chip, sides, turned)

    @pl.when(core == 1)
    def _():
        terms_of_second(flat, LATE, chip, sides, local)

    give_tiles(place, flat, tiles, 960, (own, send1, send2, send3))


def sum_kernel(place, *refs):
    ins, (keep, send1, send2, send3, whole, tiles) = refs[:8], refs[8:]
    core, x, y, z = place[0], place[1], place[2], place[3]
    zero = core == 0

    def add(refs, i):
        total = refs[0][i].astype(F32)
        for ref in refs[1:]:
            total = total + ref[i].astype(F32)
        return total

    def join(i, row):
        early, late = add(ins[0:4], i), add(ins[4:8], i)
        before = (0, 576, 384, 960)[row]
        if before:
            whole[i, :, 0:before] = late[:, 0:before]
        whole[i, :, before : before + 768] = early
        if before < 960:
            whole[i, :, before + 768 : 1728] = late[:, before:960]

    @pl.when(zero)
    def _():
        for i in range(8):
            join(i, i // 2)

    for row in range(4):

        @pl.when(jnp.logical_and(core == 1, y == row))
        def _():
            for i in range(8):
                join(i, row)

    for i in range(8):
        whole[i, :, 1728:1792] = jnp.zeros((32, 64), F32)
        for high in range(2):
            tiles[i * 2 + high] = whole[i, :, high * 864 : high * 864 + LANES]
    for second, ref in enumerate((keep, send1, send2, send3)):
        for third in range(4):
            to_z = lax.rem(z + jnp.where(zero, third, second), 4)
            other = jnp.where(zero, lax.rem(y + second, 4), lax.rem(x + third, 4))
            at = (other * 2 + lax.rem(to_z, 2)) * 2 + lax.div(to_z, 2)
            ref[third] = tiles[at].astype(ref.dtype)


def call(kernel, name, flops, args, outs, scratch, limit, far=()):
    whole = pl.BlockSpec(memory_space=pltpu.VMEM)
    return pl.pallas_call(
        kernel,
        name=name,
        out_shape=outs,
        in_specs=[pl.BlockSpec(memory_space=pltpu.SMEM)]
        + [
            pl.BlockSpec(memory_space=pltpu.HBM) if i in far else whole
            for i in range(1, len(args))
        ],
        out_specs=[whole] * len(outs),
        scratch_shapes=scratch,
        compiler_params=pltpu.CompilerParams(vmem_limit_bytes=limit * 2**20),
        cost_estimate=pl.CostEstimate(
            flops=flops, bytes_accessed=8 * 2**20, transcendentals=0
        ),
    )(*args)


def swap_cores(value):
    return lax.ppermute(value, "py", [(0, 1), (1, 0)])


def swap_slabs(first, second, first_face, second_face, low_half):
    count = lax.axis_size("px")
    near = [(i, i ^ 1) for i in range(count)]
    far = [(i, i + 1 if i % 2 else i - 1) for i in range(1, count - 1)]

    def slab(i):
        return jnp.stack(
            [
                jnp.concatenate([first[i], first_face[i]], axis=0),
                jnp.concatenate([second[i], second_face[i]], axis=0),
            ]
        )

    low, high = slab(0), slab(3)
    got_far = lax.ppermute(jnp.where(low_half, low, high), "px", far)
    got_near = lax.ppermute(jnp.where(low_half, high, low), "px", near)
    return got_near, got_far


def hop(parts, stage):
    return [
        lax.ppermute(part, ALL, hop_pairs(stage, distance))
        for part, distance in zip(parts, (1, 3, 2))
    ]


def reduce_tiles(place, halves, core):
    shape = jax.ShapeDtypeStruct
    keep, send1, send2, send3 = call(
        sum_kernel,
        "sum",
        0,
        (place, *halves),
        [shape((4, 32, LANES), F32)] + [shape((4, 32, LANES), BF)] * 3,
        [pltpu.VMEM((8, 32, 1792), F32), pltpu.VMEM((16, 32, LANES), F32)],
        18,
    )
    total = keep
    for part in hop((send1, send3, send2), 1):
        total = total + part.astype(F32)
    got = hop([total[d] for d in (1, 3, 2)], 2)
    total = total[0] + got[0] + got[1] + got[2]
    keep = jnp.where(core == 0, total[:16], total[16:])
    give = jnp.where(core == 0, total[16:], total[:16])
    other = swap_cores(give)
    first = jnp.where(core == 0, keep, other)[:, :864]
    second = jnp.where(core == 0, other, keep)[:, :864]
    return first.T, second.T


def body(fields, cotangent, first_weight, second_weight):
    shape = jax.ShapeDtypeStruct
    core = lax.axis_index("py")
    dp, px = lax.axis_index("dp"), lax.axis_index("px")
    zero = core == 0
    two = jnp.int32(2)
    place = jnp.stack(
        [core, lax.div(px, two), lax.div(dp, two), lax.rem(dp, two) * 2 + lax.rem(px, two)]
    )
    field, cot = fields[0], cotangent[0]
    grid, half = shape((4, 8, 32, 256), BF), shape((2, 8, 32, 256), BF)

    part = shape((2, 256, 256), F32)
    low_half = lax.rem(px, two) == 0
    own_scratch = [pltpu.VMEM((4, 10, 32, 768), BF)] * 2 + [pltpu.VMEM((1024, 256), F32)] * 2
    edge_scratch = [pltpu.VMEM((2, 10, 32, 768), BF)] * 2
    weights = (first_weight, second_weight)
    flops = 2 * 2 * 1024 * 6912 * 256
    sent1, slabs = call(
        pack_kernel,
        "pack",
        0,
        (core.astype(jnp.int32).reshape(1), cot, field),
        [shape((4, 9, 32, 256), BF), shape((2, 2, 8, 32, 256), BF)],
        [pltpu.SemaphoreType.DMA((6,))],
        40,
        (1, 2),
    )
    other1 = swap_cores(sent1)
    near1, far1 = swap_slabs(
        {0: slabs[0, 0], 3: slabs[1, 0]},
        {0: slabs[0, 1], 3: slabs[1, 1]},
        jnp.where(zero, other1[:, 8:9], other1[:, 7:8]),
        jnp.where(zero, other1[:, 0:1], other1[:, 8:9]),
        low_half,
    )
    inner = call(
        inner_kernel,
        "inner",
        flops * 5 // 6,
        (place, cot, field, other1, *weights),
        [half, half, part, part, shape((6912, 256), BF), shape((6912, 256), BF)],
        own_scratch + [pltpu.SemaphoreType.DMA((2,))],
        38,
        (4, 5),
    )
    inner, weights = inner[:4], inner[4:]
    inner_hidden, beside = lax.optimization_barrier((inner[0], other1))
    (chip,) = call(
        chip_kernel,
        "chip",
        flops // 8,
        (place, cot, field, beside),
        [shape((4, 18, 32, 768), BF)],
        [],
        12,
    )
    inner_hidden, chip = lax.optimization_barrier((inner_hidden, chip))
    inner = (inner_hidden, *inner[1:])
    hidden, pre_grad, sent2 = call(
        outer_kernel,
        "outer",
        flops // 6,
        (place, near1, far1, *inner, *weights),
        [grid, grid, shape((4, 9, 32, 256), BF)],
        edge_scratch,
        24,
    )
    edges = swap_cores(
        jnp.where(
            zero,
            jnp.stack([near1[0, 0:8], far1[0, 0:8]]),
            jnp.stack([near1[1, 0:8], far1[1, 0:8]]),
        )
    )
    other2 = swap_cores(sent2)
    near2, far2 = swap_slabs(
        hidden,
        pre_grad,
        jnp.where(zero, other2[:, 8:9], other2[:, 7:8]),
        jnp.where(zero, other2[:, 0:1], other2[:, 8:9]),
        low_half,
    )
    own1, *sent1, sides, turned, local = call(
        weight_kernel,
        "weight_terms",
        flops * 4 // 9,
        (place, chip, near1, far1, edges, hidden, pre_grad, other2),
        [shape((8, 32, 768), BF)] * 4
        + [shape((2, 18, 32, 768), BF), shape((256, 2048), BF), shape((2048, 256), BF)],
        [pltpu.VMEM((256, 3072), BF), pltpu.VMEM((4, 256, 768), BF)],
        26,
    )
    got1 = hop((sent1[0], sent1[2], sent1[1]), 0)
    own2, *sent2 = call(
        weight_rest_kernel,
        "weight_terms_rest",
        flops * 5 // 9,
        (place, chip, sides, turned, local),
        [shape((8, 32, 960), BF)] * 4,
        [pltpu.VMEM((256, 3840), BF), pltpu.VMEM((4, 256, 960), BF)],
        26,
    )
    got2 = hop((sent2[0], sent2[2], sent2[1]), 0)
    hidden, pre_grad, other2, own2, *got1 = lax.optimization_barrier(
        (hidden, pre_grad, other2, own2, *got1)
    )
    last = call(
        last_inner_kernel,
        "outputs_inner",
        flops * 5 // 6,
        (place, hidden, pre_grad, other2, field, cot, *weights),
        [half, half, part, part],
        own_scratch,
        26,
    )
    output, field_grad = call(
        last_outer_kernel,
        "outputs_outer",
        flops // 6,
        (place, near2, far2, *last, field, cot, *weights),
        [grid, grid],
        edge_scratch,
        24,
    )
    own2, output, field_grad = lax.optimization_barrier((own2, output, field_grad))
    first_grad, second_grad = reduce_tiles(place, (own1, *got1, own2, *got2), core)
    return output[None], field_grad[None], first_grad, second_grad


def solution(mesh):
    placed = P("dp", "px", "py", None, None)
    return jax.shard_map(
        body,
        mesh=mesh,
        in_specs=(placed, placed, P(), P()),
        out_specs=(placed, placed, P("dp", ("px", "py")), P("dp", ("px", "py"))),
        check_vma=False,
    )
```
